32 devices in a mesh: box: 8 (over y, x, core), dir: 4 (over z).
Axes of the slice: x: 2, y: 2, z: 4, core: 2. Of those that a mesh axis runs over, the one named last changes fastest.
Arguments:
- outgoing: float32 [512, 8, 2048], P(('box', 'dir')), may hold values from -6 to 6
- fine_slot: int32 [512], P('box'), may hold values from 0 to 511, as said below
- translator: float32 [316, 2, 8192], P(None, None, 'dir'), may hold values from -0.4 to 0.4
- list_partner: int32 [64, 189], replicated, may hold values from 0 to 63
- list_kind: int32 [64, 189], replicated, may hold values from 0 to 315
- list_count: int32 [64], replicated, may hold values from 63 to 189, as said below
Outputs:
- fine_incoming: float32 [512, 8, 2048], P(('box', 'dir'))
The draws below stay inside these ranges and needn't reach their ends.
Inputs may be any that keep to these rules, and one draw needn't show every extreme that they name: `fine_slot`: the fine boxes 8 * 8 * g to 8 * 8 * (g + 1) - 1 carry each of the values 8 * 8 * g to 8 * 8 * (g + 1) - 1 exactly once, so every parent has its 8 children, one in each octant, within that group. Slots from list_count[p] on are ignored.
All inputs are finite; a program needn't handle non-finite values.
Results may differ from the reference program's by a relative error of at most 0.0003.
Values sent between devices are 32-bit elements; how exact they have to be, the bound alone decides.
A program may use at most 64 MiB of HBM per device.

```python
import jax
import jax.numpy as jnp
from jax import lax

TF = 32
PF = 64
TP = 64
PP = 128
EXC = 4
LIST = 189
NKIND = 316
PB_DEV = 8
NP = 64
NF = 512
KF = 2048
KP = 8192


def draw_fine_slot(key, part):
    group_width = 8 * PB_DEV
    groups = NF // group_width
    row_keys = jax.random.split(jax.random.fold_in(key, 7), groups)
    shuffled = jax.vmap(lambda row_key: jax.random.permutation(row_key, group_width))(row_keys)
    offsets = jnp.arange(groups, dtype=jnp.int32)[:, None] * group_width
    return (shuffled.astype(jnp.int32) + offsets).reshape(NF).astype(jnp.int32)


def draw_list_count(key, part):
    base_key = jax.random.fold_in(key, 11)
    count_key, first_key, second_key = jax.random.split(base_key, 3)
    counts = jax.random.randint(count_key, (NP,), LIST // 3, LIST + 1)
    longest = jax.random.randint(first_key, (), 0, NP)
    shortest = (longest + 1 + jax.random.randint(second_key, (), 0, NP - 1)) % NP
    counts = counts.at[longest].set(LIST)
    counts = counts.at[shortest].set(LIST // 3)
    return counts.astype(jnp.int32)


def touch_ends(entries, own_key, smallest, top_value):
    dims = entries.shape
    index_at = [jax.random.randint(jax.random.fold_in(own_key, axis), (), 0, dims[axis]) for axis in range(len(dims))]
    entries = entries.at[tuple(index_at)].set(smallest)
    longest = dims.index(max(dims))
    index_at[longest] = (index_at[longest] + 1) % dims[longest]
    return entries.at[tuple(index_at)].set(top_value)


def levels(key, dims, shards, low, high):
    level, own = 1.0, jax.random.fold_in(key, 6)
    for position, parts in shards:
        heights = jnp.exp(jax.random.uniform(jax.random.fold_in(own, position), (parts,), jnp.float32, low / len(shards), high / len(shards)))
        level = level * jnp.repeat(heights, dims[position] // parts).reshape([-1 if axis == position else 1 for axis in range(len(dims))])
    return level


def scatter_about(own_key, extent, scale, limit, shards=(), kind=jnp.bfloat16):
    level = levels(own_key, extent, shards, -0.22, 0.18) if shards else 1.0
    values = jax.random.normal(own_key, extent, jnp.float32) * scale * level
    return jnp.minimum(jnp.maximum(values, -limit), limit).astype(kind)


def setup_inputs(seed: int = 0) -> dict:
    streams_of = jax.random.split(jax.random.key(seed), 7)
    outgoing = scatter_about(streams_of[0], (NF, 2 * EXC, KF), 1.0, 6.0, ((0, 32),), jnp.float32)
    fine_slot = draw_fine_slot(jax.random.fold_in(streams_of[6], 71), 0)
    translator = scatter_about(streams_of[2], (NKIND, 2, KP), 0.06, 0.4, ((2, 4),), jnp.float32)
    list_partner = touch_ends(jax.random.randint(streams_of[3], (NP, LIST), 0, NP), jax.random.fold_in(streams_of[3], 1), 0, NP - 1).astype(jnp.int32)
    list_kind = touch_ends(jax.random.randint(streams_of[4], (NP, LIST), 0, NKIND), jax.random.fold_in(streams_of[4], 1), 0, NKIND - 1).astype(jnp.int32)
    list_count = draw_list_count(jax.random.fold_in(streams_of[6], 71), 0)
    return dict(outgoing=outgoing, fine_slot=fine_slot, translator=translator, list_partner=list_partner, list_kind=list_kind, list_count=list_count)


wave_shift = 5.0
highest = lax.Precision.HIGHEST


def theta_table(fine_count, coarse_count):
    fine_angle = (jnp.arange(fine_count, dtype=jnp.float32) + 0.5) * (jnp.pi / fine_count)
    coarse_angle = (jnp.arange(coarse_count, dtype=jnp.float32) + 0.5) * (jnp.pi / coarse_count)
    orders = jnp.arange(1, fine_count, dtype=jnp.float32)
    products = jnp.cos(coarse_angle[:, None, None] * orders) * jnp.cos(fine_angle[None, :, None] * orders)
    return (1.0 + 2.0 * jnp.sum(products, axis=2)) / fine_count


def phi_table(fine_count, coarse_count):
    fine_angle = jnp.arange(fine_count, dtype=jnp.float32) * (2.0 * jnp.pi / fine_count)
    coarse_angle = jnp.arange(coarse_count, dtype=jnp.float32) * (2.0 * jnp.pi / coarse_count)
    offset = coarse_angle[:, None] - fine_angle[None, :]
    orders = jnp.arange(1, fine_count // 2, dtype=jnp.float32)
    series = jnp.sum(jnp.cos(offset[:, :, None] * orders), axis=2)
    return (1.0 + 2.0 * series + jnp.cos(offset * (fine_count // 2))) / fine_count


def octant_phase(octant, first_theta, theta_count, coarse_theta, coarse_phi):
    theta_index = first_theta + jnp.arange(theta_count, dtype=jnp.int32)
    polar = (theta_index.astype(jnp.float32) + 0.5) * (jnp.pi / coarse_theta)
    azimuth = jnp.arange(coarse_phi, dtype=jnp.float32) * (2.0 * jnp.pi / coarse_phi)
    along_x = jnp.sin(polar)[:, None] * jnp.cos(azimuth)[None, :]
    along_y = jnp.sin(polar)[:, None] * jnp.sin(azimuth)[None, :]
    along_z = jnp.cos(polar)[:, None] + 0.0 * azimuth[None, :]
    sign_x = (2 * (octant % 2) - 1).astype(jnp.float32)
    sign_y = (2 * ((octant // 2) % 2) - 1).astype(jnp.float32)
    sign_z = (2 * (octant // 4) - 1).astype(jnp.float32)
    phase_angle = wave_shift * (sign_x[:, None, None] * along_x[None] + sign_y[:, None, None] * along_y[None] + sign_z[:, None, None] * along_z[None])
    return jnp.cos(phase_angle), jnp.sin(phase_angle)


def reference(outgoing, fine_slot, translator, list_partner, list_kind, list_count):
    channels = outgoing.shape[1]
    excite = channels // 2
    row_boxes = 8 * PB_DEV
    groups = NF // row_boxes
    up_theta = theta_table(TF, TP)
    up_phi = phi_table(PF, PP)
    parent_index = jnp.arange(PB_DEV, dtype=jnp.int32)

    def aggregate_group(inputs):
        group_data, group_slot = inputs
        pattern = group_data.reshape(row_boxes, channels, TF, PF)
        raised = jnp.einsum("ut,fctp->fcup", up_theta, pattern, precision=highest)
        raised = jnp.einsum("qp,fcup->fcuq", up_phi, raised, precision=highest)
        cos_table, sin_table = octant_phase(group_slot % 8, 0, TP, TP, PP)
        cos_table = cos_table[:, None]
        sin_table = sin_table[:, None]
        real_part = raised[:, :excite]
        imag_part = raised[:, excite:]
        shifted = jnp.concatenate([real_part * cos_table + imag_part * sin_table, imag_part * cos_table - real_part * sin_table], axis=1)
        onehot = (((group_slot // 8) % PB_DEV)[None, :] == parent_index[:, None]).astype(jnp.float32)
        summed = jnp.einsum("pf,fcuq->pcuq", onehot, shifted, precision=highest)
        return summed.reshape(PB_DEV, channels, TP * PP)

    parent_out = lax.map(aggregate_group, (outgoing.reshape(groups, row_boxes, channels, TF * PF), fine_slot.reshape(groups, row_boxes)))
    parent_out = parent_out.reshape(NP, channels, TP * PP)
    positions = jnp.arange(LIST, dtype=jnp.int32)

    def translate_parent(inputs):
        partner_row, kind_row, live_count = inputs
        picked = parent_out[partner_row]
        alive_mask = (positions < live_count).astype(jnp.float32)[:, None]
        kernel_rows = translator[kind_row]
        along_real = (kernel_rows[:, 0] * alive_mask)[:, None]
        along_imag = (kernel_rows[:, 1] * alive_mask)[:, None]
        real_part = picked[:, :excite]
        imag_part = picked[:, excite:]
        new_real = jnp.sum(along_real * real_part - along_imag * imag_part, axis=0)
        new_imag = jnp.sum(along_real * imag_part + along_imag * real_part, axis=0)
        return jnp.concatenate([new_real, new_imag], axis=0)

    incoming = lax.map(translate_parent, (list_partner, list_kind, list_count))

    def disaggregate_group(inputs):
        group_field, group_slot = inputs
        onehot = (((group_slot // 8) % PB_DEV)[None, :] == parent_index[:, None]).astype(jnp.float32)
        fields = group_field.reshape(PB_DEV, channels, TP, PP)
        spread = jnp.einsum("pf,pcuq->fcuq", onehot, fields, precision=highest)
        cos_table, sin_table = octant_phase(group_slot % 8, 0, TP, TP, PP)
        cos_table = cos_table[:, None]
        sin_table = sin_table[:, None]
        real_part = spread[:, :excite]
        imag_part = spread[:, excite:]
        shifted = jnp.concatenate([real_part * cos_table - imag_part * sin_table, imag_part * cos_table + real_part * sin_table], axis=1)
        lowered = jnp.einsum("qp,fcuq->fcup", up_phi, shifted, precision=highest) * (PF / PP)
        result = jnp.einsum("ut,fcup->fctp", up_theta, lowered, precision=highest) * (TF / TP)
        return result.reshape(row_boxes, channels, TF * PF)

    fine_incoming = lax.map(disaggregate_group, (incoming.reshape(groups, PB_DEV, channels, TP * PP), fine_slot.reshape(groups, row_boxes)))
    return fine_incoming.reshape(NF, channels, TF * PF)
```

```python
import functools

import jax
import jax.numpy as jnp
import ml_dtypes
import numpy as np
from jax import lax
from jax.experimental import pallas as pl
from jax.experimental.pallas import tpu as pltpu
from jax.sharding import PartitionSpec as P

TF = 32
PF = 64
TP = 64
PP = 128


wave_shift = 5.0
highest = lax.Precision.HIGHEST


def theta_table(fine_count, coarse_count):
    fine_angle = (jnp.arange(fine_count, dtype=jnp.float32) + 0.5) * (jnp.pi / fine_count)
    coarse_angle = (jnp.arange(coarse_count, dtype=jnp.float32) + 0.5) * (jnp.pi / coarse_count)
    orders = jnp.arange(1, fine_count, dtype=jnp.float32)
    products = jnp.cos(coarse_angle[:, None, None] * orders) * jnp.cos(
        fine_angle[None, :, None] * orders
    )
    return (1.0 + 2.0 * jnp.sum(products, axis=2)) / fine_count


def phi_table(fine_count, coarse_count):
    fine_angle = jnp.arange(fine_count, dtype=jnp.float32) * (2.0 * jnp.pi / fine_count)
    coarse_angle = jnp.arange(coarse_count, dtype=jnp.float32) * (2.0 * jnp.pi / coarse_count)
    offset = coarse_angle[:, None] - fine_angle[None, :]
    orders = jnp.arange(1, fine_count // 2, dtype=jnp.float32)
    series = jnp.sum(jnp.cos(offset[:, :, None] * orders), axis=2)
    return (1.0 + 2.0 * series + jnp.cos(offset * (fine_count // 2))) / fine_count


def octant_phase(octant, first_theta, theta_count, coarse_theta, coarse_phi):
    theta_index = first_theta + jnp.arange(theta_count, dtype=jnp.int32)
    polar = (theta_index.astype(jnp.float32) + 0.5) * (jnp.pi / coarse_theta)
    azimuth = jnp.arange(coarse_phi, dtype=jnp.float32) * (2.0 * jnp.pi / coarse_phi)
    along_x = jnp.sin(polar)[:, None] * jnp.cos(azimuth)[None, :]
    along_y = jnp.sin(polar)[:, None] * jnp.sin(azimuth)[None, :]
    along_z = jnp.cos(polar)[:, None] + 0.0 * azimuth[None, :]
    sign_x = (2 * (octant % 2) - 1).astype(jnp.float32)
    sign_y = (2 * (octant // 2 % 2) - 1).astype(jnp.float32)
    sign_z = (2 * (octant // 4) - 1).astype(jnp.float32)
    phase_angle = wave_shift * (
        sign_x[:, None, None] * along_x[None]
        + sign_y[:, None, None] * along_y[None]
        + sign_z[:, None, None] * along_z[None]
    )
    return (jnp.cos(phase_angle), jnp.sin(phase_angle))


def translate(sources, kernel_table, partner, kind, count):
    targets, length = partner.shape
    source_rows, _, excite, lanes = sources.shape
    kinds = kernel_table.shape[0]
    blocks = 7
    block_width = length // blocks
    flat_sources = sources.reshape(source_rows, 2 * excite * lanes)
    flat_kernel = kernel_table.reshape(kinds, 2 * lanes)
    source_ids = jnp.arange(source_rows, dtype=jnp.int32)
    kind_ids = jnp.arange(kinds, dtype=jnp.int32)

    def add_block(block_step, running):
        begin_at = block_step * block_width
        near_rows = lax.dynamic_slice_in_dim(partner, begin_at, block_width, 1)
        kind_rows = lax.dynamic_slice_in_dim(kind, begin_at, block_width, 1)
        position = begin_at + jnp.arange(block_width, dtype=jnp.int32)
        alive_mask = (position[None, :] < count[:, None]).astype(jnp.float32)
        select_source = (
            (near_rows[:, :, None] == source_ids)
            .astype(jnp.float32)
            .reshape(targets * block_width, source_rows)
        )
        select_kind = (
            (kind_rows[:, :, None] == kind_ids).astype(jnp.float32) * alive_mask[:, :, None]
        ).reshape(targets * block_width, kinds)
        picked = jnp.dot(
            select_source, flat_sources, precision=highest, preferred_element_type=jnp.float32
        )
        picked = picked.reshape(targets, block_width, 2, excite, lanes)
        factor = jnp.dot(
            select_kind, flat_kernel, precision=highest, preferred_element_type=jnp.float32
        )
        factor = factor.reshape(targets, block_width, 2, 1, lanes)
        along_real = factor[:, :, 0]
        along_imag = factor[:, :, 1]
        real_part = picked[:, :, 0]
        imag_part = picked[:, :, 1]
        new_real = jnp.sum(along_real * real_part - along_imag * imag_part, axis=1)
        new_imag = jnp.sum(along_real * imag_part + along_imag * real_part, axis=1)
        return running + jnp.stack([new_real, new_imag], axis=1)

    initial = jnp.zeros((targets, 2, excite, lanes), jnp.float32)
    return lax.fori_loop(0, blocks, add_block, initial)


def general_body(outgoing, fine_slot, translator, list_partner, list_kind, list_count):
    dir_count = lax.axis_size("dir")
    box_count = lax.axis_size("box")
    box_index = lax.axis_index("box")
    dir_index = lax.axis_index("dir")
    channels = outgoing.shape[1]
    excite = channels // 2
    fine_here = outgoing.shape[0]
    row_boxes = fine_slot.shape[0]
    parents_here = row_boxes // 8
    theta_here = TP // dir_count
    dirs_here = translator.shape[2]
    up_theta = theta_table(TF, TP)
    up_phi = phi_table(PF, PP)
    octant = fine_slot % 8
    local_parent = fine_slot // 8 % parents_here
    onehot = (local_parent[None, :] == jnp.arange(parents_here, dtype=jnp.int32)[:, None]).astype(
        jnp.float32
    )
    cos_table, sin_table = octant_phase(octant, dir_index * theta_here, theta_here, TP, PP)
    cos_table = cos_table[:, :, None, :]
    sin_table = sin_table[:, :, None, :]
    pattern = outgoing.reshape(fine_here, channels, TF, PF)
    raised = jnp.einsum("ut,fctp->fcup", up_theta, pattern, precision=highest)
    raised = jnp.einsum("qp,fcup->fucq", up_phi, raised, precision=highest)
    spread = lax.all_to_all(raised, "dir", split_axis=1, concat_axis=0, tiled=True)
    real_part = spread[:, :, :excite]
    imag_part = spread[:, :, excite:]
    shifted = jnp.concatenate(
        [
            real_part * cos_table + imag_part * sin_table,
            imag_part * cos_table - real_part * sin_table,
        ],
        axis=2,
    )
    parent_out = jnp.einsum("pf,fucq->pcuq", onehot, shifted, precision=highest)
    parent_out = parent_out.reshape(parents_here, channels, dirs_here)
    split_here = dirs_here // box_count
    sectioned = jnp.swapaxes(
        parent_out.reshape(parents_here, channels, box_count, split_here), 1, 2
    )
    sectioned = sectioned.reshape(parents_here, box_count, channels * split_here)
    gathered = lax.all_to_all(sectioned, "box", split_axis=1, concat_axis=0, tiled=True)
    sources = gathered.reshape(box_count * parents_here, 2, excite, split_here)
    kernel_rows = lax.dynamic_slice_in_dim(translator, box_index * split_here, split_here, 2)
    translated = translate(sources, kernel_rows, list_partner, list_kind, list_count)
    translated = translated.reshape(box_count * parents_here, 1, channels * split_here)
    returned = lax.all_to_all(translated, "box", split_axis=0, concat_axis=1, tiled=True)
    incoming = jnp.swapaxes(returned.reshape(parents_here, box_count, channels, split_here), 1, 2)
    incoming = incoming.reshape(parents_here, channels, dirs_here)
    fields = incoming.reshape(parents_here, channels, theta_here, PP)
    spread_back = jnp.einsum("pf,pcuq->fucq", onehot, fields, precision=highest)
    real_part = spread_back[:, :, :excite]
    imag_part = spread_back[:, :, excite:]
    shifted_back = jnp.concatenate(
        [
            real_part * cos_table - imag_part * sin_table,
            imag_part * cos_table + real_part * sin_table,
        ],
        axis=2,
    )
    arrived_back = lax.all_to_all(shifted_back, "dir", split_axis=0, concat_axis=1, tiled=True)
    arrived_back = jnp.einsum("qp,fucq->fucp", up_phi, arrived_back, precision=highest) * (PF / PP)
    result = jnp.einsum("ut,fucp->fctp", up_theta, arrived_back, precision=highest) * (TF / TP)
    return result.reshape(fine_here, channels, TF * PF)


def np_theta(fine_count, coarse_count):
    fine_angle = (np.arange(fine_count) + 0.5) * (np.pi / fine_count)
    coarse_angle = (np.arange(coarse_count) + 0.5) * (np.pi / coarse_count)
    orders = np.arange(1, fine_count)
    products = np.cos(coarse_angle[:, None, None] * orders) * np.cos(
        fine_angle[None, :, None] * orders
    )
    return (1.0 + 2.0 * products.sum(2)) / fine_count


def np_phi(fine_count, coarse_count):
    fine_angle = np.arange(fine_count) * (2.0 * np.pi / fine_count)
    coarse_angle = np.arange(coarse_count) * (2.0 * np.pi / coarse_count)
    offset = coarse_angle[:, None] - fine_angle[None, :]
    orders = np.arange(1, fine_count // 2)
    series = np.cos(offset[:, :, None] * orders).sum(2)
    return (1.0 + 2.0 * series + np.cos(offset * (fine_count // 2))) / fine_count


def np_phase(channels):
    polar = (np.arange(TP) + 0.5) * (np.pi / TP)
    azimuth = np.arange(PP) * (2.0 * np.pi / PP)
    octant = np.arange(8)
    signs = [2.0 * (octant // step % 2) - 1.0 for step in (1, 2, 4)]
    along = [
        np.sin(polar)[:, None] * np.cos(azimuth)[None, :],
        np.sin(polar)[:, None] * np.sin(azimuth)[None, :],
        np.cos(polar)[:, None] + 0.0 * azimuth[None, :],
    ]
    angle = wave_shift * sum(s[:, None, None] * a[None] for s, a in zip(signs, along))
    half = channels // 2
    turn = np.where(np.arange(channels) < half, 1.0, -1.0)
    sin_table = np.sin(angle)[:, :, None, :] * turn[None, None, :, None]
    cos_table = np.broadcast_to(np.cos(angle)[:, :, None, :], sin_table.shape)
    return cos_table.astype(np.float32), sin_table.astype(np.float32)


def np_split(values):
    high = values.astype(ml_dtypes.bfloat16)
    low = (values - high.astype(np.float64)).astype(ml_dtypes.bfloat16)
    return high, low


def tables(channels):
    theta = np_theta(TF, TP)
    phi = np_phi(PF, PP)
    eye = np.eye(channels)
    order = np.concatenate([np.arange(0, TF, 2), np.arange(1, TF, 2)])
    theta = theta[:, order]
    up_phi = np.kron(np.eye(2), phi.T)
    up_theta = np.kron(theta, eye)
    down_theta = np.kron(theta.T, eye) * (TF / TP)
    down_phi = np.kron(np.eye(2), phi) * (PF / PP)
    uph, upl = np_split(up_phi)
    uth, utl = np_split(up_theta)
    dth, dtl = np_split(down_theta)
    dph, dpl = np_split(down_phi)
    return (
        np.concatenate([uph, uph, upl], axis=0),
        np.concatenate([uth, uth, utl], axis=1),
        np.concatenate([dth, dth, dtl], axis=1),
        np.concatenate([dph, dph, dpl], axis=0),
    )


def split3(values, axis):
    high = values.astype(jnp.bfloat16)
    low = (values - high.astype(jnp.float32)).astype(jnp.bfloat16)
    return jnp.concatenate([high, low, high], axis=axis)


def dot(a, b):
    return jnp.dot(a, b, preferred_element_type=jnp.float32)


pair = 2


def raise_kernel(slot_ref, x_ref, phi_ref, theta_ref, cos_ref, sin_ref, out_ref):
    step = pl.program_id(0)
    channels = x_ref.shape[1]
    parents = out_ref.shape[1]

    @pl.when(step == 0)
    def _():
        out_ref[...] = jnp.zeros_like(out_ref)

    stacked = []
    for i in range(pair):
        x = x_ref[i]
        x = jnp.concatenate(
            [x[:, j * 2 * PF : (j + 1) * 2 * PF] for j in range(TF // 2)], axis=0
        )
        y = dot(split3(x, 1), phi_ref[...])
        stacked.append(jnp.concatenate([y[:, :PP], y[:, PP:]], axis=0))
    z = jnp.concatenate(stacked, axis=1)
    raised = dot(theta_ref[...], split3(z, 0))
    for i in range(pair):
        slot = slot_ref[step * pair + i]
        octant = slot % 8
        parent = slot // 8 % parents
        r = raised[:, i * PP : (i + 1) * PP].reshape(TP, channels, PP)
        turned = pltpu.roll(r, channels // 2, 1)
        out_ref[:, parent] += r * cos_ref[octant] + turned * sin_ref[octant]


def lower_kernel(slot_ref, f_ref, phi_ref, theta_ref, cos_ref, sin_ref, out_ref):
    step = pl.program_id(0)
    channels = out_ref.shape[1]
    parents = f_ref.shape[1]
    fields = []
    for i in range(pair):
        slot = slot_ref[step * pair + i]
        octant = slot % 8
        parent = slot // 8 % parents
        r = f_ref[:, parent]
        turned = pltpu.roll(r, channels // 2, 1)
        child = r * cos_ref[octant] - turned * sin_ref[octant]
        fields.append(child.reshape(TP * channels, PP))
    z = dot(theta_ref[...], split3(jnp.concatenate(fields, axis=1), 0))
    half = z.shape[0] // 2
    for i in range(pair):
        part = z[:, i * PP : (i + 1) * PP]
        y = jnp.concatenate([part[:half], part[half:]], axis=1)
        x = dot(split3(y, 1), phi_ref[...])
        out_ref[i] = jnp.concatenate(
            [x[j * channels : (j + 1) * channels] for j in range(TF // 2)], axis=1
        )


def whole_spec(array):
    return pl.BlockSpec(array.shape, lambda *_: (0,) * array.ndim)


def raise_parents(slots, outgoing, parents, consts):
    fine, channels, width = outgoing.shape
    phi, theta, cos_table, sin_table = consts
    shape = (TP, parents, channels, PP)
    return pl.pallas_call(
        raise_kernel,
        out_shape=jax.ShapeDtypeStruct(shape, jnp.float32),
        grid_spec=pltpu.PrefetchScalarGridSpec(
            num_scalar_prefetch=1,
            grid=(fine // pair,),
            in_specs=[
                pl.BlockSpec((pair, channels, width), lambda i, _: (i, 0, 0)),
                whole_spec(phi),
                whole_spec(theta),
                whole_spec(cos_table),
                whole_spec(sin_table),
            ],
            out_specs=pl.BlockSpec(shape, lambda i, _: (0, 0, 0, 0)),
        ),
        compiler_params=pltpu.CompilerParams(vmem_limit_bytes=48 * 2**20),
        name="raise_parents",
    )(slots, outgoing, phi, theta, cos_table, sin_table)


def lower_parents(slots, field, consts):
    parents, channels = field.shape[1:3]
    fine = slots.shape[0]
    phi, theta, cos_table, sin_table = consts
    return pl.pallas_call(
        lower_kernel,
        out_shape=jax.ShapeDtypeStruct((fine, channels, TF * PF), jnp.float32),
        grid_spec=pltpu.PrefetchScalarGridSpec(
            num_scalar_prefetch=1,
            grid=(fine // pair,),
            in_specs=[
                whole_spec(field),
                whole_spec(phi),
                whole_spec(theta),
                whole_spec(cos_table),
                whole_spec(sin_table),
            ],
            out_specs=pl.BlockSpec((pair, channels, TF * PF), lambda i, _: (i, 0, 0)),
        ),
        compiler_params=pltpu.CompilerParams(vmem_limit_bytes=48 * 2**20),
        name="lower_parents",
    )(slots, field, phi, theta, cos_table, sin_table)


def fill_operator(partner_ref, kind_ref, rows_ref, sel_ref, store, targets, sources):
    blocks = sel_ref.shape[0]
    length = partner_ref.shape[1]
    source_ids = lax.broadcasted_iota(jnp.int32, (sources, length), 0)
    kind_ids = lax.broadcasted_iota(jnp.int32, (blocks * 128, length), 0)

    def count_pairs(p, _):
        partner = partner_ref[pl.ds(p, 1), :]
        kind = kind_ref[pl.ds(p, 1), :]
        a = jnp.where(source_ids == partner, 1.0, 0.0).astype(jnp.bfloat16)
        b = jnp.where(kind_ids == kind, 1.0, 0.0).astype(jnp.bfloat16)
        counts = lax.dot_general(
            a, b, (((1,), (1,)), ((), ())), preferred_element_type=jnp.float32
        )
        for j in range(blocks):
            sel_ref[j, pl.ds(p, sources, stride=targets), :] = counts[:, j * 128 : (j + 1) * 128]
        return 0

    lax.fori_loop(0, targets, count_pairs, 0)
    kinds, width = rows_ref.shape
    pad = blocks * 128 - kinds
    rows = rows_ref[...]
    if pad:
        rows = jnp.concatenate([rows, jnp.zeros((pad, width), jnp.float32)], axis=0)
    high = rows.astype(jnp.bfloat16)
    low = (rows - high.astype(jnp.float32)).astype(jnp.bfloat16)
    both = jnp.concatenate([high, low], axis=0)
    tile = 512

    def one_tile(i, _):
        start = pl.multiple_of(i * tile, tile)
        chosen = jnp.concatenate(
            [sel_ref[j, pl.ds(start, tile), :] for j in range(blocks)], axis=1
        ).astype(jnp.bfloat16)
        store(start, tile, dot(jnp.concatenate([chosen, chosen], axis=1), both))
        return 0

    lax.fori_loop(0, targets * sources // tile, one_tile, 0)


def operator_kernel(partner_ref, kind_ref, rows_ref, out_ref, sel_ref, *, targets, sources):
    def store(start, tile, values):
        out_ref[pl.ds(start, tile), :] = values

    fill_operator(partner_ref, kind_ref, rows_ref, sel_ref, store, targets, sources)


def build_operator(partner, kind, rows, sources):
    targets, length = partner.shape
    kinds, width = rows.shape
    blocks = -(-kinds // 128)
    return pl.pallas_call(
        functools.partial(operator_kernel, targets=targets, sources=sources),
        out_shape=jax.ShapeDtypeStruct((sources * targets, width), jnp.float32),
        scratch_shapes=[pltpu.VMEM((blocks, sources * targets, 128), jnp.float32)],
        compiler_params=pltpu.CompilerParams(vmem_limit_bytes=48 * 2**20),
        cost_estimate=pl.CostEstimate(
            flops=4 * sources * targets * blocks * 128 * width,
            bytes_accessed=4 * sources * targets * width,
            transcendentals=0,
        ),
        name="build_operator",
    )(partner, kind, rows)


def apply_tiles(op_ref, load, store, u, count, targets, sources, channels):
    half = channels // 2
    group = 2

    def add_source(s, sums, first):
        fields = [load(u, s, c) for c in range(channels)]
        out = []
        for g in range(group):
            row = pl.multiple_of(s * targets + first + g * 8, 8)
            real = op_ref[pl.ds(row, 8), u * PP : (u + 1) * PP]
            imag = op_ref[pl.ds(row, 8), (count + u) * PP : (count + u + 1) * PP]
            mine = sums[g * channels : (g + 1) * channels]
            for e in range(half):
                out.append(mine[e] + real * fields[e] - imag * fields[half + e])
            for e in range(half):
                out.append(mine[half + e] + real * fields[half + e] + imag * fields[e])
        return tuple(out)

    for first in range(0, targets, group * 8):
        sums = tuple(jnp.zeros((8, PP), jnp.float32) for _ in range(group * channels))
        sums = lax.fori_loop(
            0, sources, functools.partial(add_source, first=first), sums, unroll=4
        )
        for g in range(group):
            for c in range(channels):
                store(u, first + g * 8, c, sums[g * channels + c])


def apply_kernel(op_ref, s_ref, out_ref, *, count, targets, sources, channels):
    def load(u, s, c):
        return s_ref[u, pl.ds(s, 1), c, :]

    def store(u, p, c, values):
        out_ref[pl.ds((u * targets + p) * channels + c, 8, stride=channels), :] = values

    for u in range(count):
        apply_tiles(op_ref, load, store, u, count, targets, sources, channels)


def apply_operator(operator, fields, targets):
    count, sources, channels, _ = fields.shape
    out = pl.pallas_call(
        functools.partial(
            apply_kernel, count=count, targets=targets, sources=sources, channels=channels
        ),
        out_shape=jax.ShapeDtypeStruct((count * targets * channels, PP), jnp.float32),
        compiler_params=pltpu.CompilerParams(vmem_limit_bytes=48 * 2**20),
        name="apply_operator",
    )(operator, fields)
    return out.reshape(count, targets, channels, PP)


def body(outgoing, fine_slot, translator, list_partner, list_kind, list_count):
    dir_count = lax.axis_size("dir")
    box_count = lax.axis_size("box")
    if TP // dir_count % box_count:
        return general_body(
            outgoing, fine_slot, translator, list_partner, list_kind, list_count
        )
    box_index = lax.axis_index("box")
    dir_index = lax.axis_index("dir")
    fine_here, channels, _ = outgoing.shape
    parents_here = fine_slot.shape[0] // 8
    targets, length = list_partner.shape
    kinds, _, dirs_here = translator.shape
    split_here = dirs_here // box_count
    rows_here = split_here // PP

    up_phi, up_theta, down_theta, down_phi = tables(channels)
    cos_table, sin_table = (jnp.asarray(t) for t in np_phase(channels))
    slots = lax.dynamic_slice_in_dim(fine_slot, dir_index * fine_here, fine_here, 0)
    alive = jnp.arange(length, dtype=jnp.int32)[None, :] < list_count[:, None]
    partner = jnp.where(alive, list_partner, -1)
    rows = lax.dynamic_slice_in_dim(translator, box_index * split_here, split_here, 2)
    rows = rows.reshape(kinds, 2 * split_here)

    raised = raise_parents(
        slots, outgoing, parents_here, (jnp.asarray(up_phi), jnp.asarray(up_theta), cos_table, sin_table)
    )
    band = lax.psum_scatter(raised, "dir", scatter_dimension=0, tiled=True)
    operator = build_operator(partner, list_kind, rows, targets)
    sources = lax.all_to_all(band, "box", split_axis=0, concat_axis=1, tiled=True)
    incoming = apply_operator(operator, sources, targets)
    returned = lax.all_to_all(incoming, "box", split_axis=1, concat_axis=0, tiled=True)
    field = lax.all_gather(returned, "dir", axis=0, tiled=True)
    return lower_parents(
        slots, field, (jnp.asarray(down_phi), jnp.asarray(down_theta), cos_table, sin_table)
    )


def solution(mesh):
    placed = (P(("box", "dir"), None, None), P("box"), P(None, None, "dir"), P(), P(), P())
    return jax.shard_map(
        body, mesh=mesh, in_specs=placed, out_specs=P(("box", "dir"), None, None), check_vma=False
    )
```

```python
import functools

import jax
import jax.numpy as jnp
import ml_dtypes
import numpy as np
from jax import lax
from jax.experimental import pallas as pl
from jax.experimental.pallas import tpu as pltpu
from jax.sharding import PartitionSpec as P

TF = 32
PF = 64
TP = 64
PP = 128


wave_shift = 5.0
highest = lax.Precision.HIGHEST


def theta_table(fine_count, coarse_count):
    fine_angle = (jnp.arange(fine_count, dtype=jnp.float32) + 0.5) * (jnp.pi / fine_count)
    coarse_angle = (jnp.arange(coarse_count, dtype=jnp.float32) + 0.5) * (jnp.pi / coarse_count)
    orders = jnp.arange(1, fine_count, dtype=jnp.float32)
    products = jnp.cos(coarse_angle[:, None, None] * orders) * jnp.cos(
        fine_angle[None, :, None] * orders
    )
    return (1.0 + 2.0 * jnp.sum(products, axis=2)) / fine_count


def phi_table(fine_count, coarse_count):
    fine_angle = jnp.arange(fine_count, dtype=jnp.float32) * (2.0 * jnp.pi / fine_count)
    coarse_angle = jnp.arange(coarse_count, dtype=jnp.float32) * (2.0 * jnp.pi / coarse_count)
    offset = coarse_angle[:, None] - fine_angle[None, :]
    orders = jnp.arange(1, fine_count // 2, dtype=jnp.float32)
    series = jnp.sum(jnp.cos(offset[:, :, None] * orders), axis=2)
    return (1.0 + 2.0 * series + jnp.cos(offset * (fine_count // 2))) / fine_count


def octant_phase(octant, first_theta, theta_count, coarse_theta, coarse_phi):
    theta_index = first_theta + jnp.arange(theta_count, dtype=jnp.int32)
    polar = (theta_index.astype(jnp.float32) + 0.5) * (jnp.pi / coarse_theta)
    azimuth = jnp.arange(coarse_phi, dtype=jnp.float32) * (2.0 * jnp.pi / coarse_phi)
    along_x = jnp.sin(polar)[:, None] * jnp.cos(azimuth)[None, :]
    along_y = jnp.sin(polar)[:, None] * jnp.sin(azimuth)[None, :]
    along_z = jnp.cos(polar)[:, None] + 0.0 * azimuth[None, :]
    sign_x = (2 * (octant % 2) - 1).astype(jnp.float32)
    sign_y = (2 * (octant // 2 % 2) - 1).astype(jnp.float32)
    sign_z = (2 * (octant // 4) - 1).astype(jnp.float32)
    phase_angle = wave_shift * (
        sign_x[:, None, None] * along_x[None]
        + sign_y[:, None, None] * along_y[None]
        + sign_z[:, None, None] * along_z[None]
    )
    return (jnp.cos(phase_angle), jnp.sin(phase_angle))


def translate(sources, kernel_table, partner, kind, count):
    targets, length = partner.shape
    source_rows, _, excite, lanes = sources.shape
    kinds = kernel_table.shape[0]
    blocks = 7
    block_width = length // blocks
    flat_sources = sources.reshape(source_rows, 2 * excite * lanes)
    flat_kernel = kernel_table.reshape(kinds, 2 * lanes)
    source_ids = jnp.arange(source_rows, dtype=jnp.int32)
    kind_ids = jnp.arange(kinds, dtype=jnp.int32)

    def add_block(block_step, running):
        begin_at = block_step * block_width
        near_rows = lax.dynamic_slice_in_dim(partner, begin_at, block_width, 1)
        kind_rows = lax.dynamic_slice_in_dim(kind, begin_at, block_width, 1)
        position = begin_at + jnp.arange(block_width, dtype=jnp.int32)
        alive_mask = (position[None, :] < count[:, None]).astype(jnp.float32)
        select_source = (
            (near_rows[:, :, None] == source_ids)
            .astype(jnp.float32)
            .reshape(targets * block_width, source_rows)
        )
        select_kind = (
            (kind_rows[:, :, None] == kind_ids).astype(jnp.float32) * alive_mask[:, :, None]
        ).reshape(targets * block_width, kinds)
        picked = jnp.dot(
            select_source, flat_sources, precision=highest, preferred_element_type=jnp.float32
        )
        picked = picked.reshape(targets, block_width, 2, excite, lanes)
        factor = jnp.dot(
            select_kind, flat_kernel, precision=highest, preferred_element_type=jnp.float32
        )
        factor = factor.reshape(targets, block_width, 2, 1, lanes)
        along_real = factor[:, :, 0]
        along_imag = factor[:, :, 1]
        real_part = picked[:, :, 0]
        imag_part = picked[:, :, 1]
        new_real = jnp.sum(along_real * real_part - along_imag * imag_part, axis=1)
        new_imag = jnp.sum(along_real * imag_part + along_imag * real_part, axis=1)
        return running + jnp.stack([new_real, new_imag], axis=1)

    initial = jnp.zeros((targets, 2, excite, lanes), jnp.float32)
    return lax.fori_loop(0, blocks, add_block, initial)


def general_body(outgoing, fine_slot, translator, list_partner, list_kind, list_count):
    dir_count = lax.axis_size("dir")
    box_count = lax.axis_size("box")
    box_index = lax.axis_index("box")
    dir_index = lax.axis_index("dir")
    channels = outgoing.shape[1]
    excite = channels // 2
    fine_here = outgoing.shape[0]
    row_boxes = fine_slot.shape[0]
    parents_here = row_boxes // 8
    theta_here = TP // dir_count
    dirs_here = translator.shape[2]
    up_theta = theta_table(TF, TP)
    up_phi = phi_table(PF, PP)
    octant = fine_slot % 8
    local_parent = fine_slot // 8 % parents_here
    onehot = (local_parent[None, :] == jnp.arange(parents_here, dtype=jnp.int32)[:, None]).astype(
        jnp.float32
    )
    cos_table, sin_table = octant_phase(octant, dir_index * theta_here, theta_here, TP, PP)
    cos_table = cos_table[:, :, None, :]
    sin_table = sin_table[:, :, None, :]
    pattern = outgoing.reshape(fine_here, channels, TF, PF)
    raised = jnp.einsum("ut,fctp->fcup", up_theta, pattern, precision=highest)
    raised = jnp.einsum("qp,fcup->fucq", up_phi, raised, precision=highest)
    spread = lax.all_to_all(raised, "dir", split_axis=1, concat_axis=0, tiled=True)
    real_part = spread[:, :, :excite]
    imag_part = spread[:, :, excite:]
    shifted = jnp.concatenate(
        [
            real_part * cos_table + imag_part * sin_table,
            imag_part * cos_table - real_part * sin_table,
        ],
        axis=2,
    )
    parent_out = jnp.einsum("pf,fucq->pcuq", onehot, shifted, precision=highest)
    parent_out = parent_out.reshape(parents_here, channels, dirs_here)
    split_here = dirs_here // box_count
    sectioned = jnp.swapaxes(
        parent_out.reshape(parents_here, channels, box_count, split_here), 1, 2
    )
    sectioned = sectioned.reshape(parents_here, box_count, channels * split_here)
    gathered = lax.all_to_all(sectioned, "box", split_axis=1, concat_axis=0, tiled=True)
    sources = gathered.reshape(box_count * parents_here, 2, excite, split_here)
    kernel_rows = lax.dynamic_slice_in_dim(translator, box_index * split_here, split_here, 2)
    translated = translate(sources, kernel_rows, list_partner, list_kind, list_count)
    translated = translated.reshape(box_count * parents_here, 1, channels * split_here)
    returned = lax.all_to_all(translated, "box", split_axis=0, concat_axis=1, tiled=True)
    incoming = jnp.swapaxes(returned.reshape(parents_here, box_count, channels, split_here), 1, 2)
    incoming = incoming.reshape(parents_here, channels, dirs_here)
    fields = incoming.reshape(parents_here, channels, theta_here, PP)
    spread_back = jnp.einsum("pf,pcuq->fucq", onehot, fields, precision=highest)
    real_part = spread_back[:, :, :excite]
    imag_part = spread_back[:, :, excite:]
    shifted_back = jnp.concatenate(
        [
            real_part * cos_table - imag_part * sin_table,
            imag_part * cos_table + real_part * sin_table,
        ],
        axis=2,
    )
    arrived_back = lax.all_to_all(shifted_back, "dir", split_axis=0, concat_axis=1, tiled=True)
    arrived_back = jnp.einsum("qp,fucq->fucp", up_phi, arrived_back, precision=highest) * (PF / PP)
    result = jnp.einsum("ut,fucp->fctp", up_theta, arrived_back, precision=highest) * (TF / TP)
    return result.reshape(fine_here, channels, TF * PF)


def np_theta(fine_count, coarse_count):
    fine_angle = (np.arange(fine_count) + 0.5) * (np.pi / fine_count)
    coarse_angle = (np.arange(coarse_count) + 0.5) * (np.pi / coarse_count)
    orders = np.arange(1, fine_count)
    products = np.cos(coarse_angle[:, None, None] * orders) * np.cos(
        fine_angle[None, :, None] * orders
    )
    return (1.0 + 2.0 * products.sum(2)) / fine_count


def np_phi(fine_count, coarse_count):
    fine_angle = np.arange(fine_count) * (2.0 * np.pi / fine_count)
    coarse_angle = np.arange(coarse_count) * (2.0 * np.pi / coarse_count)
    offset = coarse_angle[:, None] - fine_angle[None, :]
    orders = np.arange(1, fine_count // 2)
    series = np.cos(offset[:, :, None] * orders).sum(2)
    return (1.0 + 2.0 * series + np.cos(offset * (fine_count // 2))) / fine_count


def np_phase(channels):
    polar = (np.arange(TP) + 0.5) * (np.pi / TP)
    azimuth = np.arange(PP) * (2.0 * np.pi / PP)
    octant = np.arange(8)
    signs = [2.0 * (octant // step % 2) - 1.0 for step in (1, 2, 4)]
    along = [
        np.sin(polar)[:, None] * np.cos(azimuth)[None, :],
        np.sin(polar)[:, None] * np.sin(azimuth)[None, :],
        np.cos(polar)[:, None] + 0.0 * azimuth[None, :],
    ]
    angle = wave_shift * sum(s[:, None, None] * a[None] for s, a in zip(signs, along))
    half = channels // 2
    turn = np.where(np.arange(channels) < half, 1.0, -1.0)
    sin_table = np.sin(angle)[:, :, None, :] * turn[None, None, :, None]
    cos_table = np.broadcast_to(np.cos(angle)[:, :, None, :], sin_table.shape)
    return cos_table.astype(np.float32), sin_table.astype(np.float32)


def np_split(values):
    high = values.astype(ml_dtypes.bfloat16)
    low = (values - high.astype(np.float64)).astype(ml_dtypes.bfloat16)
    return high, low


def tables(channels):
    theta = np_theta(TF, TP)
    phi = np_phi(PF, PP)
    eye = np.eye(channels)
    order = np.concatenate([np.arange(0, TF, 2), np.arange(1, TF, 2)])
    theta = theta[:, order]
    up_phi = np.kron(np.eye(2), phi.T)
    up_theta = np.kron(theta, eye)
    down_theta = np.kron(theta.T, eye) * (TF / TP)
    down_phi = np.kron(np.eye(2), phi) * (PF / PP)
    uph, upl = np_split(up_phi)
    uth, utl = np_split(up_theta)
    dth, dtl = np_split(down_theta)
    dph, dpl = np_split(down_phi)
    return (
        np.concatenate([uph, uph, upl], axis=0),
        np.concatenate([uth, uth, utl], axis=1),
        np.concatenate([dth, dth, dtl], axis=1),
        np.concatenate([dph, dph, dpl], axis=0),
    )


def split3(values, axis):
    high = values.astype(jnp.bfloat16)
    low = (values - high.astype(jnp.float32)).astype(jnp.bfloat16)
    return jnp.concatenate([high, low, high], axis=axis)


def dot(a, b):
    return jnp.dot(a, b, preferred_element_type=jnp.float32)


pair = 2


def raise_kernel(slot_ref, x_ref, phi_ref, theta_ref, cos_ref, sin_ref, out_ref):
    step = pl.program_id(0)
    channels = x_ref.shape[1]
    parents = out_ref.shape[1]

    @pl.when(step == 0)
    def _():
        out_ref[...] = jnp.zeros_like(out_ref)

    stacked = []
    for i in range(pair):
        x = x_ref[i]
        x = jnp.concatenate(
            [x[:, j * 2 * PF : (j + 1) * 2 * PF] for j in range(TF // 2)], axis=0
        )
        y = dot(split3(x, 1), phi_ref[...])
        stacked.append(jnp.concatenate([y[:, :PP], y[:, PP:]], axis=0))
    z = jnp.concatenate(stacked, axis=1)
    raised = dot(theta_ref[...], split3(z, 0))
    for i in range(pair):
        slot = slot_ref[step * pair + i]
        octant = slot % 8
        parent = slot // 8 % parents
        r = raised[:, i * PP : (i + 1) * PP].reshape(TP, channels, PP)
        turned = pltpu.roll(r, channels // 2, 1)
        out_ref[:, parent] += r * cos_ref[octant] + turned * sin_ref[octant]


def lower_kernel(slot_ref, f_ref, phi_ref, theta_ref, cos_ref, sin_ref, out_ref):
    step = pl.program_id(0)
    channels = out_ref.shape[1]
    parents = f_ref.shape[1]
    fields = []
    for i in range(pair):
        slot = slot_ref[step * pair + i]
        octant = slot % 8
        parent = slot // 8 % parents
        r = f_ref[:, parent]
        turned = pltpu.roll(r, channels // 2, 1)
        child = r * cos_ref[octant] - turned * sin_ref[octant]
        fields.append(child.reshape(TP * channels, PP))
    z = dot(theta_ref[...], split3(jnp.concatenate(fields, axis=1), 0))
    half = z.shape[0] // 2
    for i in range(pair):
        part = z[:, i * PP : (i + 1) * PP]
        y = jnp.concatenate([part[:half], part[half:]], axis=1)
        x = dot(split3(y, 1), phi_ref[...])
        out_ref[i] = jnp.concatenate(
            [x[j * channels : (j + 1) * channels] for j in range(TF // 2)], axis=1
        )


def whole_spec(array):
    return pl.BlockSpec(array.shape, lambda *_: (0,) * array.ndim)


def raise_parents(slots, outgoing, parents, consts):
    fine, channels, width = outgoing.shape
    phi, theta, cos_table, sin_table = consts
    shape = (TP, parents, channels, PP)
    return pl.pallas_call(
        raise_kernel,
        out_shape=jax.ShapeDtypeStruct(shape, jnp.float32),
        grid_spec=pltpu.PrefetchScalarGridSpec(
            num_scalar_prefetch=1,
            grid=(fine // pair,),
            in_specs=[
                pl.BlockSpec((pair, channels, width), lambda i, _: (i, 0, 0)),
                whole_spec(phi),
                whole_spec(theta),
                whole_spec(cos_table),
                whole_spec(sin_table),
            ],
            out_specs=pl.BlockSpec(shape, lambda i, _: (0, 0, 0, 0)),
        ),
        compiler_params=pltpu.CompilerParams(vmem_limit_bytes=48 * 2**20),
        name="raise_parents",
    )(slots, outgoing, phi, theta, cos_table, sin_table)


def lower_parents(slots, field, consts):
    parents, channels = field.shape[1:3]
    fine = slots.shape[0]
    phi, theta, cos_table, sin_table = consts
    return pl.pallas_call(
        lower_kernel,
        out_shape=jax.ShapeDtypeStruct((fine, channels, TF * PF), jnp.float32),
        grid_spec=pltpu.PrefetchScalarGridSpec(
            num_scalar_prefetch=1,
            grid=(fine // pair,),
            in_specs=[
                whole_spec(field),
                whole_spec(phi),
                whole_spec(theta),
                whole_spec(cos_table),
                whole_spec(sin_table),
            ],
            out_specs=pl.BlockSpec((pair, channels, TF * PF), lambda i, _: (i, 0, 0)),
        ),
        compiler_params=pltpu.CompilerParams(vmem_limit_bytes=48 * 2**20),
        name="lower_parents",
    )(slots, field, phi, theta, cos_table, sin_table)


MESH = pl.DeviceIdType.MESH


def exchange_kernel(
    p_ref, partner_ref, kind_ref, rows_ref, out_ref,
    sel_ref, op_ref, up_ref, down_ref, band_ref, src_ref, res_ref,
    up_send, up_recv, down_send, down_recv, go_send, go_recv, back_send, back_recv,
    rise_send, rise_recv, sink_send, sink_recv,
    *, targets, channels,
):
    n, boxes, halves, block, width = p_ref.shape
    box = lax.axis_index("box")
    z = lax.axis_index("dir")
    sources = targets
    blocks = sel_ref.shape[0]
    length = partner_ref.shape[1]
    pair_rows = sources * targets

    def remote(src, dst, send, recv, to_box, to_dir):
        return pltpu.make_async_remote_copy(
            src_ref=src, dst_ref=dst, send_sem=send, recv_sem=recv,
            device_id=(to_box, to_dir), device_id_type=MESH,
        )

    def up_copy(h, b, src):
        return remote(src, up_ref.at[h, b], up_send.at[h, b], up_recv.at[h, b], box, z + 1)

    def down_copy(h, b, src):
        return remote(src, down_ref.at[h, b], down_send.at[h, b], down_recv.at[h, b], box, z - 1)

    def sum_start(h):
        @pl.when(z == 0)
        def _():
            for b in range(n - 1, 0, -1):
                up_copy(h, b, p_ref.at[b, :, h]).start()

        @pl.when(z == n - 1)
        def _():
            for b in range(n - 1):
                down_copy(h, b, p_ref.at[b, :, h]).start()

    def sum_step(h, step):
        up_b = n - 1 - step
        down_b = step

        @pl.when((z > 0) & (z < up_b))
        def _():
            copy = up_copy(h, up_b, up_ref.at[h, up_b])
            copy.wait_recv()
            up_ref[h, up_b] += p_ref[up_b, :, h]
            copy.start()

        @pl.when((z < n - 1) & (z > down_b))
        def _():
            copy = down_copy(h, down_b, down_ref.at[h, down_b])
            copy.wait_recv()
            down_ref[h, down_b] += p_ref[down_b, :, h]
            copy.start()

    def sum_finish(h):
        band_ref[h] = p_ref[z, :, h]

        @pl.when(z > 0)
        def _():
            up_copy(h, z, up_ref.at[h, z]).wait_recv()
            band_ref[h] += up_ref[h, z]

        @pl.when(z < n - 1)
        def _():
            down_copy(h, z, down_ref.at[h, z]).wait_recv()
            band_ref[h] += down_ref[h, z]

    def sum_drain(h):
        for b in range(n):
            @pl.when(z < b)
            def _():
                up_copy(h, b, up_ref.at[h, b]).wait_send()

            @pl.when(z > b)
            def _():
                down_copy(h, b, down_ref.at[h, b]).wait_send()

    def peer(k):
        return lax.rem(box + k, boxes)

    def go_copy(h, k):
        return remote(
            band_ref.at[h, peer(k)], src_ref.at[h, box], go_send.at[h, k], go_recv.at[h, k], peer(k), z
        )

    def back_copy(h, k):
        return remote(
            res_ref.at[h, pl.ds(pl.multiple_of(peer(k) * block, block), block)],
            out_ref.at[z, box, h],
            back_send.at[h, k], back_recv.at[h, k], peer(k), z,
        )

    def go_start(h):
        for k in range(1, boxes):
            go_copy(h, k).start()
        src_ref[h, box] = band_ref[h, box]

    def go_wait(h):
        for k in range(1, boxes):
            go_copy(h, k).wait_recv()

    def back_start(h):
        for k in range(1, boxes):
            back_copy(h, k).start()
        out_ref[z, box, h] = res_ref[h, pl.ds(pl.multiple_of(box * block, block), block)]

    def back_wait(h):
        for k in range(1, boxes):
            back_copy(h, k).wait_recv()

    def rise_copy(h, b):
        piece = out_ref.at[b, :, h]
        return remote(piece, piece, rise_send.at[h, b], rise_recv.at[h, b], box, z + 1)

    def sink_copy(h, b):
        piece = out_ref.at[b, :, h]
        return remote(piece, piece, sink_send.at[h, b], sink_recv.at[h, b], box, z - 1)

    def share_step(h, step):
        @pl.when(z >= step)
        def _():
            if step:
                rise_copy(h, z - step).wait_recv()

            @pl.when(z < n - 1)
            def _():
                rise_copy(h, z - step).start()

        @pl.when(z + step <= n - 1)
        def _():
            if step:
                sink_copy(h, z + step).wait_recv()

            @pl.when(z > 0)
            def _():
                sink_copy(h, z + step).start()

    def share_drain(h):
        for b in range(n):
            @pl.when((z >= b) & (z < n - 1))
            def _():
                rise_copy(h, b).wait_send()

            @pl.when((z <= b) & (z > 0))
            def _():
                sink_copy(h, b).wait_send()

    source_ids = lax.broadcasted_iota(jnp.int32, (sources, length), 0)
    kind_ids = lax.broadcasted_iota(jnp.int32, (blocks * 128, length), 0)

    def count_pairs(p, _):
        partner = partner_ref[pl.ds(p, 1), :]
        kind = kind_ref[pl.ds(p, 1), :]
        a = jnp.where(source_ids == partner, 1.0, 0.0).astype(jnp.bfloat16)
        b = jnp.where(kind_ids == kind, 1.0, 0.0).astype(jnp.bfloat16)
        counts = lax.dot_general(
            a, b, (((1,), (1,)), ((), ())), preferred_element_type=jnp.float32
        )
        for j in range(blocks):
            sel_ref[j, pl.ds(p, sources, stride=targets), :] = counts[:, j * 128 : (j + 1) * 128]
        return 0

    def count_part(part, parts):
        first, last = targets * part // parts, targets * (part + 1) // parts
        lax.fori_loop(first, last, count_pairs, 0, unroll=4)

    def operator_half(h):
        rows = jnp.concatenate(
            [rows_ref[:, i * width : (i + 1) * width] for i in (h, halves + h)], axis=1
        )
        pad = blocks * 128 - rows.shape[0]
        if pad:
            rows = jnp.concatenate([rows, jnp.zeros((pad, 2 * width), jnp.float32)], axis=0)
        high = rows.astype(jnp.bfloat16)
        low = (rows - high.astype(jnp.float32)).astype(jnp.bfloat16)
        both = jnp.concatenate([high, low], axis=0)
        tile = 512

        def one_tile(i, _):
            start = pl.multiple_of(i * tile, tile)
            chosen = jnp.concatenate(
                [sel_ref[j, pl.ds(start, tile), :] for j in range(blocks)], axis=1
            ).astype(jnp.bfloat16)
            op_ref[h, pl.ds(start, tile), :] = dot(
                jnp.concatenate([chosen, chosen], axis=1), both
            )
            return 0

        lax.fori_loop(0, pair_rows // tile, one_tile, 0)

    def apply_half(h):
        half = channels // 2
        group = 2
        per_box = block // channels

        def add_source(s, sums, first):
            giver = s // per_box
            row0 = (s % per_box) * channels
            fields = [src_ref[h, giver, pl.ds(row0 + c, 1), :] for c in range(channels)]
            out = []
            for g in range(group):
                row = pl.multiple_of(s * targets + first + g * 8, 8)
                real = op_ref[h, pl.ds(row, 8), 0:width]
                imag = op_ref[h, pl.ds(row, 8), width : 2 * width]
                mine = sums[g * channels : (g + 1) * channels]
                for e in range(half):
                    out.append(mine[e] + real * fields[e] - imag * fields[half + e])
                for e in range(half):
                    out.append(mine[half + e] + real * fields[half + e] + imag * fields[e])
            return tuple(out)

        for first in range(0, targets, group * 8):
            sums = tuple(jnp.zeros((8, width), jnp.float32) for _ in range(group * channels))
            sums = lax.fori_loop(
                0, sources, functools.partial(add_source, first=first), sums, unroll=4
            )
            for g in range(group):
                for c in range(channels):
                    start = (first + g * 8) * channels + c
                    res_ref[h, pl.ds(start, 8, stride=channels), :] = sums[g * channels + c]

    barrier = pltpu.get_barrier_semaphore()
    for k in range(1, boxes):
        pl.semaphore_signal(barrier, inc=1, device_id=(peer(k), z), device_id_type=MESH)

    @pl.when(z > 0)
    def _():
        pl.semaphore_signal(barrier, inc=1, device_id=(box, z - 1), device_id_type=MESH)

    @pl.when(z < n - 1)
    def _():
        pl.semaphore_signal(barrier, inc=1, device_id=(box, z + 1), device_id_type=MESH)

    ends = jnp.where(z > 0, 1, 0) + jnp.where(z < n - 1, 1, 0)
    pl.semaphore_wait(barrier, boxes - 1 + ends)

    for h in range(halves):
        sum_start(h)
    for h in range(halves):
        for step in range(n - 1):
            if h == 0:
                count_part(step, n - 1)
            sum_step(h, step)
        sum_finish(h)
        go_start(h)
        operator_half(h)
        if h:
            back_wait(h - 1)
            share_step(h - 1, 0)
        go_wait(h)
        apply_half(h)
        back_start(h)
        if h:
            share_step(h - 1, 1)
    last = halves - 1
    back_wait(last)
    share_step(last, 0)
    for h in range(halves):
        for step in range(2 if h < last else 1, n):
            share_step(h, step)
    for h in range(halves):
        sum_drain(h)
        share_drain(h)
        for k in range(1, boxes):
            go_copy(h, k).wait_send()
            back_copy(h, k).wait_send()


def exchange(raised, partner, kind, rows, n, boxes, targets):
    polar, parents, channels, width = raised.shape
    halves = polar // n // boxes
    block = parents * channels
    kinds = rows.shape[0]
    kind_blocks = -(-kinds // 128)
    shape = (n, boxes, halves, block, width)
    vmem = pl.BlockSpec(memory_space=pltpu.VMEM)
    dma = pltpu.SemaphoreType.DMA
    out = pl.pallas_call(
        functools.partial(exchange_kernel, targets=targets, channels=channels),
        out_shape=jax.ShapeDtypeStruct(shape, jnp.float32),
        in_specs=[vmem] * 4,
        out_specs=vmem,
        scratch_shapes=[
            pltpu.VMEM((kind_blocks, targets * targets, 128), jnp.float32),
            pltpu.VMEM((halves, targets * targets, 2 * width), jnp.float32),
            pltpu.VMEM((halves, n, boxes, block, width), jnp.float32),
            pltpu.VMEM((halves, n, boxes, block, width), jnp.float32),
            pltpu.VMEM((halves, boxes, block, width), jnp.float32),
            pltpu.VMEM((halves, boxes, block, width), jnp.float32),
            pltpu.VMEM((halves, targets * channels, width), jnp.float32),
        ]
        + [dma((halves, n))] * 4
        + [dma((halves, boxes))] * 4
        + [dma((halves, n))] * 4,
        compiler_params=pltpu.CompilerParams(
            vmem_limit_bytes=52 * 2**20, collective_id=0, has_side_effects=True
        ),
        name="exchange",
    )(raised.reshape(shape), partner, kind, rows)
    return out.reshape(raised.shape)


def body(outgoing, fine_slot, translator, list_partner, list_kind, list_count):
    dir_count = lax.axis_size("dir")
    box_count = lax.axis_size("box")
    if TP // dir_count % box_count:
        return general_body(
            outgoing, fine_slot, translator, list_partner, list_kind, list_count
        )
    box_index = lax.axis_index("box")
    dir_index = lax.axis_index("dir")
    fine_here, channels, _ = outgoing.shape
    parents_here = fine_slot.shape[0] // 8
    targets, length = list_partner.shape
    kinds, _, dirs_here = translator.shape
    split_here = dirs_here // box_count
    rows_here = split_here // PP

    up_phi, up_theta, down_theta, down_phi = tables(channels)
    cos_table, sin_table = (jnp.asarray(t) for t in np_phase(channels))
    slots = lax.dynamic_slice_in_dim(fine_slot, dir_index * fine_here, fine_here, 0)
    alive = jnp.arange(length, dtype=jnp.int32)[None, :] < list_count[:, None]
    partner = jnp.where(alive, list_partner, -1)
    rows = lax.dynamic_slice_in_dim(translator, box_index * split_here, split_here, 2)
    rows = rows.reshape(kinds, 2 * split_here)

    raised = raise_parents(
        slots, outgoing, parents_here, (jnp.asarray(up_phi), jnp.asarray(up_theta), cos_table, sin_table)
    )
    field = exchange(raised, partner, list_kind, rows, dir_count, box_count, targets)
    return lower_parents(
        slots, field, (jnp.asarray(down_phi), jnp.asarray(down_theta), cos_table, sin_table)
    )


def solution(mesh):
    placed = (P(("box", "dir"), None, None), P("box"), P(None, None, "dir"), P(), P(), P())
    return jax.shard_map(
        body, mesh=mesh, in_specs=placed, out_specs=P(("box", "dir"), None, None), check_vma=False
    )
```

```python
import functools

import jax
import jax.numpy as jnp
import ml_dtypes
import numpy as np
from jax import lax
from jax.experimental import pallas as pl
from jax.experimental.pallas import tpu as pltpu
from jax.sharding import PartitionSpec as P

TF = 32
PF = 64
TP = 64
PP = 128


wave_shift = 5.0
highest = lax.Precision.HIGHEST


def theta_table(fine_count, coarse_count):
    fine_angle = (jnp.arange(fine_count, dtype=jnp.float32) + 0.5) * (jnp.pi / fine_count)
    coarse_angle = (jnp.arange(coarse_count, dtype=jnp.float32) + 0.5) * (jnp.pi / coarse_count)
    orders = jnp.arange(1, fine_count, dtype=jnp.float32)
    products = jnp.cos(coarse_angle[:, None, None] * orders) * jnp.cos(
        fine_angle[None, :, None] * orders
    )
    return (1.0 + 2.0 * jnp.sum(products, axis=2)) / fine_count


def phi_table(fine_count, coarse_count):
    fine_angle = jnp.arange(fine_count, dtype=jnp.float32) * (2.0 * jnp.pi / fine_count)
    coarse_angle = jnp.arange(coarse_count, dtype=jnp.float32) * (2.0 * jnp.pi / coarse_count)
    offset = coarse_angle[:, None] - fine_angle[None, :]
    orders = jnp.arange(1, fine_count // 2, dtype=jnp.float32)
    series = jnp.sum(jnp.cos(offset[:, :, None] * orders), axis=2)
    return (1.0 + 2.0 * series + jnp.cos(offset * (fine_count // 2))) / fine_count


def octant_phase(octant, first_theta, theta_count, coarse_theta, coarse_phi):
    theta_index = first_theta + jnp.arange(theta_count, dtype=jnp.int32)
    polar = (theta_index.astype(jnp.float32) + 0.5) * (jnp.pi / coarse_theta)
    azimuth = jnp.arange(coarse_phi, dtype=jnp.float32) * (2.0 * jnp.pi / coarse_phi)
    along_x = jnp.sin(polar)[:, None] * jnp.cos(azimuth)[None, :]
    along_y = jnp.sin(polar)[:, None] * jnp.sin(azimuth)[None, :]
    along_z = jnp.cos(polar)[:, None] + 0.0 * azimuth[None, :]
    sign_x = (2 * (octant % 2) - 1).astype(jnp.float32)
    sign_y = (2 * (octant // 2 % 2) - 1).astype(jnp.float32)
    sign_z = (2 * (octant // 4) - 1).astype(jnp.float32)
    phase_angle = wave_shift * (
        sign_x[:, None, None] * along_x[None]
        + sign_y[:, None, None] * along_y[None]
        + sign_z[:, None, None] * along_z[None]
    )
    return (jnp.cos(phase_angle), jnp.sin(phase_angle))


def translate(sources, kernel_table, partner, kind, count):
    targets, length = partner.shape
    source_rows, _, excite, lanes = sources.shape
    kinds = kernel_table.shape[0]
    blocks = 7
    block_width = length // blocks
    flat_sources = sources.reshape(source_rows, 2 * excite * lanes)
    flat_kernel = kernel_table.reshape(kinds, 2 * lanes)
    source_ids = jnp.arange(source_rows, dtype=jnp.int32)
    kind_ids = jnp.arange(kinds, dtype=jnp.int32)

    def add_block(block_step, running):
        begin_at = block_step * block_width
        near_rows = lax.dynamic_slice_in_dim(partner, begin_at, block_width, 1)
        kind_rows = lax.dynamic_slice_in_dim(kind, begin_at, block_width, 1)
        position = begin_at + jnp.arange(block_width, dtype=jnp.int32)
        alive_mask = (position[None, :] < count[:, None]).astype(jnp.float32)
        select_source = (
            (near_rows[:, :, None] == source_ids)
            .astype(jnp.float32)
            .reshape(targets * block_width, source_rows)
        )
        select_kind = (
            (kind_rows[:, :, None] == kind_ids).astype(jnp.float32) * alive_mask[:, :, None]
        ).reshape(targets * block_width, kinds)
        picked = jnp.dot(
            select_source, flat_sources, precision=highest, preferred_element_type=jnp.float32
        )
        picked = picked.reshape(targets, block_width, 2, excite, lanes)
        factor = jnp.dot(
            select_kind, flat_kernel, precision=highest, preferred_element_type=jnp.float32
        )
        factor = factor.reshape(targets, block_width, 2, 1, lanes)
        along_real = factor[:, :, 0]
        along_imag = factor[:, :, 1]
        real_part = picked[:, :, 0]
        imag_part = picked[:, :, 1]
        new_real = jnp.sum(along_real * real_part - along_imag * imag_part, axis=1)
        new_imag = jnp.sum(along_real * imag_part + along_imag * real_part, axis=1)
        return running + jnp.stack([new_real, new_imag], axis=1)

    initial = jnp.zeros((targets, 2, excite, lanes), jnp.float32)
    return lax.fori_loop(0, blocks, add_block, initial)


def general_body(outgoing, fine_slot, translator, list_partner, list_kind, list_count):
    dir_count = lax.axis_size("dir")
    box_count = lax.axis_size("box")
    box_index = lax.axis_index("box")
    dir_index = lax.axis_index("dir")
    channels = outgoing.shape[1]
    excite = channels // 2
    fine_here = outgoing.shape[0]
    row_boxes = fine_slot.shape[0]
    parents_here = row_boxes // 8
    theta_here = TP // dir_count
    dirs_here = translator.shape[2]
    up_theta = theta_table(TF, TP)
    up_phi = phi_table(PF, PP)
    octant = fine_slot % 8
    local_parent = fine_slot // 8 % parents_here
    onehot = (local_parent[None, :] == jnp.arange(parents_here, dtype=jnp.int32)[:, None]).astype(
        jnp.float32
    )
    cos_table, sin_table = octant_phase(octant, dir_index * theta_here, theta_here, TP, PP)
    cos_table = cos_table[:, :, None, :]
    sin_table = sin_table[:, :, None, :]
    pattern = outgoing.reshape(fine_here, channels, TF, PF)
    raised = jnp.einsum("ut,fctp->fcup", up_theta, pattern, precision=highest)
    raised = jnp.einsum("qp,fcup->fucq", up_phi, raised, precision=highest)
    spread = lax.all_to_all(raised, "dir", split_axis=1, concat_axis=0, tiled=True)
    real_part = spread[:, :, :excite]
    imag_part = spread[:, :, excite:]
    shifted = jnp.concatenate(
        [
            real_part * cos_table + imag_part * sin_table,
            imag_part * cos_table - real_part * sin_table,
        ],
        axis=2,
    )
    parent_out = jnp.einsum("pf,fucq->pcuq", onehot, shifted, precision=highest)
    parent_out = parent_out.reshape(parents_here, channels, dirs_here)
    split_here = dirs_here // box_count
    sectioned = jnp.swapaxes(
        parent_out.reshape(parents_here, channels, box_count, split_here), 1, 2
    )
    sectioned = sectioned.reshape(parents_here, box_count, channels * split_here)
    gathered = lax.all_to_all(sectioned, "box", split_axis=1, concat_axis=0, tiled=True)
    sources = gathered.reshape(box_count * parents_here, 2, excite, split_here)
    kernel_rows = lax.dynamic_slice_in_dim(translator, box_index * split_here, split_here, 2)
    translated = translate(sources, kernel_rows, list_partner, list_kind, list_count)
    translated = translated.reshape(box_count * parents_here, 1, channels * split_here)
    returned = lax.all_to_all(translated, "box", split_axis=0, concat_axis=1, tiled=True)
    incoming = jnp.swapaxes(returned.reshape(parents_here, box_count, channels, split_here), 1, 2)
    incoming = incoming.reshape(parents_here, channels, dirs_here)
    fields = incoming.reshape(parents_here, channels, theta_here, PP)
    spread_back = jnp.einsum("pf,pcuq->fucq", onehot, fields, precision=highest)
    real_part = spread_back[:, :, :excite]
    imag_part = spread_back[:, :, excite:]
    shifted_back = jnp.concatenate(
        [
            real_part * cos_table - imag_part * sin_table,
            imag_part * cos_table + real_part * sin_table,
        ],
        axis=2,
    )
    arrived_back = lax.all_to_all(shifted_back, "dir", split_axis=0, concat_axis=1, tiled=True)
    arrived_back = jnp.einsum("qp,fucq->fucp", up_phi, arrived_back, precision=highest) * (PF / PP)
    result = jnp.einsum("ut,fucp->fctp", up_theta, arrived_back, precision=highest) * (TF / TP)
    return result.reshape(fine_here, channels, TF * PF)


def np_theta(fine_count, coarse_count):
    fine_angle = (np.arange(fine_count) + 0.5) * (np.pi / fine_count)
    coarse_angle = (np.arange(coarse_count) + 0.5) * (np.pi / coarse_count)
    orders = np.arange(1, fine_count)
    products = np.cos(coarse_angle[:, None, None] * orders) * np.cos(
        fine_angle[None, :, None] * orders
    )
    return (1.0 + 2.0 * products.sum(2)) / fine_count


def np_phi(fine_count, coarse_count):
    fine_angle = np.arange(fine_count) * (2.0 * np.pi / fine_count)
    coarse_angle = np.arange(coarse_count) * (2.0 * np.pi / coarse_count)
    offset = coarse_angle[:, None] - fine_angle[None, :]
    orders = np.arange(1, fine_count // 2)
    series = np.cos(offset[:, :, None] * orders).sum(2)
    return (1.0 + 2.0 * series + np.cos(offset * (fine_count // 2))) / fine_count


def np_phase(channels):
    polar = (np.arange(TP) + 0.5) * (np.pi / TP)
    azimuth = np.arange(PP) * (2.0 * np.pi / PP)
    octant = np.arange(8)
    signs = [2.0 * (octant // step % 2) - 1.0 for step in (1, 2, 4)]
    along = [
        np.sin(polar)[:, None] * np.cos(azimuth)[None, :],
        np.sin(polar)[:, None] * np.sin(azimuth)[None, :],
        np.cos(polar)[:, None] + 0.0 * azimuth[None, :],
    ]
    angle = wave_shift * sum(s[:, None, None] * a[None] for s, a in zip(signs, along))
    half = channels // 2
    turn = np.where(np.arange(channels) < half, 1.0, -1.0)
    sin_table = np.sin(angle)[:, :, None, :] * turn[None, None, :, None]
    cos_table = np.broadcast_to(np.cos(angle)[:, :, None, :], sin_table.shape)
    return cos_table.astype(np.float32), sin_table.astype(np.float32)


def np_split(values):
    high = values.astype(ml_dtypes.bfloat16)
    low = (values - high.astype(np.float64)).astype(ml_dtypes.bfloat16)
    return high, low


def tables(channels):
    theta = np_theta(TF, TP)
    phi = np_phi(PF, PP)
    eye = np.eye(channels)
    order = np.concatenate([np.arange(0, TF, 2), np.arange(1, TF, 2)])
    theta = theta[:, order]
    up_phi = np.kron(np.eye(2), phi.T)
    up_theta = np.kron(theta, eye)
    down_theta = np.kron(theta.T, eye) * (TF / TP)
    down_phi = np.kron(np.eye(2), phi) * (PF / PP)
    uph, upl = np_split(up_phi)
    uth, utl = np_split(up_theta)
    dth, dtl = np_split(down_theta)
    dph, dpl = np_split(down_phi)
    return (
        np.concatenate([uph, uph, upl], axis=0),
        np.concatenate([uth, uth, utl], axis=1),
        np.concatenate([dth, dth, dtl], axis=1),
        np.concatenate([dph, dph, dpl], axis=0),
    )


def split3(values, axis):
    high = values.astype(jnp.bfloat16)
    low = (values - high.astype(jnp.float32)).astype(jnp.bfloat16)
    return jnp.concatenate([high, low, high], axis=axis)


def dot(a, b):
    return jnp.dot(a, b, preferred_element_type=jnp.float32)


pair = 2


def raise_kernel(slot_ref, x_ref, phi_ref, theta_ref, cos_ref, sin_ref, out_ref):
    step = pl.program_id(0)
    channels = x_ref.shape[1]
    parents = out_ref.shape[1]

    @pl.when(step == 0)
    def _():
        out_ref[...] = jnp.zeros_like(out_ref)

    stacked = []
    for i in range(pair):
        x = x_ref[i]
        x = jnp.concatenate(
            [x[:, j * 2 * PF : (j + 1) * 2 * PF] for j in range(TF // 2)], axis=0
        )
        y = dot(split3(x, 1), phi_ref[...])
        stacked.append(jnp.concatenate([y[:, :PP], y[:, PP:]], axis=0))
    z = jnp.concatenate(stacked, axis=1)
    raised = dot(theta_ref[...], split3(z, 0))
    for i in range(pair):
        slot = slot_ref[step * pair + i]
        octant = slot % 8
        parent = slot // 8 % parents
        r = raised[:, i * PP : (i + 1) * PP].reshape(TP, channels, PP)
        turned = pltpu.roll(r, channels // 2, 1)
        out_ref[:, parent] += r * cos_ref[octant] + turned * sin_ref[octant]


def lower_kernel(slot_ref, f_ref, phi_ref, theta_ref, cos_ref, sin_ref, out_ref):
    step = pl.program_id(0)
    channels = out_ref.shape[1]
    parents = f_ref.shape[1]
    fields = []
    for i in range(pair):
        slot = slot_ref[step * pair + i]
        octant = slot % 8
        parent = slot // 8 % parents
        r = f_ref[:, parent]
        turned = pltpu.roll(r, channels // 2, 1)
        child = r * cos_ref[octant] - turned * sin_ref[octant]
        fields.append(child.reshape(TP * channels, PP))
    z = dot(theta_ref[...], split3(jnp.concatenate(fields, axis=1), 0))
    half = z.shape[0] // 2
    for i in range(pair):
        part = z[:, i * PP : (i + 1) * PP]
        y = jnp.concatenate([part[:half], part[half:]], axis=1)
        x = dot(split3(y, 1), phi_ref[...])
        out_ref[i] = jnp.concatenate(
            [x[j * channels : (j + 1) * channels] for j in range(TF // 2)], axis=1
        )


def whole_spec(array):
    return pl.BlockSpec(array.shape, lambda *_: (0,) * array.ndim)


def raise_parents(slots, outgoing, parents, consts):
    fine, channels, width = outgoing.shape
    phi, theta, cos_table, sin_table = consts
    shape = (TP, parents, channels, PP)
    return pl.pallas_call(
        raise_kernel,
        out_shape=jax.ShapeDtypeStruct(shape, jnp.float32),
        grid_spec=pltpu.PrefetchScalarGridSpec(
            num_scalar_prefetch=1,
            grid=(fine // pair,),
            in_specs=[
                pl.BlockSpec((pair, channels, width), lambda i, _: (i, 0, 0)),
                whole_spec(phi),
                whole_spec(theta),
                whole_spec(cos_table),
                whole_spec(sin_table),
            ],
            out_specs=pl.BlockSpec(shape, lambda i, _: (0, 0, 0, 0)),
        ),
        compiler_params=pltpu.CompilerParams(vmem_limit_bytes=48 * 2**20),
        name="raise_parents",
    )(slots, outgoing, phi, theta, cos_table, sin_table)


def lower_parents(slots, field, consts):
    parents, channels = field.shape[1:3]
    fine = slots.shape[0]
    phi, theta, cos_table, sin_table = consts
    return pl.pallas_call(
        lower_kernel,
        out_shape=jax.ShapeDtypeStruct((fine, channels, TF * PF), jnp.float32),
        grid_spec=pltpu.PrefetchScalarGridSpec(
            num_scalar_prefetch=1,
            grid=(fine // pair,),
            in_specs=[
                whole_spec(field),
                whole_spec(phi),
                whole_spec(theta),
                whole_spec(cos_table),
                whole_spec(sin_table),
            ],
            out_specs=pl.BlockSpec((pair, channels, TF * PF), lambda i, _: (i, 0, 0)),
        ),
        compiler_params=pltpu.CompilerParams(vmem_limit_bytes=48 * 2**20),
        name="lower_parents",
    )(slots, field, phi, theta, cos_table, sin_table)


MESH = pl.DeviceIdType.MESH


def exchange_kernel(
    p_ref, partner_ref, kind_ref, rows_ref, out_ref,
    sel_ref, op_ref, up_ref, down_ref, band_ref, src_ref, res_ref,
    up_send, up_recv, down_send, down_recv, go_send, go_recv, back_send, back_recv,
    rise_send, rise_recv, sink_send, sink_recv,
    *, targets, channels,
):
    n, boxes, halves, block, width = p_ref.shape
    box = lax.axis_index("box")
    z = lax.axis_index("dir")
    sources = targets
    blocks = sel_ref.shape[0]
    length = partner_ref.shape[1]
    pair_rows = sources * targets

    def remote(src, dst, send, recv, to_box, to_dir):
        return pltpu.make_async_remote_copy(
            src_ref=src, dst_ref=dst, send_sem=send, recv_sem=recv,
            device_id=(to_box, to_dir), device_id_type=MESH,
        )

    def up_copy(h, b, src):
        return remote(src, up_ref.at[h, b], up_send.at[h, b], up_recv.at[h, b], box, z + 1)

    def down_copy(h, b, src):
        return remote(src, down_ref.at[h, b], down_send.at[h, b], down_recv.at[h, b], box, z - 1)

    chunks = n - 1

    def sum_send(g):
        if g >= halves * chunks:
            return
        h, j = divmod(g, chunks)

        @pl.when(z == 0)
        def _():
            if g >= 2:
                h2, j2 = divmod(g - 2, chunks)
                up_copy(h2, n - 1 - j2, p_ref.at[n - 1 - j2, :, h2]).wait_send()
            up_copy(h, n - 1 - j, p_ref.at[n - 1 - j, :, h]).start()

        @pl.when(z == n - 1)
        def _():
            if g >= 2:
                h2, j2 = divmod(g - 2, chunks)
                down_copy(h2, j2, p_ref.at[j2, :, h2]).wait_send()
            down_copy(h, j, p_ref.at[j, :, h]).start()

    def sum_tick(tick):
        h = (tick - 1) // chunks
        j = tick - h * chunks
        up_b = n - 1 - j + z
        down_b = j - (n - 1 - z)

        @pl.when((z > 0) & (z < up_b) & (up_b < n))
        def _():
            copy = up_copy(h, up_b, up_ref.at[h, up_b])
            copy.wait_recv()
            up_ref[h, up_b] += p_ref[up_b, :, h]
            copy.start()

        @pl.when((z < n - 1) & (z > down_b) & (down_b >= 0))
        def _():
            copy = down_copy(h, down_b, down_ref.at[h, down_b])
            copy.wait_recv()
            down_ref[h, down_b] += p_ref[down_b, :, h]
            copy.start()

        sum_send(tick + 1)

    def sum_finish(h):
        band_ref[h] = p_ref[z, :, h]

        @pl.when(z > 0)
        def _():
            up_copy(h, z, up_ref.at[h, z]).wait_recv()
            band_ref[h] += up_ref[h, z]

        @pl.when(z < n - 1)
        def _():
            down_copy(h, z, down_ref.at[h, z]).wait_recv()
            band_ref[h] += down_ref[h, z]

    def sum_drain(h):
        for b in range(n):
            @pl.when((z < b) & (z > 0))
            def _():
                up_copy(h, b, up_ref.at[h, b]).wait_send()

            @pl.when((z > b) & (z < n - 1))
            def _():
                down_copy(h, b, down_ref.at[h, b]).wait_send()

        for j in range(chunks):
            if h * chunks + j >= halves * chunks - 2:
                @pl.when(z == 0)
                def _():
                    up_copy(h, n - 1 - j, p_ref.at[n - 1 - j, :, h]).wait_send()

                @pl.when(z == n - 1)
                def _():
                    down_copy(h, j, p_ref.at[j, :, h]).wait_send()

    def peer(k):
        return lax.rem(box + k, boxes)

    def go_copy(h, k):
        return remote(
            band_ref.at[h, peer(k)], src_ref.at[h, box], go_send.at[h, k], go_recv.at[h, k], peer(k), z
        )

    def back_copy(h, k):
        return remote(
            res_ref.at[h, pl.ds(pl.multiple_of(peer(k) * block, block), block)],
            out_ref.at[z, box, h],
            back_send.at[h, k], back_recv.at[h, k], peer(k), z,
        )

    def go_start(h):
        for k in range(1, boxes):
            go_copy(h, k).start()
        src_ref[h, box] = band_ref[h, box]

    def go_wait(h):
        for k in range(1, boxes):
            go_copy(h, k).wait_recv()

    def back_start(h):
        for k in range(1, boxes):
            back_copy(h, k).start()
        out_ref[z, box, h] = res_ref[h, pl.ds(pl.multiple_of(box * block, block), block)]

    def back_wait(h):
        for k in range(1, boxes):
            back_copy(h, k).wait_recv()

    def rise_copy(h, b):
        piece = out_ref.at[b, :, h]
        return remote(piece, piece, rise_send.at[h, b], rise_recv.at[h, b], box, z + 1)

    def sink_copy(h, b):
        piece = out_ref.at[b, :, h]
        return remote(piece, piece, sink_send.at[h, b], sink_recv.at[h, b], box, z - 1)

    def share_step(h, step):
        @pl.when(z >= step)
        def _():
            if step:
                rise_copy(h, z - step).wait_recv()

            @pl.when(z < n - 1)
            def _():
                rise_copy(h, z - step).start()

        @pl.when(z + step <= n - 1)
        def _():
            if step:
                sink_copy(h, z + step).wait_recv()

            @pl.when(z > 0)
            def _():
                sink_copy(h, z + step).start()

    def share_drain(h):
        for b in range(n):
            @pl.when((z >= b) & (z < n - 1))
            def _():
                rise_copy(h, b).wait_send()

            @pl.when((z <= b) & (z > 0))
            def _():
                sink_copy(h, b).wait_send()

    source_ids = lax.broadcasted_iota(jnp.int32, (sources, length), 0)
    kind_ids = lax.broadcasted_iota(jnp.int32, (blocks * 128, length), 0)

    def count_pairs(p, _):
        partner = partner_ref[pl.ds(p, 1), :]
        kind = kind_ref[pl.ds(p, 1), :]
        a = jnp.where(source_ids == partner, 1.0, 0.0).astype(jnp.bfloat16)
        b = jnp.where(kind_ids == kind, 1.0, 0.0).astype(jnp.bfloat16)
        counts = lax.dot_general(
            a, b, (((1,), (1,)), ((), ())), preferred_element_type=jnp.float32
        )
        for j in range(blocks):
            sel_ref[j, pl.ds(p, sources, stride=targets), :] = counts[:, j * 128 : (j + 1) * 128]
        return 0

    def count_part(part, parts):
        first, last = targets * part // parts, targets * (part + 1) // parts
        lax.fori_loop(first, last, count_pairs, 0, unroll=4)

    def operator_half(h):
        rows = jnp.concatenate(
            [rows_ref[:, i * width : (i + 1) * width] for i in (h, halves + h)], axis=1
        )
        pad = blocks * 128 - rows.shape[0]
        if pad:
            rows = jnp.concatenate([rows, jnp.zeros((pad, 2 * width), jnp.float32)], axis=0)
        high = rows.astype(jnp.bfloat16)
        low = (rows - high.astype(jnp.float32)).astype(jnp.bfloat16)
        both = jnp.concatenate([high, low], axis=0)
        tile = 512

        def one_tile(i, _):
            start = pl.multiple_of(i * tile, tile)
            chosen = jnp.concatenate(
                [sel_ref[j, pl.ds(start, tile), :] for j in range(blocks)], axis=1
            ).astype(jnp.bfloat16)
            op_ref[h, pl.ds(start, tile), :] = dot(
                jnp.concatenate([chosen, chosen], axis=1), both
            )
            return 0

        lax.fori_loop(0, pair_rows // tile, one_tile, 0)

    def apply_half(h, part, parts):
        half = channels // 2
        group = 2
        per_box = block // channels

        def add_source(s, sums, first):
            giver = s // per_box
            row0 = (s % per_box) * channels
            fields = [src_ref[h, giver, pl.ds(row0 + c, 1), :] for c in range(channels)]
            out = []
            for g in range(group):
                row = pl.multiple_of(s * targets + first + g * 8, 8)
                real = op_ref[h, pl.ds(row, 8), 0:width]
                imag = op_ref[h, pl.ds(row, 8), width : 2 * width]
                mine = sums[g * channels : (g + 1) * channels]
                for e in range(half):
                    out.append(mine[e] + real * fields[e] - imag * fields[half + e])
                for e in range(half):
                    out.append(mine[half + e] + real * fields[half + e] + imag * fields[e])
            return tuple(out)

        for first in range(targets * part // parts, targets * (part + 1) // parts, group * 8):
            sums = tuple(jnp.zeros((8, width), jnp.float32) for _ in range(group * channels))
            sums = lax.fori_loop(
                0, sources, functools.partial(add_source, first=first), sums, unroll=4
            )
            for g in range(group):
                for c in range(channels):
                    start = (first + g * 8) * channels + c
                    res_ref[h, pl.ds(start, 8, stride=channels), :] = sums[g * channels + c]

    barrier = pltpu.get_barrier_semaphore()
    for k in range(1, boxes):
        pl.semaphore_signal(barrier, inc=1, device_id=(peer(k), z), device_id_type=MESH)

    @pl.when(z > 0)
    def _():
        pl.semaphore_signal(barrier, inc=1, device_id=(box, z - 1), device_id_type=MESH)

    @pl.when(z < n - 1)
    def _():
        pl.semaphore_signal(barrier, inc=1, device_id=(box, z + 1), device_id_type=MESH)

    ends = jnp.where(z > 0, 1, 0) + jnp.where(z < n - 1, 1, 0)
    pl.semaphore_wait(barrier, boxes - 1 + ends)

    sum_send(0)
    sum_send(1)
    for h in range(halves):
        tick = h * chunks
        for step in range(1, chunks + 1):
            if h == 0 and step < chunks:
                count_part(step - 1, chunks - 1)
            if h == 0 and step == chunks:
                operator_half(h)
            if h and step == 1:
                apply_half(h - 1, 0, 2)
            if h and step == 2:
                apply_half(h - 1, 1, 2)
                back_start(h - 1)
            if h and step == chunks:
                back_wait(h - 1)
                share_step(h - 1, 0)
                operator_half(h)
            sum_tick(tick + step)
        sum_finish(h)
        go_start(h)
        if h:
            share_step(h - 1, 1)
        go_wait(h)
    apply_half(halves - 1, 0, 2)
    apply_half(halves - 1, 1, 2)
    back_start(halves - 1)
    if halves > 1:
        share_step(halves - 2, 2)
    last = halves - 1
    back_wait(last)
    share_step(last, 0)
    for h in range(halves):
        for step in range(3 if h == last - 1 else 1, n):
            share_step(h, step)
    for h in range(halves):
        sum_drain(h)
        share_drain(h)
        for k in range(1, boxes):
            go_copy(h, k).wait_send()
            back_copy(h, k).wait_send()


def exchange(raised, partner, kind, rows, n, boxes, targets):
    polar, parents, channels, width = raised.shape
    halves = polar // n // boxes
    block = parents * channels
    kinds = rows.shape[0]
    kind_blocks = -(-kinds // 128)
    shape = (n, boxes, halves, block, width)
    vmem = pl.BlockSpec(memory_space=pltpu.VMEM)
    dma = pltpu.SemaphoreType.DMA
    out = pl.pallas_call(
        functools.partial(exchange_kernel, targets=targets, channels=channels),
        out_shape=jax.ShapeDtypeStruct(shape, jnp.float32),
        in_specs=[vmem] * 4,
        out_specs=vmem,
        scratch_shapes=[
            pltpu.VMEM((kind_blocks, targets * targets, 128), jnp.float32),
            pltpu.VMEM((halves, targets * targets, 2 * width), jnp.float32),
            pltpu.VMEM((halves, n, boxes, block, width), jnp.float32),
            pltpu.VMEM((halves, n, boxes, block, width), jnp.float32),
            pltpu.VMEM((halves, boxes, block, width), jnp.float32),
            pltpu.VMEM((halves, boxes, block, width), jnp.float32),
            pltpu.VMEM((halves, targets * channels, width), jnp.float32),
        ]
        + [dma((halves, n))] * 4
        + [dma((halves, boxes))] * 4
        + [dma((halves, n))] * 4,
        compiler_params=pltpu.CompilerParams(
            vmem_limit_bytes=52 * 2**20, collective_id=0, has_side_effects=True
        ),
        name="exchange",
    )(raised.reshape(shape), partner, kind, rows)
    return out.reshape(raised.shape)


def body(outgoing, fine_slot, translator, list_partner, list_kind, list_count):
    dir_count = lax.axis_size("dir")
    box_count = lax.axis_size("box")
    if TP // dir_count % box_count:
        return general_body(
            outgoing, fine_slot, translator, list_partner, list_kind, list_count
        )
    box_index = lax.axis_index("box")
    dir_index = lax.axis_index("dir")
    fine_here, channels, _ = outgoing.shape
    parents_here = fine_slot.shape[0] // 8
    targets, length = list_partner.shape
    kinds, _, dirs_here = translator.shape
    split_here = dirs_here // box_count
    rows_here = split_here // PP

    up_phi, up_theta, down_theta, down_phi = tables(channels)
    cos_table, sin_table = (jnp.asarray(t) for t in np_phase(channels))
    slots = lax.dynamic_slice_in_dim(fine_slot, dir_index * fine_here, fine_here, 0)
    alive = jnp.arange(length, dtype=jnp.int32)[None, :] < list_count[:, None]
    partner = jnp.where(alive, list_partner, -1)
    rows = lax.dynamic_slice_in_dim(translator, box_index * split_here, split_here, 2)
    rows = rows.reshape(kinds, 2 * split_here)

    raised = raise_parents(
        slots, outgoing, parents_here, (jnp.asarray(up_phi), jnp.asarray(up_theta), cos_table, sin_table)
    )
    field = exchange(raised, partner, list_kind, rows, dir_count, box_count, targets)
    return lower_parents(
        slots, field, (jnp.asarray(down_phi), jnp.asarray(down_theta), cos_table, sin_table)
    )


def solution(mesh):
    placed = (P(("box", "dir"), None, None), P("box"), P(None, None, "dir"), P(), P(), P())
    return jax.shard_map(
        body, mesh=mesh, in_specs=placed, out_specs=P(("box", "dir"), None, None), check_vma=False
    )
```

```python
import functools

import jax
import jax.numpy as jnp
import ml_dtypes
import numpy as np
from jax import lax
from jax.experimental import pallas as pl
from jax.experimental.pallas import tpu as pltpu
from jax.sharding import PartitionSpec as P

TF = 32
PF = 64
TP = 64
PP = 128


wave_shift = 5.0
highest = lax.Precision.HIGHEST


def theta_table(fine_count, coarse_count):
    fine_angle = (jnp.arange(fine_count, dtype=jnp.float32) + 0.5) * (jnp.pi / fine_count)
    coarse_angle = (jnp.arange(coarse_count, dtype=jnp.float32) + 0.5) * (jnp.pi / coarse_count)
    orders = jnp.arange(1, fine_count, dtype=jnp.float32)
    products = jnp.cos(coarse_angle[:, None, None] * orders) * jnp.cos(
        fine_angle[None, :, None] * orders
    )
    return (1.0 + 2.0 * jnp.sum(products, axis=2)) / fine_count


def phi_table(fine_count, coarse_count):
    fine_angle = jnp.arange(fine_count, dtype=jnp.float32) * (2.0 * jnp.pi / fine_count)
    coarse_angle = jnp.arange(coarse_count, dtype=jnp.float32) * (2.0 * jnp.pi / coarse_count)
    offset = coarse_angle[:, None] - fine_angle[None, :]
    orders = jnp.arange(1, fine_count // 2, dtype=jnp.float32)
    series = jnp.sum(jnp.cos(offset[:, :, None] * orders), axis=2)
    return (1.0 + 2.0 * series + jnp.cos(offset * (fine_count // 2))) / fine_count


def octant_phase(octant, first_theta, theta_count, coarse_theta, coarse_phi):
    theta_index = first_theta + jnp.arange(theta_count, dtype=jnp.int32)
    polar = (theta_index.astype(jnp.float32) + 0.5) * (jnp.pi / coarse_theta)
    azimuth = jnp.arange(coarse_phi, dtype=jnp.float32) * (2.0 * jnp.pi / coarse_phi)
    along_x = jnp.sin(polar)[:, None] * jnp.cos(azimuth)[None, :]
    along_y = jnp.sin(polar)[:, None] * jnp.sin(azimuth)[None, :]
    along_z = jnp.cos(polar)[:, None] + 0.0 * azimuth[None, :]
    sign_x = (2 * (octant % 2) - 1).astype(jnp.float32)
    sign_y = (2 * (octant // 2 % 2) - 1).astype(jnp.float32)
    sign_z = (2 * (octant // 4) - 1).astype(jnp.float32)
    phase_angle = wave_shift * (
        sign_x[:, None, None] * along_x[None]
        + sign_y[:, None, None] * along_y[None]
        + sign_z[:, None, None] * along_z[None]
    )
    return (jnp.cos(phase_angle), jnp.sin(phase_angle))


def translate(sources, kernel_table, partner, kind, count):
    targets, length = partner.shape
    source_rows, _, excite, lanes = sources.shape
    kinds = kernel_table.shape[0]
    blocks = 7
    block_width = length // blocks
    flat_sources = sources.reshape(source_rows, 2 * excite * lanes)
    flat_kernel = kernel_table.reshape(kinds, 2 * lanes)
    source_ids = jnp.arange(source_rows, dtype=jnp.int32)
    kind_ids = jnp.arange(kinds, dtype=jnp.int32)

    def add_block(block_step, running):
        begin_at = block_step * block_width
        near_rows = lax.dynamic_slice_in_dim(partner, begin_at, block_width, 1)
        kind_rows = lax.dynamic_slice_in_dim(kind, begin_at, block_width, 1)
        position = begin_at + jnp.arange(block_width, dtype=jnp.int32)
        alive_mask = (position[None, :] < count[:, None]).astype(jnp.float32)
        select_source = (
            (near_rows[:, :, None] == source_ids)
            .astype(jnp.float32)
            .reshape(targets * block_width, source_rows)
        )
        select_kind = (
            (kind_rows[:, :, None] == kind_ids).astype(jnp.float32) * alive_mask[:, :, None]
        ).reshape(targets * block_width, kinds)
        picked = jnp.dot(
            select_source, flat_sources, precision=highest, preferred_element_type=jnp.float32
        )
        picked = picked.reshape(targets, block_width, 2, excite, lanes)
        factor = jnp.dot(
            select_kind, flat_kernel, precision=highest, preferred_element_type=jnp.float32
        )
        factor = factor.reshape(targets, block_width, 2, 1, lanes)
        along_real = factor[:, :, 0]
        along_imag = factor[:, :, 1]
        real_part = picked[:, :, 0]
        imag_part = picked[:, :, 1]
        new_real = jnp.sum(along_real * real_part - along_imag * imag_part, axis=1)
        new_imag = jnp.sum(along_real * imag_part + along_imag * real_part, axis=1)
        return running + jnp.stack([new_real, new_imag], axis=1)

    initial = jnp.zeros((targets, 2, excite, lanes), jnp.float32)
    return lax.fori_loop(0, blocks, add_block, initial)


def general_body(outgoing, fine_slot, translator, list_partner, list_kind, list_count):
    dir_count = lax.axis_size("dir")
    box_count = lax.axis_size("box")
    box_index = lax.axis_index("box")
    dir_index = lax.axis_index("dir")
    channels = outgoing.shape[1]
    excite = channels // 2
    fine_here = outgoing.shape[0]
    row_boxes = fine_slot.shape[0]
    parents_here = row_boxes // 8
    theta_here = TP // dir_count
    dirs_here = translator.shape[2]
    up_theta = theta_table(TF, TP)
    up_phi = phi_table(PF, PP)
    octant = fine_slot % 8
    local_parent = fine_slot // 8 % parents_here
    onehot = (local_parent[None, :] == jnp.arange(parents_here, dtype=jnp.int32)[:, None]).astype(
        jnp.float32
    )
    cos_table, sin_table = octant_phase(octant, dir_index * theta_here, theta_here, TP, PP)
    cos_table = cos_table[:, :, None, :]
    sin_table = sin_table[:, :, None, :]
    pattern = outgoing.reshape(fine_here, channels, TF, PF)
    raised = jnp.einsum("ut,fctp->fcup", up_theta, pattern, precision=highest)
    raised = jnp.einsum("qp,fcup->fucq", up_phi, raised, precision=highest)
    spread = lax.all_to_all(raised, "dir", split_axis=1, concat_axis=0, tiled=True)
    real_part = spread[:, :, :excite]
    imag_part = spread[:, :, excite:]
    shifted = jnp.concatenate(
        [
            real_part * cos_table + imag_part * sin_table,
            imag_part * cos_table - real_part * sin_table,
        ],
        axis=2,
    )
    parent_out = jnp.einsum("pf,fucq->pcuq", onehot, shifted, precision=highest)
    parent_out = parent_out.reshape(parents_here, channels, dirs_here)
    split_here = dirs_here // box_count
    sectioned = jnp.swapaxes(
        parent_out.reshape(parents_here, channels, box_count, split_here), 1, 2
    )
    sectioned = sectioned.reshape(parents_here, box_count, channels * split_here)
    gathered = lax.all_to_all(sectioned, "box", split_axis=1, concat_axis=0, tiled=True)
    sources = gathered.reshape(box_count * parents_here, 2, excite, split_here)
    kernel_rows = lax.dynamic_slice_in_dim(translator, box_index * split_here, split_here, 2)
    translated = translate(sources, kernel_rows, list_partner, list_kind, list_count)
    translated = translated.reshape(box_count * parents_here, 1, channels * split_here)
    returned = lax.all_to_all(translated, "box", split_axis=0, concat_axis=1, tiled=True)
    incoming = jnp.swapaxes(returned.reshape(parents_here, box_count, channels, split_here), 1, 2)
    incoming = incoming.reshape(parents_here, channels, dirs_here)
    fields = incoming.reshape(parents_here, channels, theta_here, PP)
    spread_back = jnp.einsum("pf,pcuq->fucq", onehot, fields, precision=highest)
    real_part = spread_back[:, :, :excite]
    imag_part = spread_back[:, :, excite:]
    shifted_back = jnp.concatenate(
        [
            real_part * cos_table - imag_part * sin_table,
            imag_part * cos_table + real_part * sin_table,
        ],
        axis=2,
    )
    arrived_back = lax.all_to_all(shifted_back, "dir", split_axis=0, concat_axis=1, tiled=True)
    arrived_back = jnp.einsum("qp,fucq->fucp", up_phi, arrived_back, precision=highest) * (PF / PP)
    result = jnp.einsum("ut,fucp->fctp", up_theta, arrived_back, precision=highest) * (TF / TP)
    return result.reshape(fine_here, channels, TF * PF)


def np_theta(fine_count, coarse_count):
    fine_angle = (np.arange(fine_count) + 0.5) * (np.pi / fine_count)
    coarse_angle = (np.arange(coarse_count) + 0.5) * (np.pi / coarse_count)
    orders = np.arange(1, fine_count)
    products = np.cos(coarse_angle[:, None, None] * orders) * np.cos(
        fine_angle[None, :, None] * orders
    )
    return (1.0 + 2.0 * products.sum(2)) / fine_count


def np_phi(fine_count, coarse_count):
    fine_angle = np.arange(fine_count) * (2.0 * np.pi / fine_count)
    coarse_angle = np.arange(coarse_count) * (2.0 * np.pi / coarse_count)
    offset = coarse_angle[:, None] - fine_angle[None, :]
    orders = np.arange(1, fine_count // 2)
    series = np.cos(offset[:, :, None] * orders).sum(2)
    return (1.0 + 2.0 * series + np.cos(offset * (fine_count // 2))) / fine_count


def np_phase():
    polar = (np.arange(TP) + 0.5) * (np.pi / TP)
    azimuth = np.arange(PP) * (2.0 * np.pi / PP)
    along = [
        np.sin(polar)[:, None] * np.cos(azimuth)[None, :],
        np.sin(polar)[:, None] * np.sin(azimuth)[None, :],
        np.cos(polar)[:, None] + 0.0 * azimuth[None, :],
    ]
    cx, cy, cz = (np.cos(wave_shift * a) for a in along)
    sx, sy, sz = (np.sin(wave_shift * a) for a in along)
    terms = [
        cx * cy * cz, sx * sy * cz, sx * cy * sz, cx * sy * sz,
        sx * cy * cz, cx * sy * cz, cx * cy * sz, sx * sy * sz,
    ]
    return np.stack(terms).astype(np.float32)


def np_split(values):
    high = values.astype(ml_dtypes.bfloat16)
    low = (values - high.astype(np.float64)).astype(ml_dtypes.bfloat16)
    return high, low


def tables(channels, n, boxes, halves):
    theta = np_theta(TF, TP)
    phi = np_phi(PF, PP)
    eye = np.eye(channels)
    order = np.concatenate([np.arange(0, TF, 2), np.arange(1, TF, 2)])
    theta = theta[:, order]
    up_phi = np.kron(np.eye(2), phi.T)
    up_theta = np.kron(theta, eye)
    down_phi = np.kron(np.eye(2), phi) * (PF / PP)
    uph, upl = np_split(up_phi)
    uth, utl = np_split(up_theta)
    dph, dpl = np_split(down_phi)
    blocks = theta.reshape(n, boxes, halves, TF).transpose(0, 2, 3, 1) * (TF / TP)
    down = []
    for block in blocks.reshape(n * halves, TF, boxes):
        high, low = np_split(np.kron(block, eye))
        down.append(np.concatenate([high, high, low], axis=1))
    return (
        np.concatenate([uph, uph, upl], axis=0),
        np.concatenate([uth, uth, utl], axis=1),
        np.stack(down),
        np.concatenate([dph, dph, dpl], axis=0),
    )


def split3(values, axis):
    high = values.astype(jnp.bfloat16)
    low = (values - high.astype(jnp.float32)).astype(jnp.bfloat16)
    return jnp.concatenate([high, low, high], axis=axis)


def dot(a, b):
    return jnp.dot(a, b, preferred_element_type=jnp.float32)


MESH = pl.DeviceIdType.MESH


def exchange_kernel(
    x_ref, slot_ref, up_phi_ref, up_theta_ref, down_theta_ref, down_phi_ref, phase_ref,
    partner_ref, kind_ref, count_ref, rows_ref, out_ref,
    r_ref, turn_ref, own_ref, p_ref, f_ref, child_ref, low_ref,
    sel_ref, op_ref, up_ref, down_ref, band_ref, src_ref, res_ref,
    up_send, up_recv, down_send, down_recv, go_send, go_recv, back_send, back_recv,
    rise_send, rise_recv, sink_send, sink_recv,
    *, targets, channels,
):
    n, boxes, halves, block, width = p_ref.shape
    box = lax.axis_index("box")
    z = lax.axis_index("dir")
    sources = targets
    blocks = sel_ref.shape[0]
    length = partner_ref.shape[1]
    pair_rows = sources * targets
    fine = x_ref.shape[0]
    parents = block // channels
    turn_sign = jnp.where(
        lax.broadcasted_iota(jnp.int32, (channels, width), 0) < channels // 2, 1.0, -1.0
    )

    def raise_pair(i, _):
        stacked = []
        for f in range(2):
            x = x_ref[2 * i + f]
            x = jnp.concatenate(
                [x[:, j * 2 * PF : (j + 1) * 2 * PF] for j in range(TF // 2)], axis=0
            )
            y = dot(split3(x, 1), up_phi_ref[...])
            stacked.append(jnp.concatenate([y[:, :PP], y[:, PP:]], axis=0))
        z3 = split3(jnp.concatenate(stacked, axis=1), 0)
        raised = dot(up_theta_ref[...], z3)
        r_ref[2 * i] = raised[:, :PP]
        r_ref[2 * i + 1] = raised[:, PP:]
        return 0

    def turn_one(f, _):
        slot = slot_ref[z * fine + f]
        octant = slot % 8
        parent = slot // 8 % parents
        x = (2 * (octant % 2) - 1).astype(jnp.float32)
        y = (2 * (octant // 2 % 2) - 1).astype(jnp.float32)
        w = (2 * (octant // 4) - 1).astype(jnp.float32)
        t = [phase_ref[i] for i in range(8)]
        turn_ref[f, 0] = t[0] - (x * y) * t[1] - (x * w) * t[2] - (y * w) * t[3]
        turn_ref[f, 1] = x * t[4] + y * t[5] + w * t[6] - (x * y * w) * t[7]
        rows = lax.broadcasted_iota(jnp.int32, (parents, width), 0)
        own_ref[f] = jnp.where(rows == parent, 1.0, 0.0)
        return 0

    def make_piece(b, h):
        def one_row(bb, _):
            u = (b * boxes + bb) * halves + h
            sums = [jnp.zeros((channels, width), jnp.float32) for _ in range(parents)]
            for f in range(fine):
                r = r_ref[f, pl.ds(pl.multiple_of(u * channels, channels), channels), :]
                cos = turn_ref[f, 0, pl.ds(u, 1), :]
                sin = turn_ref[f, 1, pl.ds(u, 1), :]
                moved = r * cos + pltpu.roll(r, channels // 2, 0) * (turn_sign * sin)
                for p in range(parents):
                    sums[p] = sums[p] + moved * own_ref[f, p : p + 1, :]
            for p in range(parents):
                p_ref[b, bb, h, p * channels : (p + 1) * channels, :] = sums[p]
            return 0

        lax.fori_loop(0, boxes, one_row, 0)

    def band_at(k):
        middle = n - 1 - k // 2 if k % 2 == 0 else k // 2
        return jnp.where(z == 0, n - 1 - k, jnp.where(z == n - 1, k, middle))

    def lower_piece(b, h):
        def two_rows(i, _):
            fields = [
                [
                    f_ref[b, 2 * i + r, h, p * channels : (p + 1) * channels, :]
                    for p in range(parents)
                ]
                for r in range(2)
            ]
            first = (b * boxes + 2 * i) * halves + h
            for f in range(fine):
                both = []
                for r in range(2):
                    u = first + r * halves
                    mine = fields[r][0] * own_ref[f, 0:1, :]
                    for p in range(1, parents):
                        mine = mine + fields[r][p] * own_ref[f, p : p + 1, :]
                    cos = turn_ref[f, 0, pl.ds(u, 1), :]
                    sin = turn_ref[f, 1, pl.ds(u, 1), :]
                    both.append(
                        mine * cos - pltpu.roll(mine, channels // 2, 0) * (turn_sign * sin)
                    )
                child = jnp.concatenate(both, axis=0)
                high = child.astype(jnp.bfloat16)
                low = (child - high.astype(jnp.float32)).astype(jnp.bfloat16)
                row = pl.multiple_of(i * 2 * channels, 2 * channels)
                lanes = slice(f * width, (f + 1) * width)
                child_ref[0, pl.ds(row, 2 * channels), lanes] = high
                child_ref[1, pl.ds(row, 2 * channels), lanes] = low
            return 0

        lax.fori_loop(0, boxes // 2, two_rows, 0)
        tile = 4 * width

        def add_tile(i, _):
            lanes = pl.ds(pl.multiple_of(i * tile, tile), tile)
            high = child_ref[0, :, lanes]
            low = child_ref[1, :, lanes]
            low_ref[:, lanes] += dot(
                down_theta_ref[b * halves + h], jnp.concatenate([high, low, high], axis=0)
            )
            return 0

        lax.fori_loop(0, fine * width // tile, add_tile, 0)

    def lower_step(h, step):
        if step == 0:
            lower_piece(z, h)
            return

        def one_side(i, _):
            b = jnp.where(i == 0, z - step, z + step)

            @pl.when((b >= 0) & (b < n))
            def _():
                lower_piece(b, h)

            return 0

        lax.fori_loop(0, 2, one_side, 0)

    def lower_last(f, _):
        part = low_ref[:, pl.ds(pl.multiple_of(f * width, width), width)]
        half = part.shape[0] // 2
        y = jnp.concatenate([part[:half], part[half:]], axis=1)
        x = dot(split3(y, 1), down_phi_ref[...])
        out_ref[f] = jnp.concatenate(
            [x[j * channels : (j + 1) * channels] for j in range(TF // 2)], axis=1
        )
        return 0

    def remote(src, dst, send, recv, to_box, to_dir):
        return pltpu.make_async_remote_copy(
            src_ref=src, dst_ref=dst, send_sem=send, recv_sem=recv,
            device_id=(to_box, to_dir), device_id_type=MESH,
        )

    def up_copy(h, b, src):
        return remote(src, up_ref.at[h, b], up_send.at[h, b], up_recv.at[h, b], box, z + 1)

    def down_copy(h, b, src):
        return remote(src, down_ref.at[h, b], down_send.at[h, b], down_recv.at[h, b], box, z - 1)

    chunks = n - 1

    def sum_send(g):
        if g >= halves * chunks:
            return
        h, j = divmod(g, chunks)

        @pl.when(z == 0)
        def _():
            if g >= 2:
                h2, j2 = divmod(g - 2, chunks)
                up_copy(h2, n - 1 - j2, p_ref.at[n - 1 - j2, :, h2]).wait_send()
            up_copy(h, n - 1 - j, p_ref.at[n - 1 - j, :, h]).start()

        @pl.when(z == n - 1)
        def _():
            if g >= 2:
                h2, j2 = divmod(g - 2, chunks)
                down_copy(h2, j2, p_ref.at[j2, :, h2]).wait_send()
            down_copy(h, j, p_ref.at[j, :, h]).start()

    def sum_tick(tick):
        h = (tick - 1) // chunks
        j = tick - h * chunks
        up_b = n - 1 - j + z
        down_b = j - (n - 1 - z)

        @pl.when((z > 0) & (z < up_b) & (up_b < n))
        def _():
            copy = up_copy(h, up_b, up_ref.at[h, up_b])
            copy.wait_recv()
            up_ref[h, up_b] += p_ref[up_b, :, h]
            copy.start()

        @pl.when((z < n - 1) & (z > down_b) & (down_b >= 0))
        def _():
            copy = down_copy(h, down_b, down_ref.at[h, down_b])
            copy.wait_recv()
            down_ref[h, down_b] += p_ref[down_b, :, h]
            copy.start()

        sum_send(tick + 1)

    def sum_finish(h):
        band_ref[h] = p_ref[z, :, h]

        @pl.when(z > 0)
        def _():
            up_copy(h, z, up_ref.at[h, z]).wait_recv()
            band_ref[h] += up_ref[h, z]

        @pl.when(z < n - 1)
        def _():
            down_copy(h, z, down_ref.at[h, z]).wait_recv()
            band_ref[h] += down_ref[h, z]

    def sum_drain(h):
        for b in range(n):
            @pl.when((z < b) & (z > 0))
            def _():
                up_copy(h, b, up_ref.at[h, b]).wait_send()

            @pl.when((z > b) & (z < n - 1))
            def _():
                down_copy(h, b, down_ref.at[h, b]).wait_send()

        for j in range(chunks):
            if h * chunks + j >= halves * chunks - 2:
                @pl.when(z == 0)
                def _():
                    up_copy(h, n - 1 - j, p_ref.at[n - 1 - j, :, h]).wait_send()

                @pl.when(z == n - 1)
                def _():
                    down_copy(h, j, p_ref.at[j, :, h]).wait_send()

    def peer(k):
        return lax.rem(box + k, boxes)

    def go_copy(h, k):
        return remote(
            band_ref.at[h, peer(k)], src_ref.at[h, box], go_send.at[h, k], go_recv.at[h, k], peer(k), z
        )

    def back_copy(h, k):
        return remote(
            res_ref.at[h, pl.ds(pl.multiple_of(peer(k) * block, block), block)],
            f_ref.at[z, box, h],
            back_send.at[h, k], back_recv.at[h, k], peer(k), z,
        )

    def go_start(h):
        for k in range(1, boxes):
            go_copy(h, k).start()
        src_ref[h, box] = band_ref[h, box]

    def go_wait(h):
        for k in range(1, boxes):
            go_copy(h, k).wait_recv()

    def back_start(h):
        for k in range(1, boxes):
            back_copy(h, k).start()
        f_ref[z, box, h] = res_ref[h, pl.ds(pl.multiple_of(box * block, block), block)]

    def back_wait(h):
        for k in range(1, boxes):
            back_copy(h, k).wait_recv()

    def rise_copy(h, b):
        piece = f_ref.at[b, :, h]
        return remote(piece, piece, rise_send.at[h, b], rise_recv.at[h, b], box, z + 1)

    def sink_copy(h, b):
        piece = f_ref.at[b, :, h]
        return remote(piece, piece, sink_send.at[h, b], sink_recv.at[h, b], box, z - 1)

    def share_step(h, step):
        @pl.when(z >= step)
        def _():
            if step:
                rise_copy(h, z - step).wait_recv()

            @pl.when(z < n - 1)
            def _():
                rise_copy(h, z - step).start()

        @pl.when(z + step <= n - 1)
        def _():
            if step:
                sink_copy(h, z + step).wait_recv()

            @pl.when(z > 0)
            def _():
                sink_copy(h, z + step).start()

    def share_drain(h):
        for b in range(n):
            @pl.when((z >= b) & (z < n - 1))
            def _():
                rise_copy(h, b).wait_send()

            @pl.when((z <= b) & (z > 0))
            def _():
                sink_copy(h, b).wait_send()

    source_ids = lax.broadcasted_iota(jnp.int32, (sources, length), 0)
    kind_ids = lax.broadcasted_iota(jnp.int32, (blocks * 128, length), 0)

    def count_pairs(p, _):
        partner = partner_ref[pl.ds(p, 1), :]
        slots = lax.broadcasted_iota(jnp.int32, (1, length), 1)
        partner = jnp.where(slots < count_ref[p], partner, -1)
        kind = kind_ref[pl.ds(p, 1), :]
        a = jnp.where(source_ids == partner, 1.0, 0.0).astype(jnp.bfloat16)
        b = jnp.where(kind_ids == kind, 1.0, 0.0).astype(jnp.bfloat16)
        counts = lax.dot_general(
            a, b, (((1,), (1,)), ((), ())), preferred_element_type=jnp.float32
        )
        for j in range(blocks):
            sel_ref[j, pl.ds(p, sources, stride=targets), :] = counts[:, j * 128 : (j + 1) * 128]
        return 0

    def count_part(part, parts):
        first, last = targets * part // parts, targets * (part + 1) // parts
        lax.fori_loop(first, last, count_pairs, 0, unroll=4)

    def operator_half(h):
        rows = jnp.concatenate(
            [rows_ref[:, i * width : (i + 1) * width] for i in (h, halves + h)], axis=1
        )
        pad = blocks * 128 - rows.shape[0]
        if pad:
            rows = jnp.concatenate([rows, jnp.zeros((pad, 2 * width), jnp.float32)], axis=0)
        high = rows.astype(jnp.bfloat16)
        low = (rows - high.astype(jnp.float32)).astype(jnp.bfloat16)
        both = jnp.concatenate([high, low], axis=0)
        tile = 512

        def one_tile(i, _):
            start = pl.multiple_of(i * tile, tile)
            chosen = jnp.concatenate(
                [sel_ref[j, pl.ds(start, tile), :] for j in range(blocks)], axis=1
            ).astype(jnp.bfloat16)
            op_ref[h, pl.ds(start, tile), :] = dot(
                jnp.concatenate([chosen, chosen], axis=1), both
            )
            return 0

        lax.fori_loop(0, pair_rows // tile, one_tile, 0)

    def apply_half(h, part, parts):
        half = channels // 2
        group = 2
        per_box = block // channels

        def add_source(s, sums, first):
            giver = s // per_box
            row0 = (s % per_box) * channels
            fields = [src_ref[h, giver, pl.ds(row0 + c, 1), :] for c in range(channels)]
            out = []
            for g in range(group):
                row = pl.multiple_of(s * targets + first + g * 8, 8)
                real = op_ref[h, pl.ds(row, 8), 0:width]
                imag = op_ref[h, pl.ds(row, 8), width : 2 * width]
                mine = sums[g * channels : (g + 1) * channels]
                for e in range(half):
                    out.append(mine[e] + real * fields[e] - imag * fields[half + e])
                for e in range(half):
                    out.append(mine[half + e] + real * fields[half + e] + imag * fields[e])
            return tuple(out)

        for first in range(targets * part // parts, targets * (part + 1) // parts, group * 8):
            sums = tuple(jnp.zeros((8, width), jnp.float32) for _ in range(group * channels))
            sums = lax.fori_loop(
                0, sources, functools.partial(add_source, first=first), sums, unroll=4
            )
            for g in range(group):
                for c in range(channels):
                    start = (first + g * 8) * channels + c
                    res_ref[h, pl.ds(start, 8, stride=channels), :] = sums[g * channels + c]

    barrier = pltpu.get_barrier_semaphore()
    for k in range(1, boxes):
        pl.semaphore_signal(barrier, inc=1, device_id=(peer(k), z), device_id_type=MESH)

    @pl.when(z > 0)
    def _():
        pl.semaphore_signal(barrier, inc=1, device_id=(box, z - 1), device_id_type=MESH)

    @pl.when(z < n - 1)
    def _():
        pl.semaphore_signal(barrier, inc=1, device_id=(box, z + 1), device_id_type=MESH)

    ends = jnp.where(z > 0, 1, 0) + jnp.where(z < n - 1, 1, 0)
    lax.fori_loop(0, fine, turn_one, 0)
    lax.fori_loop(0, fine // 2, raise_pair, 0, unroll=2)
    low_ref[...] = jnp.zeros_like(low_ref)
    make_piece(band_at(0), 0)
    pl.semaphore_wait(barrier, boxes - 1 + ends)
    sum_send(0)
    make_piece(band_at(1), 0)
    sum_send(1)
    for i in range(2, n):
        make_piece(band_at(i), 0)

    shared = [0] * halves
    lowered = [0] * halves

    def share_to(h, last_step):
        while shared[h] <= min(last_step, n - 1):
            share_step(h, shared[h])
            shared[h] += 1

    def lower_to(h, last_step):
        while lowered[h] <= min(last_step, n - 1):
            lower_step(h, lowered[h])
            lowered[h] += 1

    for h in range(halves):
        tick = h * chunks
        for step in range(1, chunks + 1):
            if h == 0 and step < chunks:
                count_part(step - 1, chunks - 1)
                if step == 1:
                    for later in range(1, halves):
                        for i in range(n):
                            make_piece(band_at(i), later)
            if h == 0 and step == chunks:
                operator_half(h)
            if h and step == 1:
                apply_half(h - 1, 0, 2)
            if h and step == 2:
                apply_half(h - 1, 1, 2)
                back_start(h - 1)
            if h and step == chunks:
                back_wait(h - 1)
                share_to(h - 1, 0)
                operator_half(h)
            sum_tick(tick + step)
        sum_finish(h)
        go_start(h)
        if h:
            share_to(h - 1, 1)
            lower_to(h - 1, 0)
        go_wait(h)
    last = halves - 1
    apply_half(last, 0, 2)
    apply_half(last, 1, 2)
    back_start(last)
    for h in range(last):
        share_to(h, 2)
        lower_to(h, 1)
    back_wait(last)
    share_to(last, 0)
    for h in range(last):
        share_to(h, n - 1)
        lower_to(h, 2)
    lower_to(last, 0)
    share_to(last, 1)
    for h in range(last):
        lower_to(h, n - 1)
    lower_to(last, 1)
    for step in range(2, n):
        share_to(last, step)
        lower_to(last, step)
    lax.fori_loop(0, fine, lower_last, 0, unroll=4)
    for h in range(halves):
        sum_drain(h)
        share_drain(h)
        for k in range(1, boxes):
            go_copy(h, k).wait_send()
            back_copy(h, k).wait_send()


def exchange(outgoing, slots, partner, kind, count, rows, n, boxes):
    fine, channels, fine_width = outgoing.shape
    parents = slots.shape[0] // 8
    targets = partner.shape[0]
    halves = TP // n // boxes
    block = parents * channels
    kinds = rows.shape[0]
    kind_blocks = -(-kinds // 128)
    shape = (n, boxes, halves, block, PP)
    vmem = pl.BlockSpec(memory_space=pltpu.VMEM)
    smem = pl.BlockSpec(memory_space=pltpu.SMEM)
    dma = pltpu.SemaphoreType.DMA
    consts = [jnp.asarray(t) for t in tables(channels, n, boxes, halves)]
    f32 = jnp.float32
    return pl.pallas_call(
        functools.partial(exchange_kernel, targets=targets, channels=channels),
        out_shape=jax.ShapeDtypeStruct(outgoing.shape, f32),
        in_specs=[vmem, smem] + [vmem] * 7 + [smem, vmem],
        out_specs=vmem,
        scratch_shapes=[
            pltpu.VMEM((fine, TP * channels, PP), f32),
            pltpu.VMEM((fine, 2, TP, PP), f32),
            pltpu.VMEM((fine, parents, PP), f32),
            pltpu.VMEM(shape, f32),
            pltpu.VMEM(shape, f32),
            pltpu.VMEM((2, boxes * channels, fine * PP), jnp.bfloat16),
            pltpu.VMEM((TF * channels, fine * PP), f32),
            pltpu.VMEM((kind_blocks, targets * targets, 128), f32),
            pltpu.VMEM((halves, targets * targets, 2 * PP), f32),
            pltpu.VMEM((halves, n, boxes, block, PP), f32),
            pltpu.VMEM((halves, n, boxes, block, PP), f32),
            pltpu.VMEM((halves, boxes, block, PP), f32),
            pltpu.VMEM((halves, boxes, block, PP), f32),
            pltpu.VMEM((halves, targets * channels, PP), f32),
        ]
        + [dma((halves, n))] * 4
        + [dma((halves, boxes))] * 4
        + [dma((halves, n))] * 4,
        compiler_params=pltpu.CompilerParams(
            vmem_limit_bytes=56 * 2**20, collective_id=0, has_side_effects=True
        ),
        name="exchange",
    )(
        outgoing, slots, *consts, jnp.asarray(np_phase()), partner, kind, count, rows
    )


def body(outgoing, fine_slot, translator, list_partner, list_kind, list_count):
    dir_count = lax.axis_size("dir")
    box_count = lax.axis_size("box")
    fine_here, channels, _ = outgoing.shape
    whole_rows = TP // dir_count % box_count == 0 and dir_count >= 4 and box_count % 2 == 0
    if not whole_rows or fine_here % 4 or channels % 8 or list_partner.shape[0] % 32:
        return general_body(
            outgoing, fine_slot, translator, list_partner, list_kind, list_count
        )
    box_index = lax.axis_index("box")
    kinds, _, dirs_here = translator.shape
    split_here = dirs_here // box_count
    rows = lax.dynamic_slice_in_dim(translator, box_index * split_here, split_here, 2)
    rows = rows.reshape(kinds, 2 * split_here)
    return exchange(
        outgoing, fine_slot, list_partner, list_kind, list_count, rows, dir_count, box_count
    )


def solution(mesh):
    placed = (P(("box", "dir"), None, None), P("box"), P(None, None, "dir"), P(), P(), P())
    return jax.shard_map(
        body, mesh=mesh, in_specs=placed, out_specs=P(("box", "dir"), None, None), check_vma=False
    )
```

```python
import functools

import jax
import jax.numpy as jnp
import ml_dtypes
import numpy as np
from jax import lax
from jax.experimental import pallas as pl
from jax.experimental.pallas import tpu as pltpu
from jax.sharding import PartitionSpec as P

TF = 32
PF = 64
TP = 64
PP = 128


wave_shift = 5.0
highest = lax.Precision.HIGHEST


def theta_table(fine_count, coarse_count):
    fine_angle = (jnp.arange(fine_count, dtype=jnp.float32) + 0.5) * (jnp.pi / fine_count)
    coarse_angle = (jnp.arange(coarse_count, dtype=jnp.float32) + 0.5) * (jnp.pi / coarse_count)
    orders = jnp.arange(1, fine_count, dtype=jnp.float32)
    products = jnp.cos(coarse_angle[:, None, None] * orders) * jnp.cos(
        fine_angle[None, :, None] * orders
    )
    return (1.0 + 2.0 * jnp.sum(products, axis=2)) / fine_count


def phi_table(fine_count, coarse_count):
    fine_angle = jnp.arange(fine_count, dtype=jnp.float32) * (2.0 * jnp.pi / fine_count)
    coarse_angle = jnp.arange(coarse_count, dtype=jnp.float32) * (2.0 * jnp.pi / coarse_count)
    offset = coarse_angle[:, None] - fine_angle[None, :]
    orders = jnp.arange(1, fine_count // 2, dtype=jnp.float32)
    series = jnp.sum(jnp.cos(offset[:, :, None] * orders), axis=2)
    return (1.0 + 2.0 * series + jnp.cos(offset * (fine_count // 2))) / fine_count


def octant_phase(octant, first_theta, theta_count, coarse_theta, coarse_phi):
    theta_index = first_theta + jnp.arange(theta_count, dtype=jnp.int32)
    polar = (theta_index.astype(jnp.float32) + 0.5) * (jnp.pi / coarse_theta)
    azimuth = jnp.arange(coarse_phi, dtype=jnp.float32) * (2.0 * jnp.pi / coarse_phi)
    along_x = jnp.sin(polar)[:, None] * jnp.cos(azimuth)[None, :]
    along_y = jnp.sin(polar)[:, None] * jnp.sin(azimuth)[None, :]
    along_z = jnp.cos(polar)[:, None] + 0.0 * azimuth[None, :]
    sign_x = (2 * (octant % 2) - 1).astype(jnp.float32)
    sign_y = (2 * (octant // 2 % 2) - 1).astype(jnp.float32)
    sign_z = (2 * (octant // 4) - 1).astype(jnp.float32)
    phase_angle = wave_shift * (
        sign_x[:, None, None] * along_x[None]
        + sign_y[:, None, None] * along_y[None]
        + sign_z[:, None, None] * along_z[None]
    )
    return (jnp.cos(phase_angle), jnp.sin(phase_angle))


def translate(sources, kernel_table, partner, kind, count):
    targets, length = partner.shape
    source_rows, _, excite, lanes = sources.shape
    kinds = kernel_table.shape[0]
    blocks = 7
    block_width = length // blocks
    flat_sources = sources.reshape(source_rows, 2 * excite * lanes)
    flat_kernel = kernel_table.reshape(kinds, 2 * lanes)
    source_ids = jnp.arange(source_rows, dtype=jnp.int32)
    kind_ids = jnp.arange(kinds, dtype=jnp.int32)

    def add_block(block_step, running):
        begin_at = block_step * block_width
        near_rows = lax.dynamic_slice_in_dim(partner, begin_at, block_width, 1)
        kind_rows = lax.dynamic_slice_in_dim(kind, begin_at, block_width, 1)
        position = begin_at + jnp.arange(block_width, dtype=jnp.int32)
        alive_mask = (position[None, :] < count[:, None]).astype(jnp.float32)
        select_source = (
            (near_rows[:, :, None] == source_ids)
            .astype(jnp.float32)
            .reshape(targets * block_width, source_rows)
        )
        select_kind = (
            (kind_rows[:, :, None] == kind_ids).astype(jnp.float32) * alive_mask[:, :, None]
        ).reshape(targets * block_width, kinds)
        picked = jnp.dot(
            select_source, flat_sources, precision=highest, preferred_element_type=jnp.float32
        )
        picked = picked.reshape(targets, block_width, 2, excite, lanes)
        factor = jnp.dot(
            select_kind, flat_kernel, precision=highest, preferred_element_type=jnp.float32
        )
        factor = factor.reshape(targets, block_width, 2, 1, lanes)
        along_real = factor[:, :, 0]
        along_imag = factor[:, :, 1]
        real_part = picked[:, :, 0]
        imag_part = picked[:, :, 1]
        new_real = jnp.sum(along_real * real_part - along_imag * imag_part, axis=1)
        new_imag = jnp.sum(along_real * imag_part + along_imag * real_part, axis=1)
        return running + jnp.stack([new_real, new_imag], axis=1)

    initial = jnp.zeros((targets, 2, excite, lanes), jnp.float32)
    return lax.fori_loop(0, blocks, add_block, initial)


def general_body(outgoing, fine_slot, translator, list_partner, list_kind, list_count):
    dir_count = lax.axis_size("dir")
    box_count = lax.axis_size("box")
    box_index = lax.axis_index("box")
    dir_index = lax.axis_index("dir")
    channels = outgoing.shape[1]
    excite = channels // 2
    fine_here = outgoing.shape[0]
    row_boxes = fine_slot.shape[0]
    parents_here = row_boxes // 8
    theta_here = TP // dir_count
    dirs_here = translator.shape[2]
    up_theta = theta_table(TF, TP)
    up_phi = phi_table(PF, PP)
    octant = fine_slot % 8
    local_parent = fine_slot // 8 % parents_here
    onehot = (local_parent[None, :] == jnp.arange(parents_here, dtype=jnp.int32)[:, None]).astype(
        jnp.float32
    )
    cos_table, sin_table = octant_phase(octant, dir_index * theta_here, theta_here, TP, PP)
    cos_table = cos_table[:, :, None, :]
    sin_table = sin_table[:, :, None, :]
    pattern = outgoing.reshape(fine_here, channels, TF, PF)
    raised = jnp.einsum("ut,fctp->fcup", up_theta, pattern, precision=highest)
    raised = jnp.einsum("qp,fcup->fucq", up_phi, raised, precision=highest)
    spread = lax.all_to_all(raised, "dir", split_axis=1, concat_axis=0, tiled=True)
    real_part = spread[:, :, :excite]
    imag_part = spread[:, :, excite:]
    shifted = jnp.concatenate(
        [
            real_part * cos_table + imag_part * sin_table,
            imag_part * cos_table - real_part * sin_table,
        ],
        axis=2,
    )
    parent_out = jnp.einsum("pf,fucq->pcuq", onehot, shifted, precision=highest)
    parent_out = parent_out.reshape(parents_here, channels, dirs_here)
    split_here = dirs_here // box_count
    sectioned = jnp.swapaxes(
        parent_out.reshape(parents_here, channels, box_count, split_here), 1, 2
    )
    sectioned = sectioned.reshape(parents_here, box_count, channels * split_here)
    gathered = lax.all_to_all(sectioned, "box", split_axis=1, concat_axis=0, tiled=True)
    sources = gathered.reshape(box_count * parents_here, 2, excite, split_here)
    kernel_rows = lax.dynamic_slice_in_dim(translator, box_index * split_here, split_here, 2)
    translated = translate(sources, kernel_rows, list_partner, list_kind, list_count)
    translated = translated.reshape(box_count * parents_here, 1, channels * split_here)
    returned = lax.all_to_all(translated, "box", split_axis=0, concat_axis=1, tiled=True)
    incoming = jnp.swapaxes(returned.reshape(parents_here, box_count, channels, split_here), 1, 2)
    incoming = incoming.reshape(parents_here, channels, dirs_here)
    fields = incoming.reshape(parents_here, channels, theta_here, PP)
    spread_back = jnp.einsum("pf,pcuq->fucq", onehot, fields, precision=highest)
    real_part = spread_back[:, :, :excite]
    imag_part = spread_back[:, :, excite:]
    shifted_back = jnp.concatenate(
        [
            real_part * cos_table - imag_part * sin_table,
            imag_part * cos_table + real_part * sin_table,
        ],
        axis=2,
    )
    arrived_back = lax.all_to_all(shifted_back, "dir", split_axis=0, concat_axis=1, tiled=True)
    arrived_back = jnp.einsum("qp,fucq->fucp", up_phi, arrived_back, precision=highest) * (PF / PP)
    result = jnp.einsum("ut,fucp->fctp", up_theta, arrived_back, precision=highest) * (TF / TP)
    return result.reshape(fine_here, channels, TF * PF)


def np_theta(fine_count, coarse_count):
    fine_angle = (np.arange(fine_count) + 0.5) * (np.pi / fine_count)
    coarse_angle = (np.arange(coarse_count) + 0.5) * (np.pi / coarse_count)
    orders = np.arange(1, fine_count)
    products = np.cos(coarse_angle[:, None, None] * orders) * np.cos(
        fine_angle[None, :, None] * orders
    )
    return (1.0 + 2.0 * products.sum(2)) / fine_count


def np_phi(fine_count, coarse_count):
    fine_angle = np.arange(fine_count) * (2.0 * np.pi / fine_count)
    coarse_angle = np.arange(coarse_count) * (2.0 * np.pi / coarse_count)
    offset = coarse_angle[:, None] - fine_angle[None, :]
    orders = np.arange(1, fine_count // 2)
    series = np.cos(offset[:, :, None] * orders).sum(2)
    return (1.0 + 2.0 * series + np.cos(offset * (fine_count // 2))) / fine_count


def np_phase():
    polar = (np.arange(TP) + 0.5) * (np.pi / TP)
    azimuth = np.arange(PP) * (2.0 * np.pi / PP)
    along = [
        np.sin(polar)[:, None] * np.cos(azimuth)[None, :],
        np.sin(polar)[:, None] * np.sin(azimuth)[None, :],
        np.cos(polar)[:, None] + 0.0 * azimuth[None, :],
    ]
    cx, cy, cz = (np.cos(wave_shift * a) for a in along)
    sx, sy, sz = (np.sin(wave_shift * a) for a in along)
    terms = [
        cx * cy * cz, sx * sy * cz, sx * cy * sz, cx * sy * sz,
        sx * cy * cz, cx * sy * cz, cx * cy * sz, sx * sy * sz,
    ]
    return np.stack(terms).astype(np.float32)


def np_split(values):
    high = values.astype(ml_dtypes.bfloat16)
    low = (values - high.astype(np.float64)).astype(ml_dtypes.bfloat16)
    return high, low


def tables(channels, n, boxes, halves):
    theta = np_theta(TF, TP)
    phi = np_phi(PF, PP)
    eye = np.eye(channels)
    order = np.concatenate([np.arange(0, TF, 2), np.arange(1, TF, 2)])
    theta = theta[:, order]
    up_phi = np.kron(np.eye(2), phi.T)
    up_theta = np.kron(theta, eye)
    down_phi = np.kron(np.eye(2), phi) * (PF / PP)
    uph, upl = np_split(up_phi)
    uth, utl = np_split(up_theta)
    dph, dpl = np_split(down_phi)
    blocks = theta.reshape(n, boxes, halves, TF).transpose(0, 2, 3, 1) * (TF / TP)
    down = []
    for block in blocks.reshape(n * halves, TF, boxes):
        high, low = np_split(np.kron(block, eye))
        down.append(np.concatenate([high, high, low], axis=1))
    return (
        np.concatenate([uph, uph, upl], axis=0),
        np.concatenate([uth, uth, utl], axis=1),
        np.stack(down),
        np.concatenate([dph, dph, dpl], axis=0),
    )


def split3(values, axis):
    high = values.astype(jnp.bfloat16)
    low = (values - high.astype(jnp.float32)).astype(jnp.bfloat16)
    return jnp.concatenate([high, low, high], axis=axis)


def dot(a, b):
    return jnp.dot(a, b, preferred_element_type=jnp.float32)


MESH = pl.DeviceIdType.MESH


def exchange_kernel(
    x_ref, slot_ref, up_phi_ref, up_theta_ref, down_theta_ref, down_phi_ref, phase_ref,
    partner_ref, kind_ref, count_ref, rows_ref, out_ref,
    r_ref, turn_ref, own_ref, p_ref, f_ref, child_ref, low_ref,
    sel_ref, op_ref, up_ref, down_ref, band_ref, src_ref, res_ref,
    up_send, up_recv, down_send, down_recv, go_send, go_recv, back_send, back_recv,
    rise_send, rise_recv, sink_send, sink_recv,
    *, targets, channels,
):
    n, boxes, pieces, block, width = p_ref.shape
    rows_here = pieces // 2
    box = lax.axis_index("box")
    z = lax.axis_index("dir")
    sources = targets
    blocks = sel_ref.shape[0]
    length = partner_ref.shape[1]
    pair_rows = sources * targets
    fine = x_ref.shape[0]
    parents = 2 * block // channels
    turn_sign = jnp.where(
        lax.broadcasted_iota(jnp.int32, (channels, width), 0) < channels // 2, 1.0, -1.0
    )

    sublane = lax.broadcasted_iota(jnp.int32, (channels, width), 0)
    outer = sublane % 4 < 2

    def raise_pair(i, _):
        stacked = []
        for f in range(2):
            x = x_ref[2 * i + f]
            x = jnp.concatenate(
                [x[:, j * 2 * PF : (j + 1) * 2 * PF] for j in range(TF // 2)], axis=0
            )
            y = dot(split3(x, 1), up_phi_ref[...])
            stacked.append(jnp.concatenate([y[:, :PP], y[:, PP:]], axis=0))
        z3 = split3(jnp.concatenate(stacked, axis=1), 0)
        raised = dot(up_theta_ref[...], z3)
        r_ref[2 * i] = raised[:, :PP]
        r_ref[2 * i + 1] = raised[:, PP:]
        return 0

    def turn_one(f, _):
        slot = slot_ref[z * fine + f]
        octant = slot % 8
        parent = slot // 8 % parents
        x = (2 * (octant % 2) - 1).astype(jnp.float32)
        y = (2 * (octant // 2 % 2) - 1).astype(jnp.float32)
        w = (2 * (octant // 4) - 1).astype(jnp.float32)
        t = [phase_ref[i] for i in range(8)]
        turn_ref[f, 0] = t[0] - (x * y) * t[1] - (x * w) * t[2] - (y * w) * t[3]
        turn_ref[f, 1] = x * t[4] + y * t[5] + w * t[6] - (x * y * w) * t[7]
        rows = lax.broadcasted_iota(jnp.int32, (parents, width), 0)
        own_ref[f] = jnp.where(rows == parent, 1.0, 0.0)
        return 0

    def make_piece(b, h):
        def one_row(bb, _):
            u = (b * boxes + bb) * rows_here + h
            sums = [jnp.zeros((channels, width), jnp.float32) for _ in range(parents)]
            for f in range(fine):
                r = r_ref[f, pl.ds(pl.multiple_of(u * channels, channels), channels), :]
                cos = turn_ref[f, 0, pl.ds(u, 1), :]
                sin = turn_ref[f, 1, pl.ds(u, 1), :]
                moved = r * cos + pltpu.roll(r, channels // 2, 0) * (turn_sign * sin)
                for p in range(parents):
                    sums[p] = sums[p] + moved * own_ref[f, p : p + 1, :]
            for p in range(0, parents, 2):
                tile = slice(p // 2 * channels, (p // 2 + 1) * channels)
                one, two = sums[p], sums[p + 1]
                p_ref[b, bb, 2 * h, tile, :] = jnp.where(outer, one, pltpu.roll(two, 2, 0))
                p_ref[b, bb, 2 * h + 1, tile, :] = jnp.where(
                    outer, pltpu.roll(one, channels - 2, 0), two
                )
            return 0

        lax.fori_loop(0, boxes, one_row, 0)

    def band_at(k):
        middle = n - 1 - k // 2 if k % 2 == 0 else k // 2
        return jnp.where(z == 0, n - 1 - k, jnp.where(z == n - 1, k, middle))

    def by_part(x):
        later = (sublane >= 4) & (sublane < 6)
        earlier = (sublane >= 2) & (sublane < 4)
        return jnp.where(
            later, pltpu.roll(x, 2, 0), jnp.where(earlier, pltpu.roll(x, channels - 2, 0), x)
        )

    def lower_piece(b, h):
        def two_rows(i, _):
            fields = [
                [
                    by_part(f_ref[b, 2 * i + r, h, pl.ds(p, channels, stride=parents), :])
                    for p in range(parents)
                ]
                for r in range(2)
            ]
            first = (b * boxes + 2 * i) * rows_here + h
            for f in range(fine):
                both = []
                for r in range(2):
                    u = first + r * rows_here
                    mine = fields[r][0] * own_ref[f, 0:1, :]
                    for p in range(1, parents):
                        mine = mine + fields[r][p] * own_ref[f, p : p + 1, :]
                    cos = turn_ref[f, 0, pl.ds(u, 1), :]
                    sin = turn_ref[f, 1, pl.ds(u, 1), :]
                    both.append(
                        mine * cos - pltpu.roll(mine, channels // 2, 0) * (turn_sign * sin)
                    )
                child = jnp.concatenate(both, axis=0)
                high = child.astype(jnp.bfloat16)
                low = (child - high.astype(jnp.float32)).astype(jnp.bfloat16)
                row = pl.multiple_of(i * 2 * channels, 2 * channels)
                lanes = slice(f * width, (f + 1) * width)
                child_ref[0, pl.ds(row, 2 * channels), lanes] = high
                child_ref[1, pl.ds(row, 2 * channels), lanes] = low
            return 0

        lax.fori_loop(0, boxes // 2, two_rows, 0)
        tile = 4 * width

        def add_tile(i, _):
            lanes = pl.ds(pl.multiple_of(i * tile, tile), tile)
            high = child_ref[0, :, lanes]
            low = child_ref[1, :, lanes]
            low_ref[:, lanes] += dot(
                down_theta_ref[b * rows_here + h], jnp.concatenate([high, low, high], axis=0)
            )
            return 0

        lax.fori_loop(0, fine * width // tile, add_tile, 0)

    def lower_step(h, step):
        if step == 0:
            lower_piece(z, h)
            return

        def one_side(i, _):
            b = jnp.where(i == 0, z - step, z + step)

            @pl.when((b >= 0) & (b < n))
            def _():
                lower_piece(b, h)

            return 0

        lax.fori_loop(0, 2, one_side, 0)

    def lower_last(f, _):
        part = low_ref[:, pl.ds(pl.multiple_of(f * width, width), width)]
        half = part.shape[0] // 2
        y = jnp.concatenate([part[:half], part[half:]], axis=1)
        x = dot(split3(y, 1), down_phi_ref[...])
        out_ref[f] = jnp.concatenate(
            [x[j * channels : (j + 1) * channels] for j in range(TF // 2)], axis=1
        )
        return 0

    def remote(src, dst, send, recv, to_box, to_dir):
        return pltpu.make_async_remote_copy(
            src_ref=src, dst_ref=dst, send_sem=send, recv_sem=recv,
            device_id=(to_box, to_dir), device_id_type=MESH,
        )

    def up_copy(h, b, src):
        return remote(src, up_ref.at[h, b], up_send.at[h, b], up_recv.at[h, b], box, z + 1)

    def down_copy(h, b, src):
        return remote(src, down_ref.at[h, b], down_send.at[h, b], down_recv.at[h, b], box, z - 1)

    chunks = n - 1
    flight = 3

    def sum_send(g):
        if g >= pieces * chunks:
            return
        h, j = divmod(g, chunks)

        @pl.when(z == 0)
        def _():
            if g >= flight:
                h2, j2 = divmod(g - flight, chunks)
                up_copy(h2, n - 1 - j2, p_ref.at[n - 1 - j2, :, h2]).wait_send()
            up_copy(h, n - 1 - j, p_ref.at[n - 1 - j, :, h]).start()

        @pl.when(z == n - 1)
        def _():
            if g >= flight:
                h2, j2 = divmod(g - flight, chunks)
                down_copy(h2, j2, p_ref.at[j2, :, h2]).wait_send()
            down_copy(h, j, p_ref.at[j, :, h]).start()

    def sum_tick(tick):
        h = (tick - 1) // chunks
        j = tick - h * chunks
        up_b = n - 1 - j + z
        down_b = j - (n - 1 - z)

        @pl.when((z > 0) & (z < up_b) & (up_b < n))
        def _():
            copy = up_copy(h, up_b, up_ref.at[h, up_b])
            copy.wait_recv()
            up_ref[h, up_b] += p_ref[up_b, :, h]
            copy.start()

        @pl.when((z < n - 1) & (z > down_b) & (down_b >= 0))
        def _():
            copy = down_copy(h, down_b, down_ref.at[h, down_b])
            copy.wait_recv()
            down_ref[h, down_b] += p_ref[down_b, :, h]
            copy.start()

        sum_send(tick + flight - 1)

    def sum_finish(h):
        band_ref[h] = p_ref[z, :, h]

        @pl.when(z > 0)
        def _():
            up_copy(h, z, up_ref.at[h, z]).wait_recv()
            band_ref[h] += up_ref[h, z]

        @pl.when(z < n - 1)
        def _():
            down_copy(h, z, down_ref.at[h, z]).wait_recv()
            band_ref[h] += down_ref[h, z]

    def sum_drain(h):
        for b in range(n):
            @pl.when((z < b) & (z > 0))
            def _():
                up_copy(h, b, up_ref.at[h, b]).wait_send()

            @pl.when((z > b) & (z < n - 1))
            def _():
                down_copy(h, b, down_ref.at[h, b]).wait_send()

        for j in range(chunks):
            if h * chunks + j >= pieces * chunks - flight:
                @pl.when(z == 0)
                def _():
                    up_copy(h, n - 1 - j, p_ref.at[n - 1 - j, :, h]).wait_send()

                @pl.when(z == n - 1)
                def _():
                    down_copy(h, j, p_ref.at[j, :, h]).wait_send()

    def peer(k):
        return lax.rem(box + k, boxes)

    def go_copy(h, k):
        return remote(
            band_ref.at[h, peer(k)], src_ref.at[h, box], go_send.at[h, k], go_recv.at[h, k], peer(k), z
        )

    def back_copy(h, k):
        return remote(
            res_ref.at[h, peer(k)],
            f_ref.at[z, box, h // 2, pl.ds(h % 2 * block, block)],
            back_send.at[h, k], back_recv.at[h, k], peer(k), z,
        )

    def go_start(h):
        for k in range(1, boxes):
            go_copy(h, k).start()
        src_ref[h, box] = band_ref[h, box]

    def go_wait(h):
        for k in range(1, boxes):
            go_copy(h, k).wait_recv()

    def back_start(h):
        for k in range(1, boxes):
            back_copy(h, k).start()
        f_ref[z, box, h // 2, pl.ds(h % 2 * block, block), :] = res_ref[h, box]

    def back_wait(h):
        for k in range(1, boxes):
            back_copy(h, k).wait_recv()

    def rise_copy(h, b):
        piece = f_ref.at[b, :, h // 2, pl.ds(h % 2 * block, block)]
        return remote(piece, piece, rise_send.at[h, b], rise_recv.at[h, b], box, z + 1)

    def sink_copy(h, b):
        piece = f_ref.at[b, :, h // 2, pl.ds(h % 2 * block, block)]
        return remote(piece, piece, sink_send.at[h, b], sink_recv.at[h, b], box, z - 1)

    def share_step(h, step):
        @pl.when(z >= step)
        def _():
            if step:
                rise_copy(h, z - step).wait_recv()

            @pl.when(z < n - 1)
            def _():
                rise_copy(h, z - step).start()

        @pl.when(z + step <= n - 1)
        def _():
            if step:
                sink_copy(h, z + step).wait_recv()

            @pl.when(z > 0)
            def _():
                sink_copy(h, z + step).start()

    def share_drain(h):
        for b in range(n):
            @pl.when((z >= b) & (z < n - 1))
            def _():
                rise_copy(h, b).wait_send()

            @pl.when((z <= b) & (z > 0))
            def _():
                sink_copy(h, b).wait_send()

    source_ids = lax.broadcasted_iota(jnp.int32, (sources, length), 0)
    kind_ids = lax.broadcasted_iota(jnp.int32, (blocks * 128, length), 0)

    def count_pairs(p, _):
        partner = partner_ref[pl.ds(p, 1), :]
        slots = lax.broadcasted_iota(jnp.int32, (1, length), 1)
        partner = jnp.where(slots < count_ref[p], partner, -1)
        kind = kind_ref[pl.ds(p, 1), :]
        a = jnp.where(source_ids == partner, 1.0, 0.0).astype(jnp.bfloat16)
        b = jnp.where(kind_ids == kind, 1.0, 0.0).astype(jnp.bfloat16)
        counts = lax.dot_general(
            a, b, (((1,), (1,)), ((), ())), preferred_element_type=jnp.float32
        )
        for j in range(blocks):
            sel_ref[j, pl.ds(p, sources, stride=targets), :] = counts[:, j * 128 : (j + 1) * 128]
        return 0

    def count_part(part, parts):
        first, last = targets * part // parts, targets * (part + 1) // parts
        lax.fori_loop(first, last, count_pairs, 0, unroll=4)

    def operator_part(h, part, parts):
        rows = jnp.concatenate(
            [rows_ref[:, i * width : (i + 1) * width] for i in (h, rows_here + h)], axis=1
        )
        pad = blocks * 128 - rows.shape[0]
        if pad:
            rows = jnp.concatenate([rows, jnp.zeros((pad, 2 * width), jnp.float32)], axis=0)
        high = rows.astype(jnp.bfloat16)
        low = (rows - high.astype(jnp.float32)).astype(jnp.bfloat16)
        both = jnp.concatenate([high, low], axis=0)
        tile = 512

        def one_tile(i, _):
            start = pl.multiple_of(i * tile, tile)
            chosen = jnp.concatenate(
                [sel_ref[j, pl.ds(start, tile), :] for j in range(blocks)], axis=1
            ).astype(jnp.bfloat16)
            op_ref[h, pl.ds(start, tile), :] = dot(
                jnp.concatenate([chosen, chosen], axis=1), both
            )
            return 0

        tiles = pair_rows // tile
        lax.fori_loop(tiles * part // parts, tiles * (part + 1) // parts, one_tile, 0)

    def apply_piece(h):
        group = 4
        pairs = parents // 2

        def add_sources(i, sums, first):
            tile = i % pairs * channels
            for two in range(2):
                real_rows = [tile + two * 2 + j for j in range(2)]
                reals = [src_ref[h, i // pairs, pl.ds(r, 1), :] for r in real_rows]
                imags = [src_ref[h, i // pairs, pl.ds(r + 4, 1), :] for r in real_rows]
                out = []
                for g in range(group):
                    row = pl.multiple_of((2 * i + two) * targets + first + g * 8, 8)
                    real = op_ref[h // 2, pl.ds(row, 8), 0:width]
                    imag = op_ref[h // 2, pl.ds(row, 8), width : 2 * width]
                    mine = sums[g * 4 : (g + 1) * 4]
                    for j in range(2):
                        out.append(mine[j] + real * reals[j] - imag * imags[j])
                    for j in range(2):
                        out.append(mine[2 + j] + real * imags[j] + imag * reals[j])
                sums = tuple(out)
            return sums

        for first in range(0, targets, group * 8):
            sums = tuple(jnp.zeros((8, width), jnp.float32) for _ in range(group * 4))
            sums = lax.fori_loop(
                0, sources // 2, functools.partial(add_sources, first=first), sums, unroll=2
            )
            for g in range(group):
                for c in range(4):
                    res_ref[h, first // 8 + g, c * 8 : (c + 1) * 8, :] = sums[g * 4 + c]

    barrier = pltpu.get_barrier_semaphore()
    for k in range(1, boxes):
        pl.semaphore_signal(barrier, inc=1, device_id=(peer(k), z), device_id_type=MESH)

    @pl.when(z > 0)
    def _():
        pl.semaphore_signal(barrier, inc=1, device_id=(box, z - 1), device_id_type=MESH)

    @pl.when(z < n - 1)
    def _():
        pl.semaphore_signal(barrier, inc=1, device_id=(box, z + 1), device_id_type=MESH)

    ends = jnp.where(z > 0, 1, 0) + jnp.where(z < n - 1, 1, 0)
    lax.fori_loop(0, fine, turn_one, 0)
    lax.fori_loop(0, fine // 2, raise_pair, 0, unroll=2)
    low_ref[...] = jnp.zeros_like(low_ref)
    make_piece(band_at(0), 0)
    pl.semaphore_wait(barrier, boxes - 1 + ends)
    sum_send(0)
    for i in range(1, n):
        make_piece(band_at(i), 0)
        if i < flight:
            sum_send(i)

    shared = [0] * pieces
    lowered = [0] * rows_here

    def share_to(h, last_step):
        while h < pieces and shared[h] <= min(last_step, n - 1):
            share_step(h, shared[h])
            shared[h] += 1

    def lower_to(row, last_step):
        while lowered[row] <= min(last_step, n - 1):
            lower_step(row, lowered[row])
            lowered[row] += 1

    def apply_next(h):
        go_wait(h)
        apply_piece(h)
        back_start(h)

    for h in range(pieces):
        for step in range(1, chunks + 1):
            if h == 0:
                count_part(step - 1, chunks)
            elif h == 1 and step == 1:
                for row in range(1, rows_here):
                    for i in range(n):
                        make_piece(band_at(i), row)
            elif h == 1 and step == 2:
                operator_part(0, 0, 1)
            elif h == 1 and step == chunks:
                apply_next(0)
            elif h >= 2 and step == 1:
                if h % 2 == 0:
                    operator_part(h // 2, 0, 2)
                else:
                    share_to(h - 3, 2)
                    apply_next(h - 1)
                    share_to(h - 2, 1)
            elif h >= 2 and step == 2:
                if h % 2 == 0:
                    apply_next(h - 1)
                    back_wait(h - 2)
                    share_to(h - 2, 0)
                else:
                    share_to(h - 3, n - 1)
                    back_wait(h - 1)
                    share_to(h - 1, 0)
            elif h >= 2 and step == chunks:
                if h % 2 == 0:
                    operator_part(h // 2, 1, 2)
                    back_wait(h - 1)
                    share_to(h - 1, 0)
                    share_to(h - 2, 1)
                else:
                    share_to(h - 2, 2)
                    lower_to(h // 2 - 1, 0)
            sum_tick(h * chunks + step)
        sum_finish(h)
        go_start(h)
    last = pieces - 1
    share_to(last - 1, 1)
    apply_next(last)
    for h in range(last - 1):
        share_to(h, n - 1)
    share_to(last - 1, 2)
    back_wait(last)
    share_to(last, 0)
    for row in range(rows_here - 1):
        lower_to(row, 1)
    share_to(last - 1, n - 1)
    share_to(last, 1)
    for row in range(rows_here - 1):
        lower_to(row, 2)
    lower_to(rows_here - 1, 0)
    share_to(last, 2)
    for row in range(rows_here - 1):
        lower_to(row, n - 1)
    lower_to(rows_here - 1, 1)
    for step in range(2, n):
        share_to(last, step)
        lower_to(rows_here - 1, step)
    lax.fori_loop(0, fine, lower_last, 0, unroll=4)
    for h in range(pieces):
        sum_drain(h)
        share_drain(h)
        for k in range(1, boxes):
            go_copy(h, k).wait_send()
            back_copy(h, k).wait_send()


def exchange(outgoing, slots, partner, kind, count, rows, n, boxes):
    fine, channels, fine_width = outgoing.shape
    parents = slots.shape[0] // 8
    targets = partner.shape[0]
    halves = TP // n // boxes
    pieces = 2 * halves
    block = parents * channels // 2
    kinds = rows.shape[0]
    kind_blocks = -(-kinds // 128)
    shape = (n, boxes, pieces, block, PP)
    vmem = pl.BlockSpec(memory_space=pltpu.VMEM)
    smem = pl.BlockSpec(memory_space=pltpu.SMEM)
    dma = pltpu.SemaphoreType.DMA
    consts = [jnp.asarray(t) for t in tables(channels, n, boxes, halves)]
    f32 = jnp.float32
    return pl.pallas_call(
        functools.partial(exchange_kernel, targets=targets, channels=channels),
        out_shape=jax.ShapeDtypeStruct(outgoing.shape, f32),
        in_specs=[vmem, smem] + [vmem] * 7 + [smem, vmem],
        out_specs=vmem,
        scratch_shapes=[
            pltpu.VMEM((fine, TP * channels, PP), f32),
            pltpu.VMEM((fine, 2, TP, PP), f32),
            pltpu.VMEM((fine, parents, PP), f32),
            pltpu.VMEM(shape, f32),
            pltpu.VMEM((n, boxes, halves, 2 * block, PP), f32),
            pltpu.VMEM((2, boxes * channels, fine * PP), jnp.bfloat16),
            pltpu.VMEM((TF * channels, fine * PP), f32),
            pltpu.VMEM((kind_blocks, targets * targets, 128), f32),
            pltpu.VMEM((halves, targets * targets, 2 * PP), f32),
            pltpu.VMEM((pieces, n, boxes, block, PP), f32),
            pltpu.VMEM((pieces, n, boxes, block, PP), f32),
            pltpu.VMEM((pieces, boxes, block, PP), f32),
            pltpu.VMEM((pieces, boxes, block, PP), f32),
            pltpu.VMEM((pieces, boxes, block, PP), f32),
        ]
        + [dma((pieces, n))] * 4
        + [dma((pieces, boxes))] * 4
        + [dma((pieces, n))] * 4,
        compiler_params=pltpu.CompilerParams(
            vmem_limit_bytes=56 * 2**20, collective_id=0, has_side_effects=True
        ),
        name="exchange",
    )(
        outgoing, slots, *consts, jnp.asarray(np_phase()), partner, kind, count, rows
    )


def body(outgoing, fine_slot, translator, list_partner, list_kind, list_count):
    dir_count = lax.axis_size("dir")
    box_count = lax.axis_size("box")
    fine_here, channels, _ = outgoing.shape
    whole_rows = TP // dir_count % box_count == 0 and dir_count >= 4 and box_count % 2 == 0
    if not whole_rows or fine_here % 4 or channels != 8 or fine_slot.shape[0] != 64 or list_partner.shape[0] % 32:
        return general_body(
            outgoing, fine_slot, translator, list_partner, list_kind, list_count
        )
    box_index = lax.axis_index("box")
    kinds, _, dirs_here = translator.shape
    split_here = dirs_here // box_count
    rows = lax.dynamic_slice_in_dim(translator, box_index * split_here, split_here, 2)
    rows = rows.reshape(kinds, 2 * split_here)
    return exchange(
        outgoing, fine_slot, list_partner, list_kind, list_count, rows, dir_count, box_count
    )


def solution(mesh):
    placed = (P(("box", "dir"), None, None), P("box"), P(None, None, "dir"), P(), P(), P())
    return jax.shard_map(
        body, mesh=mesh, in_specs=placed, out_specs=P(("box", "dir"), None, None), check_vma=False
    )
```

```python
import functools

import jax
import jax.numpy as jnp
import ml_dtypes
import numpy as np
from jax import lax
from jax.experimental import pallas as pl
from jax.experimental.pallas import tpu as pltpu
from jax.sharding import PartitionSpec as P

TF = 32
PF = 64
TP = 64
PP = 128


wave_shift = 5.0
highest = lax.Precision.HIGHEST


def theta_table(fine_count, coarse_count):
    fine_angle = (jnp.arange(fine_count, dtype=jnp.float32) + 0.5) * (jnp.pi / fine_count)
    coarse_angle = (jnp.arange(coarse_count, dtype=jnp.float32) + 0.5) * (jnp.pi / coarse_count)
    orders = jnp.arange(1, fine_count, dtype=jnp.float32)
    products = jnp.cos(coarse_angle[:, None, None] * orders) * jnp.cos(
        fine_angle[None, :, None] * orders
    )
    return (1.0 + 2.0 * jnp.sum(products, axis=2)) / fine_count


def phi_table(fine_count, coarse_count):
    fine_angle = jnp.arange(fine_count, dtype=jnp.float32) * (2.0 * jnp.pi / fine_count)
    coarse_angle = jnp.arange(coarse_count, dtype=jnp.float32) * (2.0 * jnp.pi / coarse_count)
    offset = coarse_angle[:, None] - fine_angle[None, :]
    orders = jnp.arange(1, fine_count // 2, dtype=jnp.float32)
    series = jnp.sum(jnp.cos(offset[:, :, None] * orders), axis=2)
    return (1.0 + 2.0 * series + jnp.cos(offset * (fine_count // 2))) / fine_count


def octant_phase(octant, first_theta, theta_count, coarse_theta, coarse_phi):
    theta_index = first_theta + jnp.arange(theta_count, dtype=jnp.int32)
    polar = (theta_index.astype(jnp.float32) + 0.5) * (jnp.pi / coarse_theta)
    azimuth = jnp.arange(coarse_phi, dtype=jnp.float32) * (2.0 * jnp.pi / coarse_phi)
    along_x = jnp.sin(polar)[:, None] * jnp.cos(azimuth)[None, :]
    along_y = jnp.sin(polar)[:, None] * jnp.sin(azimuth)[None, :]
    along_z = jnp.cos(polar)[:, None] + 0.0 * azimuth[None, :]
    sign_x = (2 * (octant % 2) - 1).astype(jnp.float32)
    sign_y = (2 * (octant // 2 % 2) - 1).astype(jnp.float32)
    sign_z = (2 * (octant // 4) - 1).astype(jnp.float32)
    phase_angle = wave_shift * (
        sign_x[:, None, None] * along_x[None]
        + sign_y[:, None, None] * along_y[None]
        + sign_z[:, None, None] * along_z[None]
    )
    return (jnp.cos(phase_angle), jnp.sin(phase_angle))


def translate(sources, kernel_table, partner, kind, count):
    targets, length = partner.shape
    source_rows, _, excite, lanes = sources.shape
    kinds = kernel_table.shape[0]
    blocks = 7
    block_width = length // blocks
    flat_sources = sources.reshape(source_rows, 2 * excite * lanes)
    flat_kernel = kernel_table.reshape(kinds, 2 * lanes)
    source_ids = jnp.arange(source_rows, dtype=jnp.int32)
    kind_ids = jnp.arange(kinds, dtype=jnp.int32)

    def add_block(block_step, running):
        begin_at = block_step * block_width
        near_rows = lax.dynamic_slice_in_dim(partner, begin_at, block_width, 1)
        kind_rows = lax.dynamic_slice_in_dim(kind, begin_at, block_width, 1)
        position = begin_at + jnp.arange(block_width, dtype=jnp.int32)
        alive_mask = (position[None, :] < count[:, None]).astype(jnp.float32)
        select_source = (
            (near_rows[:, :, None] == source_ids)
            .astype(jnp.float32)
            .reshape(targets * block_width, source_rows)
        )
        select_kind = (
            (kind_rows[:, :, None] == kind_ids).astype(jnp.float32) * alive_mask[:, :, None]
        ).reshape(targets * block_width, kinds)
        picked = jnp.dot(
            select_source, flat_sources, precision=highest, preferred_element_type=jnp.float32
        )
        picked = picked.reshape(targets, block_width, 2, excite, lanes)
        factor = jnp.dot(
            select_kind, flat_kernel, precision=highest, preferred_element_type=jnp.float32
        )
        factor = factor.reshape(targets, block_width, 2, 1, lanes)
        along_real = factor[:, :, 0]
        along_imag = factor[:, :, 1]
        real_part = picked[:, :, 0]
        imag_part = picked[:, :, 1]
        new_real = jnp.sum(along_real * real_part - along_imag * imag_part, axis=1)
        new_imag = jnp.sum(along_real * imag_part + along_imag * real_part, axis=1)
        return running + jnp.stack([new_real, new_imag], axis=1)

    initial = jnp.zeros((targets, 2, excite, lanes), jnp.float32)
    return lax.fori_loop(0, blocks, add_block, initial)


def general_body(outgoing, fine_slot, translator, list_partner, list_kind, list_count):
    dir_count = lax.axis_size("dir")
    box_count = lax.axis_size("box")
    box_index = lax.axis_index("box")
    dir_index = lax.axis_index("dir")
    channels = outgoing.shape[1]
    excite = channels // 2
    fine_here = outgoing.shape[0]
    row_boxes = fine_slot.shape[0]
    parents_here = row_boxes // 8
    theta_here = TP // dir_count
    dirs_here = translator.shape[2]
    up_theta = theta_table(TF, TP)
    up_phi = phi_table(PF, PP)
    octant = fine_slot % 8
    local_parent = fine_slot // 8 % parents_here
    onehot = (local_parent[None, :] == jnp.arange(parents_here, dtype=jnp.int32)[:, None]).astype(
        jnp.float32
    )
    cos_table, sin_table = octant_phase(octant, dir_index * theta_here, theta_here, TP, PP)
    cos_table = cos_table[:, :, None, :]
    sin_table = sin_table[:, :, None, :]
    pattern = outgoing.reshape(fine_here, channels, TF, PF)
    raised = jnp.einsum("ut,fctp->fcup", up_theta, pattern, precision=highest)
    raised = jnp.einsum("qp,fcup->fucq", up_phi, raised, precision=highest)
    spread = lax.all_to_all(raised, "dir", split_axis=1, concat_axis=0, tiled=True)
    real_part = spread[:, :, :excite]
    imag_part = spread[:, :, excite:]
    shifted = jnp.concatenate(
        [
            real_part * cos_table + imag_part * sin_table,
            imag_part * cos_table - real_part * sin_table,
        ],
        axis=2,
    )
    parent_out = jnp.einsum("pf,fucq->pcuq", onehot, shifted, precision=highest)
    parent_out = parent_out.reshape(parents_here, channels, dirs_here)
    split_here = dirs_here // box_count
    sectioned = jnp.swapaxes(
        parent_out.reshape(parents_here, channels, box_count, split_here), 1, 2
    )
    sectioned = sectioned.reshape(parents_here, box_count, channels * split_here)
    gathered = lax.all_to_all(sectioned, "box", split_axis=1, concat_axis=0, tiled=True)
    sources = gathered.reshape(box_count * parents_here, 2, excite, split_here)
    kernel_rows = lax.dynamic_slice_in_dim(translator, box_index * split_here, split_here, 2)
    translated = translate(sources, kernel_rows, list_partner, list_kind, list_count)
    translated = translated.reshape(box_count * parents_here, 1, channels * split_here)
    returned = lax.all_to_all(translated, "box", split_axis=0, concat_axis=1, tiled=True)
    incoming = jnp.swapaxes(returned.reshape(parents_here, box_count, channels, split_here), 1, 2)
    incoming = incoming.reshape(parents_here, channels, dirs_here)
    fields = incoming.reshape(parents_here, channels, theta_here, PP)
    spread_back = jnp.einsum("pf,pcuq->fucq", onehot, fields, precision=highest)
    real_part = spread_back[:, :, :excite]
    imag_part = spread_back[:, :, excite:]
    shifted_back = jnp.concatenate(
        [
            real_part * cos_table - imag_part * sin_table,
            imag_part * cos_table + real_part * sin_table,
        ],
        axis=2,
    )
    arrived_back = lax.all_to_all(shifted_back, "dir", split_axis=0, concat_axis=1, tiled=True)
    arrived_back = jnp.einsum("qp,fucq->fucp", up_phi, arrived_back, precision=highest) * (PF / PP)
    result = jnp.einsum("ut,fucp->fctp", up_theta, arrived_back, precision=highest) * (TF / TP)
    return result.reshape(fine_here, channels, TF * PF)


def np_theta(fine_count, coarse_count):
    fine_angle = (np.arange(fine_count) + 0.5) * (np.pi / fine_count)
    coarse_angle = (np.arange(coarse_count) + 0.5) * (np.pi / coarse_count)
    orders = np.arange(1, fine_count)
    products = np.cos(coarse_angle[:, None, None] * orders) * np.cos(
        fine_angle[None, :, None] * orders
    )
    return (1.0 + 2.0 * products.sum(2)) / fine_count


def np_phi(fine_count, coarse_count):
    fine_angle = np.arange(fine_count) * (2.0 * np.pi / fine_count)
    coarse_angle = np.arange(coarse_count) * (2.0 * np.pi / coarse_count)
    offset = coarse_angle[:, None] - fine_angle[None, :]
    orders = np.arange(1, fine_count // 2)
    series = np.cos(offset[:, :, None] * orders).sum(2)
    return (1.0 + 2.0 * series + np.cos(offset * (fine_count // 2))) / fine_count


def np_phase():
    polar = (np.arange(TP) + 0.5) * (np.pi / TP)
    azimuth = np.arange(PP) * (2.0 * np.pi / PP)
    along = [
        np.sin(polar)[:, None] * np.cos(azimuth)[None, :],
        np.sin(polar)[:, None] * np.sin(azimuth)[None, :],
        np.cos(polar)[:, None] + 0.0 * azimuth[None, :],
    ]
    cx, cy, cz = (np.cos(wave_shift * a) for a in along)
    sx, sy, sz = (np.sin(wave_shift * a) for a in along)
    terms = [
        cx * cy * cz, sx * sy * cz, sx * cy * sz, cx * sy * sz,
        sx * cy * cz, cx * sy * cz, cx * cy * sz, sx * sy * sz,
    ]
    return np.stack(terms).astype(np.float32)


def np_split(values):
    high = values.astype(ml_dtypes.bfloat16)
    low = (values - high.astype(np.float64)).astype(ml_dtypes.bfloat16)
    return high, low


def tables(channels, n, boxes, halves):
    theta = np_theta(TF, TP)
    phi = np_phi(PF, PP)
    eye = np.eye(channels)
    order = np.concatenate([np.arange(0, TF, 2), np.arange(1, TF, 2)])
    theta = theta[:, order]
    up_phi = np.kron(np.eye(2), phi.T)
    up_theta = np.kron(theta, eye)
    down_phi = np.kron(np.eye(2), phi) * (PF / PP)
    uph, upl = np_split(up_phi)
    uth, utl = np_split(up_theta)
    dph, dpl = np_split(down_phi)
    blocks = theta.reshape(n, boxes, halves, TF).transpose(0, 2, 3, 1) * (TF / TP)
    down = []
    for block in blocks.reshape(n * halves, TF, boxes):
        high, low = np_split(np.kron(block, eye))
        down.append(np.concatenate([high, high, low], axis=1))
    return (
        np.concatenate([uph, uph, upl], axis=0),
        np.concatenate([uth, uth, utl], axis=1),
        np.stack(down),
        np.concatenate([dph, dph, dpl], axis=0),
    )


def split3(values, axis):
    high = values.astype(jnp.bfloat16)
    low = (values - high.astype(jnp.float32)).astype(jnp.bfloat16)
    return jnp.concatenate([high, low, high], axis=axis)


def dot(a, b):
    return jnp.dot(a, b, preferred_element_type=jnp.float32)


MESH = pl.DeviceIdType.MESH


def exchange_kernel(
    x_ref, slot_ref, up_phi_ref, up_theta_ref, down_theta_ref, down_phi_ref, phase_ref,
    partner_ref, kind_ref, count_ref, rows_ref, out_ref,
    r_ref, turn_ref, own_ref, p_ref, f_ref, child_ref, low_ref,
    sel_ref, op_ref, up_ref, down_ref, band_ref, src_ref, res_ref,
    up_send, up_recv, down_send, down_recv, go_send, go_recv, back_send, back_recv,
    rise_send, rise_recv, sink_send, sink_recv,
    *, targets, channels,
):
    n, boxes, pieces, block, width = p_ref.shape
    rows_here = pieces // 2
    box = lax.axis_index("box")
    z = lax.axis_index("dir")
    sources = targets
    blocks = sel_ref.shape[0]
    length = partner_ref.shape[1]
    pair_rows = sources * targets
    fine = x_ref.shape[0]
    parents = 2 * block // channels
    turn_sign = jnp.where(
        lax.broadcasted_iota(jnp.int32, (channels, width), 0) < channels // 2, 1.0, -1.0
    )

    sublane = lax.broadcasted_iota(jnp.int32, (channels, width), 0)
    outer = sublane % 4 < 2

    def raise_pair(i, _):
        stacked = []
        for f in range(2):
            x = x_ref[2 * i + f]
            x = jnp.concatenate(
                [x[:, j * 2 * PF : (j + 1) * 2 * PF] for j in range(TF // 2)], axis=0
            )
            y = dot(split3(x, 1), up_phi_ref[...])
            stacked.append(jnp.concatenate([y[:, :PP], y[:, PP:]], axis=0))
        z3 = split3(jnp.concatenate(stacked, axis=1), 0)
        raised = dot(up_theta_ref[...], z3)
        r_ref[2 * i] = raised[:, :PP]
        r_ref[2 * i + 1] = raised[:, PP:]
        return 0

    def turn_one(f, _):
        slot = slot_ref[z * fine + f]
        octant = slot % 8
        parent = slot // 8 % parents
        x = (2 * (octant % 2) - 1).astype(jnp.float32)
        y = (2 * (octant // 2 % 2) - 1).astype(jnp.float32)
        w = (2 * (octant // 4) - 1).astype(jnp.float32)
        t = [phase_ref[i] for i in range(8)]
        turn_ref[f, 0] = t[0] - (x * y) * t[1] - (x * w) * t[2] - (y * w) * t[3]
        turn_ref[f, 1] = x * t[4] + y * t[5] + w * t[6] - (x * y * w) * t[7]
        rows = lax.broadcasted_iota(jnp.int32, (parents, width), 0)
        own_ref[f] = jnp.where(rows == parent, 1.0, 0.0)
        return 0

    def make_piece(b, h):
        def one_row(bb, _):
            u = (b * boxes + bb) * rows_here + h
            sums = [jnp.zeros((channels, width), jnp.float32) for _ in range(parents)]
            for f in range(fine):
                r = r_ref[f, pl.ds(pl.multiple_of(u * channels, channels), channels), :]
                cos = turn_ref[f, 0, pl.ds(u, 1), :]
                sin = turn_ref[f, 1, pl.ds(u, 1), :]
                moved = r * cos + pltpu.roll(r, channels // 2, 0) * (turn_sign * sin)
                for p in range(parents):
                    sums[p] = sums[p] + moved * own_ref[f, p : p + 1, :]
            for p in range(0, parents, 2):
                tile = slice(p // 2 * channels, (p // 2 + 1) * channels)
                one, two = sums[p], sums[p + 1]
                p_ref[b, bb, 2 * h, tile, :] = jnp.where(outer, one, pltpu.roll(two, 2, 0))
                p_ref[b, bb, 2 * h + 1, tile, :] = jnp.where(
                    outer, pltpu.roll(one, channels - 2, 0), two
                )
            return 0

        lax.fori_loop(0, boxes, one_row, 0)

    def band_at(k):
        middle = n - 1 - k // 2 if k % 2 == 0 else k // 2
        return jnp.where(z == 0, n - 1 - k, jnp.where(z == n - 1, k, middle))

    def by_part(x):
        later = (sublane >= 4) & (sublane < 6)
        earlier = (sublane >= 2) & (sublane < 4)
        return jnp.where(
            later, pltpu.roll(x, 2, 0), jnp.where(earlier, pltpu.roll(x, channels - 2, 0), x)
        )

    def lower_piece(b, h):
        def two_rows(i, _):
            fields = [
                [
                    by_part(f_ref[b, 2 * i + r, h, pl.ds(p, channels, stride=parents), :])
                    for p in range(parents)
                ]
                for r in range(2)
            ]
            first = (b * boxes + 2 * i) * rows_here + h
            for f in range(fine):
                both = []
                for r in range(2):
                    u = first + r * rows_here
                    mine = fields[r][0] * own_ref[f, 0:1, :]
                    for p in range(1, parents):
                        mine = mine + fields[r][p] * own_ref[f, p : p + 1, :]
                    cos = turn_ref[f, 0, pl.ds(u, 1), :]
                    sin = turn_ref[f, 1, pl.ds(u, 1), :]
                    both.append(
                        mine * cos - pltpu.roll(mine, channels // 2, 0) * (turn_sign * sin)
                    )
                child = jnp.concatenate(both, axis=0)
                high = child.astype(jnp.bfloat16)
                low = (child - high.astype(jnp.float32)).astype(jnp.bfloat16)
                row = pl.multiple_of(i * 2 * channels, 2 * channels)
                lanes = slice(f * width, (f + 1) * width)
                child_ref[0, pl.ds(row, 2 * channels), lanes] = high
                child_ref[1, pl.ds(row, 2 * channels), lanes] = low
            return 0

        lax.fori_loop(0, boxes // 2, two_rows, 0)
        tile = 4 * width

        def add_tile(i, _):
            lanes = pl.ds(pl.multiple_of(i * tile, tile), tile)
            high = child_ref[0, :, lanes]
            low = child_ref[1, :, lanes]
            low_ref[:, lanes] += dot(
                down_theta_ref[b * rows_here + h], jnp.concatenate([high, low, high], axis=0)
            )
            return 0

        lax.fori_loop(0, fine * width // tile, add_tile, 0)

    def lower_step(h, step):
        if step == 0:
            lower_piece(z, h)
            return

        def one_side(i, _):
            b = jnp.where(i == 0, z - step, z + step)

            @pl.when((b >= 0) & (b < n))
            def _():
                lower_piece(b, h)

            return 0

        lax.fori_loop(0, 2, one_side, 0)

    def lower_last(f, _):
        part = low_ref[:, pl.ds(pl.multiple_of(f * width, width), width)]
        half = part.shape[0] // 2
        y = jnp.concatenate([part[:half], part[half:]], axis=1)
        x = dot(split3(y, 1), down_phi_ref[...])
        out_ref[f] = jnp.concatenate(
            [x[j * channels : (j + 1) * channels] for j in range(TF // 2)], axis=1
        )
        return 0

    def remote(src, dst, send, recv, to_box, to_dir):
        return pltpu.make_async_remote_copy(
            src_ref=src, dst_ref=dst, send_sem=send, recv_sem=recv,
            device_id=(to_box, to_dir), device_id_type=MESH,
        )

    def up_copy(h, b, src):
        return remote(src, up_ref.at[h, b], up_send.at[h, b], up_recv.at[h, b], box, z + 1)

    def down_copy(h, b, src):
        return remote(src, down_ref.at[h, b], down_send.at[h, b], down_recv.at[h, b], box, z - 1)

    chunks = n - 1
    flight = 3

    def sum_send(g):
        if g >= pieces * chunks:
            return
        h, j = divmod(g, chunks)

        @pl.when(z == 0)
        def _():
            if g >= flight:
                h2, j2 = divmod(g - flight, chunks)
                up_copy(h2, n - 1 - j2, p_ref.at[n - 1 - j2, :, h2]).wait_send()
            up_copy(h, n - 1 - j, p_ref.at[n - 1 - j, :, h]).start()

        @pl.when(z == n - 1)
        def _():
            if g >= flight:
                h2, j2 = divmod(g - flight, chunks)
                down_copy(h2, j2, p_ref.at[j2, :, h2]).wait_send()
            down_copy(h, j, p_ref.at[j, :, h]).start()

    def sum_tick(tick):
        h = (tick - 1) // chunks
        j = tick - h * chunks
        up_b = n - 1 - j + z
        down_b = j - (n - 1 - z)

        @pl.when((z > 0) & (z < up_b) & (up_b < n))
        def _():
            copy = up_copy(h, up_b, up_ref.at[h, up_b])
            copy.wait_recv()
            up_ref[h, up_b] += p_ref[up_b, :, h]
            copy.start()

        @pl.when((z < n - 1) & (z > down_b) & (down_b >= 0))
        def _():
            copy = down_copy(h, down_b, down_ref.at[h, down_b])
            copy.wait_recv()
            down_ref[h, down_b] += p_ref[down_b, :, h]
            copy.start()

        sum_send(tick + flight - 1)

    def sum_finish(h):
        band_ref[h] = p_ref[z, :, h]

        @pl.when(z > 0)
        def _():
            up_copy(h, z, up_ref.at[h, z]).wait_recv()
            band_ref[h] += up_ref[h, z]

        @pl.when(z < n - 1)
        def _():
            down_copy(h, z, down_ref.at[h, z]).wait_recv()
            band_ref[h] += down_ref[h, z]

    def sum_drain(h):
        for b in range(n):
            @pl.when((z < b) & (z > 0))
            def _():
                up_copy(h, b, up_ref.at[h, b]).wait_send()

            @pl.when((z > b) & (z < n - 1))
            def _():
                down_copy(h, b, down_ref.at[h, b]).wait_send()

        for j in range(chunks):
            if h * chunks + j >= pieces * chunks - flight:
                @pl.when(z == 0)
                def _():
                    up_copy(h, n - 1 - j, p_ref.at[n - 1 - j, :, h]).wait_send()

                @pl.when(z == n - 1)
                def _():
                    down_copy(h, j, p_ref.at[j, :, h]).wait_send()

    def peer(k):
        return lax.rem(box + k, boxes)

    def go_copy(h, k):
        return remote(
            band_ref.at[h, peer(k)], src_ref.at[h, box], go_send.at[h, k], go_recv.at[h, k], peer(k), z
        )

    def back_copy(h, k):
        return remote(
            res_ref.at[h, peer(k)],
            f_ref.at[z, box, h // 2, pl.ds(h % 2 * block, block)],
            back_send.at[h, k], back_recv.at[h, k], peer(k), z,
        )

    def go_start(h):
        for k in range(1, boxes):
            go_copy(h, k).start()
        src_ref[h, box] = band_ref[h, box]

    def go_wait(h):
        for k in range(1, boxes):
            go_copy(h, k).wait_recv()

    def back_start(h):
        for k in range(1, boxes):
            back_copy(h, k).start()
        f_ref[z, box, h // 2, pl.ds(h % 2 * block, block), :] = res_ref[h, box]

    def back_wait(h):
        for k in range(1, boxes):
            back_copy(h, k).wait_recv()

    def rise_copy(h, b):
        piece = f_ref.at[b, :, h // 2, pl.ds(h % 2 * block, block)]
        return remote(piece, piece, rise_send.at[h, b], rise_recv.at[h, b], box, z + 1)

    def sink_copy(h, b):
        piece = f_ref.at[b, :, h // 2, pl.ds(h % 2 * block, block)]
        return remote(piece, piece, sink_send.at[h, b], sink_recv.at[h, b], box, z - 1)

    def share_step(h, step):
        @pl.when(z >= step)
        def _():
            if step:
                rise_copy(h, z - step).wait_recv()

            @pl.when(z < n - 1)
            def _():
                rise_copy(h, z - step).start()

        @pl.when(z + step <= n - 1)
        def _():
            if step:
                sink_copy(h, z + step).wait_recv()

            @pl.when(z > 0)
            def _():
                sink_copy(h, z + step).start()

    def share_drain(h):
        for b in range(n):
            @pl.when((z >= b) & (z < n - 1))
            def _():
                rise_copy(h, b).wait_send()

            @pl.when((z <= b) & (z > 0))
            def _():
                sink_copy(h, b).wait_send()

    source_ids = lax.broadcasted_iota(jnp.int32, (sources, length), 0)
    kind_ids = lax.broadcasted_iota(jnp.int32, (blocks * 128, length), 0)

    def count_pairs(p, _):
        partner = partner_ref[pl.ds(p, 1), :]
        slots = lax.broadcasted_iota(jnp.int32, (1, length), 1)
        partner = jnp.where(slots < count_ref[p], partner, -1)
        kind = kind_ref[pl.ds(p, 1), :]
        a = jnp.where(source_ids == partner, 1.0, 0.0).astype(jnp.bfloat16)
        b = jnp.where(kind_ids == kind, 1.0, 0.0).astype(jnp.bfloat16)
        counts = lax.dot_general(
            a, b, (((1,), (1,)), ((), ())), preferred_element_type=jnp.float32
        )
        for j in range(blocks):
            sel_ref[j, pl.ds(p, sources, stride=targets), :] = counts[:, j * 128 : (j + 1) * 128]
        return 0

    def count_part(part, parts):
        first, last = targets * part // parts, targets * (part + 1) // parts
        lax.fori_loop(first, last, count_pairs, 0, unroll=4)

    def operator_part(h, part, parts):
        rows = jnp.concatenate(
            [rows_ref[:, i * width : (i + 1) * width] for i in (h, rows_here + h)], axis=1
        )
        pad = blocks * 128 - rows.shape[0]
        if pad:
            rows = jnp.concatenate([rows, jnp.zeros((pad, 2 * width), jnp.float32)], axis=0)
        high = rows.astype(jnp.bfloat16)
        low = (rows - high.astype(jnp.float32)).astype(jnp.bfloat16)
        both = jnp.concatenate([high, low], axis=0)
        tile = 512

        def one_tile(i, _):
            start = pl.multiple_of(i * tile, tile)
            chosen = jnp.concatenate(
                [sel_ref[j, pl.ds(start, tile), :] for j in range(blocks)], axis=1
            ).astype(jnp.bfloat16)
            op_ref[h, pl.ds(start, tile), :] = dot(
                jnp.concatenate([chosen, chosen], axis=1), both
            )
            return 0

        tiles = pair_rows // tile
        lax.fori_loop(tiles * part // parts, tiles * (part + 1) // parts, one_tile, 0)

    def apply_piece(h):
        group = 4
        pairs = parents // 2

        def add_sources(i, sums, first):
            tile = i % pairs * channels
            for two in range(2):
                real_rows = [tile + two * 2 + j for j in range(2)]
                reals = [src_ref[h, i // pairs, pl.ds(r, 1), :] for r in real_rows]
                imags = [src_ref[h, i // pairs, pl.ds(r + 4, 1), :] for r in real_rows]
                out = []
                for g in range(group):
                    row = pl.multiple_of((2 * i + two) * targets + first + g * 8, 8)
                    real = op_ref[h // 2, pl.ds(row, 8), 0:width]
                    imag = op_ref[h // 2, pl.ds(row, 8), width : 2 * width]
                    mine = sums[g * 4 : (g + 1) * 4]
                    for j in range(2):
                        out.append(mine[j] + real * reals[j] - imag * imags[j])
                    for j in range(2):
                        out.append(mine[2 + j] + real * imags[j] + imag * reals[j])
                sums = tuple(out)
            return sums

        for first in range(0, targets, group * 8):
            sums = tuple(jnp.zeros((8, width), jnp.float32) for _ in range(group * 4))
            sums = lax.fori_loop(
                0, sources // 2, functools.partial(add_sources, first=first), sums, unroll=2
            )
            for g in range(group):
                for c in range(4):
                    res_ref[h, first // 8 + g, c * 8 : (c + 1) * 8, :] = sums[g * 4 + c]

    barrier = pltpu.get_barrier_semaphore()
    for k in range(1, boxes):
        pl.semaphore_signal(barrier, inc=1, device_id=(peer(k), z), device_id_type=MESH)

    @pl.when(z > 0)
    def _():
        pl.semaphore_signal(barrier, inc=1, device_id=(box, z - 1), device_id_type=MESH)

    @pl.when(z < n - 1)
    def _():
        pl.semaphore_signal(barrier, inc=1, device_id=(box, z + 1), device_id_type=MESH)

    ends = jnp.where(z > 0, 1, 0) + jnp.where(z < n - 1, 1, 0)
    lax.fori_loop(0, fine, turn_one, 0)
    lax.fori_loop(0, fine // 2, raise_pair, 0, unroll=2)
    low_ref[...] = jnp.zeros_like(low_ref)
    make_piece(band_at(0), 0)
    pl.semaphore_wait(barrier, boxes - 1 + ends)
    sum_send(0)
    for i in range(1, n):
        make_piece(band_at(i), 0)
        if i < flight:
            sum_send(i)

    shared = [0] * pieces
    lowered = [0] * rows_here

    def share_to(h, last_step):
        while h < pieces and shared[h] <= min(last_step, n - 1):
            share_step(h, shared[h])
            shared[h] += 1

    def lower_to(row, last_step):
        while lowered[row] <= min(last_step, n - 1):
            lower_step(row, lowered[row])
            lowered[row] += 1

    def apply_next(h):
        go_wait(h)
        apply_piece(h)
        back_start(h)

    def go_back(h):
        back_wait(h)
        share_to(h, 0)

    for h in range(pieces):
        for step in range(1, chunks + 1):
            if h == 0:
                count_part(step - 1, chunks)
            elif step == 1:
                if h == 1:
                    for row in range(1, rows_here):
                        for i in range(n):
                            make_piece(band_at(i), row)
                else:
                    if h % 2 == 0:
                        operator_part(h // 2, 1, 2)
                    else:
                        share_to(h - 3, 2)
                        share_to(h - 2, 1)
                    apply_next(h - 1)
            elif step == 2:
                if h == 1:
                    operator_part(0, 0, 1)
                    apply_next(0)
                else:
                    go_back(h - 1)
                    share_to(h - 2 if h % 2 == 0 else h - 3, n - 1 if h % 2 else 1)
            elif step == chunks:
                if h == 1:
                    go_back(0)
                if h % 2 and h + 1 < pieces:
                    operator_part(h // 2 + 1, 0, 2)
                if h % 2 and h > 1:
                    share_to(h - 2, 2)
                    share_to(h - 1, 1)
            sum_tick(h * chunks + step)
        sum_finish(h)
        go_start(h)
    last = pieces - 1
    for h in range(last - 1):
        share_to(h, n - 1)
    apply_next(last)
    share_to(last - 1, 2)
    for row in range(rows_here - 1):
        lower_to(row, 0)
    go_back(last)
    for row in range(rows_here - 1):
        lower_to(row, 1)
    share_to(last - 1, n - 1)
    share_to(last, 1)
    for row in range(rows_here - 1):
        lower_to(row, 2)
    lower_to(rows_here - 1, 0)
    share_to(last, 2)
    for row in range(rows_here - 1):
        lower_to(row, n - 1)
    lower_to(rows_here - 1, 1)
    for step in range(2, n):
        share_to(last, step)
        lower_to(rows_here - 1, step)
    lax.fori_loop(0, fine, lower_last, 0, unroll=4)
    for h in range(pieces):
        sum_drain(h)
        share_drain(h)
        for k in range(1, boxes):
            go_copy(h, k).wait_send()
            back_copy(h, k).wait_send()


def exchange(outgoing, slots, partner, kind, count, rows, n, boxes):
    fine, channels, fine_width = outgoing.shape
    parents = slots.shape[0] // 8
    targets = partner.shape[0]
    halves = TP // n // boxes
    pieces = 2 * halves
    block = parents * channels // 2
    kinds = rows.shape[0]
    kind_blocks = -(-kinds // 128)
    shape = (n, boxes, pieces, block, PP)
    vmem = pl.BlockSpec(memory_space=pltpu.VMEM)
    smem = pl.BlockSpec(memory_space=pltpu.SMEM)
    dma = pltpu.SemaphoreType.DMA
    consts = [jnp.asarray(t) for t in tables(channels, n, boxes, halves)]
    f32 = jnp.float32
    return pl.pallas_call(
        functools.partial(exchange_kernel, targets=targets, channels=channels),
        out_shape=jax.ShapeDtypeStruct(outgoing.shape, f32),
        in_specs=[vmem, smem] + [vmem] * 7 + [smem, vmem],
        out_specs=vmem,
        scratch_shapes=[
            pltpu.VMEM((fine, TP * channels, PP), f32),
            pltpu.VMEM((fine, 2, TP, PP), f32),
            pltpu.VMEM((fine, parents, PP), f32),
            pltpu.VMEM(shape, f32),
            pltpu.VMEM((n, boxes, halves, 2 * block, PP), f32),
            pltpu.VMEM((2, boxes * channels, fine * PP), jnp.bfloat16),
            pltpu.VMEM((TF * channels, fine * PP), f32),
            pltpu.VMEM((kind_blocks, targets * targets, 128), f32),
            pltpu.VMEM((halves, targets * targets, 2 * PP), f32),
            pltpu.VMEM((pieces, n, boxes, block, PP), f32),
            pltpu.VMEM((pieces, n, boxes, block, PP), f32),
            pltpu.VMEM((pieces, boxes, block, PP), f32),
            pltpu.VMEM((pieces, boxes, block, PP), f32),
            pltpu.VMEM((pieces, boxes, block, PP), f32),
        ]
        + [dma((pieces, n))] * 4
        + [dma((pieces, boxes))] * 4
        + [dma((pieces, n))] * 4,
        compiler_params=pltpu.CompilerParams(
            vmem_limit_bytes=56 * 2**20, collective_id=0, has_side_effects=True
        ),
        name="exchange",
    )(
        outgoing, slots, *consts, jnp.asarray(np_phase()), partner, kind, count, rows
    )


def body(outgoing, fine_slot, translator, list_partner, list_kind, list_count):
    dir_count = lax.axis_size("dir")
    box_count = lax.axis_size("box")
    fine_here, channels, _ = outgoing.shape
    whole_rows = TP // dir_count % box_count == 0 and dir_count >= 4 and box_count % 2 == 0
    if not whole_rows or fine_here % 4 or channels != 8 or fine_slot.shape[0] != 64 or list_partner.shape[0] % 32:
        return general_body(
            outgoing, fine_slot, translator, list_partner, list_kind, list_count
        )
    box_index = lax.axis_index("box")
    kinds, _, dirs_here = translator.shape
    split_here = dirs_here // box_count
    rows = lax.dynamic_slice_in_dim(translator, box_index * split_here, split_here, 2)
    rows = rows.reshape(kinds, 2 * split_here)
    return exchange(
        outgoing, fine_slot, list_partner, list_kind, list_count, rows, dir_count, box_count
    )


def solution(mesh):
    placed = (P(("box", "dir"), None, None), P("box"), P(None, None, "dir"), P(), P(), P())
    return jax.shard_map(
        body, mesh=mesh, in_specs=placed, out_specs=P(("box", "dir"), None, None), check_vma=False
    )
```

```python
import functools

import jax
import jax.numpy as jnp
import ml_dtypes
import numpy as np
from jax import lax
from jax.experimental import pallas as pl
from jax.experimental.pallas import tpu as pltpu
from jax.sharding import PartitionSpec as P

TF = 32
PF = 64
TP = 64
PP = 128


wave_shift = 5.0
highest = lax.Precision.HIGHEST


def theta_table(fine_count, coarse_count):
    fine_angle = (jnp.arange(fine_count, dtype=jnp.float32) + 0.5) * (jnp.pi / fine_count)
    coarse_angle = (jnp.arange(coarse_count, dtype=jnp.float32) + 0.5) * (jnp.pi / coarse_count)
    orders = jnp.arange(1, fine_count, dtype=jnp.float32)
    products = jnp.cos(coarse_angle[:, None, None] * orders) * jnp.cos(
        fine_angle[None, :, None] * orders
    )
    return (1.0 + 2.0 * jnp.sum(products, axis=2)) / fine_count


def phi_table(fine_count, coarse_count):
    fine_angle = jnp.arange(fine_count, dtype=jnp.float32) * (2.0 * jnp.pi / fine_count)
    coarse_angle = jnp.arange(coarse_count, dtype=jnp.float32) * (2.0 * jnp.pi / coarse_count)
    offset = coarse_angle[:, None] - fine_angle[None, :]
    orders = jnp.arange(1, fine_count // 2, dtype=jnp.float32)
    series = jnp.sum(jnp.cos(offset[:, :, None] * orders), axis=2)
    return (1.0 + 2.0 * series + jnp.cos(offset * (fine_count // 2))) / fine_count


def octant_phase(octant, first_theta, theta_count, coarse_theta, coarse_phi):
    theta_index = first_theta + jnp.arange(theta_count, dtype=jnp.int32)
    polar = (theta_index.astype(jnp.float32) + 0.5) * (jnp.pi / coarse_theta)
    azimuth = jnp.arange(coarse_phi, dtype=jnp.float32) * (2.0 * jnp.pi / coarse_phi)
    along_x = jnp.sin(polar)[:, None] * jnp.cos(azimuth)[None, :]
    along_y = jnp.sin(polar)[:, None] * jnp.sin(azimuth)[None, :]
    along_z = jnp.cos(polar)[:, None] + 0.0 * azimuth[None, :]
    sign_x = (2 * (octant % 2) - 1).astype(jnp.float32)
    sign_y = (2 * (octant // 2 % 2) - 1).astype(jnp.float32)
    sign_z = (2 * (octant // 4) - 1).astype(jnp.float32)
    phase_angle = wave_shift * (
        sign_x[:, None, None] * along_x[None]
        + sign_y[:, None, None] * along_y[None]
        + sign_z[:, None, None] * along_z[None]
    )
    return (jnp.cos(phase_angle), jnp.sin(phase_angle))


def translate(sources, kernel_table, partner, kind, count):
    targets, length = partner.shape
    source_rows, _, excite, lanes = sources.shape
    kinds = kernel_table.shape[0]
    blocks = 7
    block_width = length // blocks
    flat_sources = sources.reshape(source_rows, 2 * excite * lanes)
    flat_kernel = kernel_table.reshape(kinds, 2 * lanes)
    source_ids = jnp.arange(source_rows, dtype=jnp.int32)
    kind_ids = jnp.arange(kinds, dtype=jnp.int32)

    def add_block(block_step, running):
        begin_at = block_step * block_width
        near_rows = lax.dynamic_slice_in_dim(partner, begin_at, block_width, 1)
        kind_rows = lax.dynamic_slice_in_dim(kind, begin_at, block_width, 1)
        position = begin_at + jnp.arange(block_width, dtype=jnp.int32)
        alive_mask = (position[None, :] < count[:, None]).astype(jnp.float32)
        select_source = (
            (near_rows[:, :, None] == source_ids)
            .astype(jnp.float32)
            .reshape(targets * block_width, source_rows)
        )
        select_kind = (
            (kind_rows[:, :, None] == kind_ids).astype(jnp.float32) * alive_mask[:, :, None]
        ).reshape(targets * block_width, kinds)
        picked = jnp.dot(
            select_source, flat_sources, precision=highest, preferred_element_type=jnp.float32
        )
        picked = picked.reshape(targets, block_width, 2, excite, lanes)
        factor = jnp.dot(
            select_kind, flat_kernel, precision=highest, preferred_element_type=jnp.float32
        )
        factor = factor.reshape(targets, block_width, 2, 1, lanes)
        along_real = factor[:, :, 0]
        along_imag = factor[:, :, 1]
        real_part = picked[:, :, 0]
        imag_part = picked[:, :, 1]
        new_real = jnp.sum(along_real * real_part - along_imag * imag_part, axis=1)
        new_imag = jnp.sum(along_real * imag_part + along_imag * real_part, axis=1)
        return running + jnp.stack([new_real, new_imag], axis=1)

    initial = jnp.zeros((targets, 2, excite, lanes), jnp.float32)
    return lax.fori_loop(0, blocks, add_block, initial)


def general_body(outgoing, fine_slot, translator, list_partner, list_kind, list_count):
    dir_count = lax.axis_size("dir")
    box_count = lax.axis_size("box")
    box_index = lax.axis_index("box")
    dir_index = lax.axis_index("dir")
    channels = outgoing.shape[1]
    excite = channels // 2
    fine_here = outgoing.shape[0]
    row_boxes = fine_slot.shape[0]
    parents_here = row_boxes // 8
    theta_here = TP // dir_count
    dirs_here = translator.shape[2]
    up_theta = theta_table(TF, TP)
    up_phi = phi_table(PF, PP)
    octant = fine_slot % 8
    local_parent = fine_slot // 8 % parents_here
    onehot = (local_parent[None, :] == jnp.arange(parents_here, dtype=jnp.int32)[:, None]).astype(
        jnp.float32
    )
    cos_table, sin_table = octant_phase(octant, dir_index * theta_here, theta_here, TP, PP)
    cos_table = cos_table[:, :, None, :]
    sin_table = sin_table[:, :, None, :]
    pattern = outgoing.reshape(fine_here, channels, TF, PF)
    raised = jnp.einsum("ut,fctp->fcup", up_theta, pattern, precision=highest)
    raised = jnp.einsum("qp,fcup->fucq", up_phi, raised, precision=highest)
    spread = lax.all_to_all(raised, "dir", split_axis=1, concat_axis=0, tiled=True)
    real_part = spread[:, :, :excite]
    imag_part = spread[:, :, excite:]
    shifted = jnp.concatenate(
        [
            real_part * cos_table + imag_part * sin_table,
            imag_part * cos_table - real_part * sin_table,
        ],
        axis=2,
    )
    parent_out = jnp.einsum("pf,fucq->pcuq", onehot, shifted, precision=highest)
    parent_out = parent_out.reshape(parents_here, channels, dirs_here)
    split_here = dirs_here // box_count
    sectioned = jnp.swapaxes(
        parent_out.reshape(parents_here, channels, box_count, split_here), 1, 2
    )
    sectioned = sectioned.reshape(parents_here, box_count, channels * split_here)
    gathered = lax.all_to_all(sectioned, "box", split_axis=1, concat_axis=0, tiled=True)
    sources = gathered.reshape(box_count * parents_here, 2, excite, split_here)
    kernel_rows = lax.dynamic_slice_in_dim(translator, box_index * split_here, split_here, 2)
    translated = translate(sources, kernel_rows, list_partner, list_kind, list_count)
    translated = translated.reshape(box_count * parents_here, 1, channels * split_here)
    returned = lax.all_to_all(translated, "box", split_axis=0, concat_axis=1, tiled=True)
    incoming = jnp.swapaxes(returned.reshape(parents_here, box_count, channels, split_here), 1, 2)
    incoming = incoming.reshape(parents_here, channels, dirs_here)
    fields = incoming.reshape(parents_here, channels, theta_here, PP)
    spread_back = jnp.einsum("pf,pcuq->fucq", onehot, fields, precision=highest)
    real_part = spread_back[:, :, :excite]
    imag_part = spread_back[:, :, excite:]
    shifted_back = jnp.concatenate(
        [
            real_part * cos_table - imag_part * sin_table,
            imag_part * cos_table + real_part * sin_table,
        ],
        axis=2,
    )
    arrived_back = lax.all_to_all(shifted_back, "dir", split_axis=0, concat_axis=1, tiled=True)
    arrived_back = jnp.einsum("qp,fucq->fucp", up_phi, arrived_back, precision=highest) * (PF / PP)
    result = jnp.einsum("ut,fucp->fctp", up_theta, arrived_back, precision=highest) * (TF / TP)
    return result.reshape(fine_here, channels, TF * PF)


def np_theta(fine_count, coarse_count):
    fine_angle = (np.arange(fine_count) + 0.5) * (np.pi / fine_count)
    coarse_angle = (np.arange(coarse_count) + 0.5) * (np.pi / coarse_count)
    orders = np.arange(1, fine_count)
    products = np.cos(coarse_angle[:, None, None] * orders) * np.cos(
        fine_angle[None, :, None] * orders
    )
    return (1.0 + 2.0 * products.sum(2)) / fine_count


def np_phi(fine_count, coarse_count):
    fine_angle = np.arange(fine_count) * (2.0 * np.pi / fine_count)
    coarse_angle = np.arange(coarse_count) * (2.0 * np.pi / coarse_count)
    offset = coarse_angle[:, None] - fine_angle[None, :]
    orders = np.arange(1, fine_count // 2)
    series = np.cos(offset[:, :, None] * orders).sum(2)
    return (1.0 + 2.0 * series + np.cos(offset * (fine_count // 2))) / fine_count


def np_phase():
    polar = (np.arange(TP) + 0.5) * (np.pi / TP)
    azimuth = np.arange(PP) * (2.0 * np.pi / PP)
    along = [
        np.sin(polar)[:, None] * np.cos(azimuth)[None, :],
        np.sin(polar)[:, None] * np.sin(azimuth)[None, :],
        np.cos(polar)[:, None] + 0.0 * azimuth[None, :],
    ]
    cx, cy, cz = (np.cos(wave_shift * a) for a in along)
    sx, sy, sz = (np.sin(wave_shift * a) for a in along)
    terms = [
        cx * cy * cz, sx * sy * cz, sx * cy * sz, cx * sy * sz,
        sx * cy * cz, cx * sy * cz, cx * cy * sz, sx * sy * sz,
    ]
    return np.stack(terms).astype(np.float32)


def np_split(values):
    high = values.astype(ml_dtypes.bfloat16)
    low = (values - high.astype(np.float64)).astype(ml_dtypes.bfloat16)
    return high, low


def tables(channels, n, boxes, halves):
    theta = np_theta(TF, TP)
    phi = np_phi(PF, PP)
    eye = np.eye(channels)
    order = np.concatenate([np.arange(0, TF, 2), np.arange(1, TF, 2)])
    theta = theta[:, order]
    up_phi = np.kron(np.eye(2), phi.T)
    up_theta = np.kron(theta, eye)
    down_phi = np.kron(np.eye(2), phi) * (PF / PP)
    uph, upl = np_split(up_phi)
    uth, utl = np_split(up_theta)
    dph, dpl = np_split(down_phi)
    blocks = theta.reshape(n, boxes, halves, TF).transpose(0, 2, 3, 1) * (TF / TP)
    down = []
    for block in blocks.reshape(n * halves, TF, boxes):
        high, low = np_split(np.kron(block, eye))
        down.append(np.concatenate([high, high, low], axis=1))
    return (
        np.concatenate([uph, uph, upl], axis=0),
        np.concatenate([uth, uth, utl], axis=1),
        np.stack(down),
        np.concatenate([dph, dph, dpl], axis=0),
    )


def split3(values, axis):
    high = values.astype(jnp.bfloat16)
    low = (values - high.astype(jnp.float32)).astype(jnp.bfloat16)
    return jnp.concatenate([high, low, high], axis=axis)


def dot(a, b):
    return jnp.dot(a, b, preferred_element_type=jnp.float32)


MESH = pl.DeviceIdType.MESH


def exchange_kernel(
    x_ref, slot_ref, up_phi_ref, up_theta_ref, down_theta_ref, down_phi_ref, phase_ref,
    partner_ref, kind_ref, count_ref, rows_ref, out_ref,
    r_ref, turn_ref, own_ref, p_ref, f_ref, child_ref, low_ref,
    sel_ref, op_ref, up_ref, down_ref, band_ref, src_ref, res_ref,
    up_send, up_recv, down_send, down_recv, go_send, go_recv, back_send, back_recv,
    rise_send, rise_recv, sink_send, sink_recv,
    *, targets, channels,
):
    n, boxes, halves, block, width = p_ref.shape
    box = lax.axis_index("box")
    z = lax.axis_index("dir")
    sources = targets
    blocks = sel_ref.shape[0]
    length = partner_ref.shape[1]
    pair_rows = sources * targets
    fine = x_ref.shape[0]
    parents = block // channels
    turn_sign = jnp.where(
        lax.broadcasted_iota(jnp.int32, (channels, width), 0) < channels // 2, 1.0, -1.0
    )

    def raise_pair(i, _):
        stacked = []
        for f in range(2):
            x = x_ref[2 * i + f]
            x = jnp.concatenate(
                [x[:, j * 2 * PF : (j + 1) * 2 * PF] for j in range(TF // 2)], axis=0
            )
            y = dot(split3(x, 1), up_phi_ref[...])
            stacked.append(jnp.concatenate([y[:, :PP], y[:, PP:]], axis=0))
        z3 = split3(jnp.concatenate(stacked, axis=1), 0)
        raised = dot(up_theta_ref[...], z3)
        r_ref[2 * i] = raised[:, :PP]
        r_ref[2 * i + 1] = raised[:, PP:]
        return 0

    def turn_one(f, _):
        slot = slot_ref[z * fine + f]
        octant = slot % 8
        parent = slot // 8 % parents
        x = (2 * (octant % 2) - 1).astype(jnp.float32)
        y = (2 * (octant // 2 % 2) - 1).astype(jnp.float32)
        w = (2 * (octant // 4) - 1).astype(jnp.float32)
        t = [phase_ref[i] for i in range(8)]
        turn_ref[f, 0] = t[0] - (x * y) * t[1] - (x * w) * t[2] - (y * w) * t[3]
        turn_ref[f, 1] = x * t[4] + y * t[5] + w * t[6] - (x * y * w) * t[7]
        rows = lax.broadcasted_iota(jnp.int32, (parents, width), 0)
        own_ref[f] = jnp.where(rows == parent, 1.0, 0.0)
        return 0

    def make_piece(b, h):
        def one_row(bb, _):
            u = (b * boxes + bb) * halves + h
            sums = [jnp.zeros((channels, width), jnp.float32) for _ in range(parents)]
            for f in range(fine):
                r = r_ref[f, pl.ds(pl.multiple_of(u * channels, channels), channels), :]
                cos = turn_ref[f, 0, pl.ds(u, 1), :]
                sin = turn_ref[f, 1, pl.ds(u, 1), :]
                moved = r * cos + pltpu.roll(r, channels // 2, 0) * (turn_sign * sin)
                for p in range(parents):
                    sums[p] = sums[p] + moved * own_ref[f, p : p + 1, :]
            for p in range(parents):
                p_ref[b, bb, h, p * channels : (p + 1) * channels, :] = sums[p]
            return 0

        lax.fori_loop(0, boxes, one_row, 0)

    def band_at(k):
        middle = n - 1 - k // 2 if k % 2 == 0 else k // 2
        return jnp.where(z == 0, n - 1 - k, jnp.where(z == n - 1, k, middle))

    def lower_piece(b, h):
        def two_rows(i, _):
            fields = [
                [
                    f_ref[b, 2 * i + r, h, p * channels : (p + 1) * channels, :]
                    for p in range(parents)
                ]
                for r in range(2)
            ]
            first = (b * boxes + 2 * i) * halves + h
            for f in range(fine):
                both = []
                for r in range(2):
                    u = first + r * halves
                    mine = fields[r][0] * own_ref[f, 0:1, :]
                    for p in range(1, parents):
                        mine = mine + fields[r][p] * own_ref[f, p : p + 1, :]
                    cos = turn_ref[f, 0, pl.ds(u, 1), :]
                    sin = turn_ref[f, 1, pl.ds(u, 1), :]
                    both.append(
                        mine * cos - pltpu.roll(mine, channels // 2, 0) * (turn_sign * sin)
                    )
                child = jnp.concatenate(both, axis=0)
                high = child.astype(jnp.bfloat16)
                low = (child - high.astype(jnp.float32)).astype(jnp.bfloat16)
                row = pl.multiple_of(i * 2 * channels, 2 * channels)
                lanes = slice(f * width, (f + 1) * width)
                child_ref[0, pl.ds(row, 2 * channels), lanes] = high
                child_ref[1, pl.ds(row, 2 * channels), lanes] = low
            return 0

        lax.fori_loop(0, boxes // 2, two_rows, 0)
        tile = 4 * width

        def add_tile(i, _):
            lanes = pl.ds(pl.multiple_of(i * tile, tile), tile)
            high = child_ref[0, :, lanes]
            low = child_ref[1, :, lanes]
            low_ref[:, lanes] += dot(
                down_theta_ref[b * halves + h], jnp.concatenate([high, low, high], axis=0)
            )
            return 0

        lax.fori_loop(0, fine * width // tile, add_tile, 0)

    def lower_step(h, step):
        if step == 0:
            lower_piece(z, h)
            return

        def one_side(i, _):
            b = jnp.where(i == 0, z - step, z + step)

            @pl.when((b >= 0) & (b < n))
            def _():
                lower_piece(b, h)

            return 0

        lax.fori_loop(0, 2, one_side, 0)

    def lower_last(f, _):
        part = low_ref[:, pl.ds(pl.multiple_of(f * width, width), width)]
        half = part.shape[0] // 2
        y = jnp.concatenate([part[:half], part[half:]], axis=1)
        x = dot(split3(y, 1), down_phi_ref[...])
        out_ref[f] = jnp.concatenate(
            [x[j * channels : (j + 1) * channels] for j in range(TF // 2)], axis=1
        )
        return 0

    def remote(src, dst, send, recv, to_box, to_dir):
        return pltpu.make_async_remote_copy(
            src_ref=src, dst_ref=dst, send_sem=send, recv_sem=recv,
            device_id=(to_box, to_dir), device_id_type=MESH,
        )

    def up_copy(h, b, src):
        return remote(src, up_ref.at[h, b], up_send.at[h, b], up_recv.at[h, b], box, z + 1)

    def down_copy(h, b, src):
        return remote(src, down_ref.at[h, b], down_send.at[h, b], down_recv.at[h, b], box, z - 1)

    chunks = n - 1

    def sum_send(g):
        if g >= halves * chunks:
            return
        h, j = divmod(g, chunks)

        @pl.when(z == 0)
        def _():
            if g >= 2:
                h2, j2 = divmod(g - 2, chunks)
                up_copy(h2, n - 1 - j2, p_ref.at[n - 1 - j2, :, h2]).wait_send()
            up_copy(h, n - 1 - j, p_ref.at[n - 1 - j, :, h]).start()

        @pl.when(z == n - 1)
        def _():
            if g >= 2:
                h2, j2 = divmod(g - 2, chunks)
                down_copy(h2, j2, p_ref.at[j2, :, h2]).wait_send()
            down_copy(h, j, p_ref.at[j, :, h]).start()

    def sum_tick(tick):
        h = (tick - 1) // chunks
        j = tick - h * chunks
        up_b = n - 1 - j + z
        down_b = j - (n - 1 - z)

        @pl.when((z > 0) & (z < up_b) & (up_b < n))
        def _():
            copy = up_copy(h, up_b, up_ref.at[h, up_b])
            copy.wait_recv()
            up_ref[h, up_b] += p_ref[up_b, :, h]
            copy.start()

        @pl.when((z < n - 1) & (z > down_b) & (down_b >= 0))
        def _():
            copy = down_copy(h, down_b, down_ref.at[h, down_b])
            copy.wait_recv()
            down_ref[h, down_b] += p_ref[down_b, :, h]
            copy.start()

        sum_send(tick + 1)

    def sum_finish(h):
        band_ref[h] = p_ref[z, :, h]

        @pl.when(z > 0)
        def _():
            up_copy(h, z, up_ref.at[h, z]).wait_recv()
            band_ref[h] += up_ref[h, z]

        @pl.when(z < n - 1)
        def _():
            down_copy(h, z, down_ref.at[h, z]).wait_recv()
            band_ref[h] += down_ref[h, z]

    def sum_drain(h):
        for b in range(n):
            @pl.when((z < b) & (z > 0))
            def _():
                up_copy(h, b, up_ref.at[h, b]).wait_send()

            @pl.when((z > b) & (z < n - 1))
            def _():
                down_copy(h, b, down_ref.at[h, b]).wait_send()

        for j in range(chunks):
            if h * chunks + j >= halves * chunks - 2:
                @pl.when(z == 0)
                def _():
                    up_copy(h, n - 1 - j, p_ref.at[n - 1 - j, :, h]).wait_send()

                @pl.when(z == n - 1)
                def _():
                    down_copy(h, j, p_ref.at[j, :, h]).wait_send()

    def peer(k):
        return lax.rem(box + k, boxes)

    def go_copy(h, k):
        return remote(
            band_ref.at[h, peer(k)], src_ref.at[h, box], go_send.at[h, k], go_recv.at[h, k], peer(k), z
        )

    def back_copy(h, k):
        return remote(
            res_ref.at[h, pl.ds(pl.multiple_of(peer(k) * block, block), block)],
            f_ref.at[z, box, h],
            back_send.at[h, k], back_recv.at[h, k], peer(k), z,
        )

    def go_start(h):
        for k in range(1, boxes):
            go_copy(h, k).start()
        src_ref[h, box] = band_ref[h, box]

    def go_wait(h):
        for k in range(1, boxes):
            go_copy(h, k).wait_recv()

    def back_start(h):
        for k in range(1, boxes):
            back_copy(h, k).start()
        f_ref[z, box, h] = res_ref[h, pl.ds(pl.multiple_of(box * block, block), block)]

    def back_wait(h):
        for k in range(1, boxes):
            back_copy(h, k).wait_recv()

    def rise_copy(h, b):
        piece = f_ref.at[b, :, h]
        return remote(piece, piece, rise_send.at[h, b], rise_recv.at[h, b], box, z + 1)

    def sink_copy(h, b):
        piece = f_ref.at[b, :, h]
        return remote(piece, piece, sink_send.at[h, b], sink_recv.at[h, b], box, z - 1)

    def share_step(h, step):
        @pl.when(z >= step)
        def _():
            if step:
                rise_copy(h, z - step).wait_recv()

            @pl.when(z < n - 1)
            def _():
                rise_copy(h, z - step).start()

        @pl.when(z + step <= n - 1)
        def _():
            if step:
                sink_copy(h, z + step).wait_recv()

            @pl.when(z > 0)
            def _():
                sink_copy(h, z + step).start()

    def share_drain(h):
        for b in range(n):
            @pl.when((z >= b) & (z < n - 1))
            def _():
                rise_copy(h, b).wait_send()

            @pl.when((z <= b) & (z > 0))
            def _():
                sink_copy(h, b).wait_send()

    source_ids = lax.broadcasted_iota(jnp.int32, (sources, length), 0)
    kind_ids = lax.broadcasted_iota(jnp.int32, (blocks * 128, length), 0)

    def count_pairs(p, _):
        partner = partner_ref[pl.ds(p, 1), :]
        slots = lax.broadcasted_iota(jnp.int32, (1, length), 1)
        partner = jnp.where(slots < count_ref[p], partner, -1)
        kind = kind_ref[pl.ds(p, 1), :]
        a = jnp.where(source_ids == partner, 1.0, 0.0).astype(jnp.bfloat16)
        b = jnp.where(kind_ids == kind, 1.0, 0.0).astype(jnp.bfloat16)
        counts = lax.dot_general(
            a, b, (((1,), (1,)), ((), ())), preferred_element_type=jnp.float32
        )
        for j in range(blocks):
            sel_ref[j, pl.ds(p, sources, stride=targets), :] = counts[:, j * 128 : (j + 1) * 128]
        return 0

    def count_part(part, parts):
        first, last = targets * part // parts, targets * (part + 1) // parts
        lax.fori_loop(first, last, count_pairs, 0, unroll=4)

    def operator_half(h):
        rows = jnp.concatenate(
            [rows_ref[:, i * width : (i + 1) * width] for i in (h, halves + h)], axis=1
        )
        pad = blocks * 128 - rows.shape[0]
        if pad:
            rows = jnp.concatenate([rows, jnp.zeros((pad, 2 * width), jnp.float32)], axis=0)
        high = rows.astype(jnp.bfloat16)
        low = (rows - high.astype(jnp.float32)).astype(jnp.bfloat16)
        both = jnp.concatenate([high, low], axis=0)
        tile = 512

        def one_tile(i, _):
            start = pl.multiple_of(i * tile, tile)
            chosen = jnp.concatenate(
                [sel_ref[j, pl.ds(start, tile), :] for j in range(blocks)], axis=1
            ).astype(jnp.bfloat16)
            op_ref[h, pl.ds(start, tile), :] = dot(
                jnp.concatenate([chosen, chosen], axis=1), both
            )
            return 0

        lax.fori_loop(0, pair_rows // tile, one_tile, 0)

    def apply_half(h, part, parts):
        half = channels // 2
        group = 2
        per_box = block // channels

        def add_source(s, sums, first):
            giver = s // per_box
            row0 = (s % per_box) * channels
            fields = [src_ref[h, giver, pl.ds(row0 + c, 1), :] for c in range(channels)]
            out = []
            for g in range(group):
                row = pl.multiple_of(s * targets + first + g * 8, 8)
                real = op_ref[h, pl.ds(row, 8), 0:width]
                imag = op_ref[h, pl.ds(row, 8), width : 2 * width]
                mine = sums[g * channels : (g + 1) * channels]
                for e in range(half):
                    out.append(mine[e] + real * fields[e] - imag * fields[half + e])
                for e in range(half):
                    out.append(mine[half + e] + real * fields[half + e] + imag * fields[e])
            return tuple(out)

        for first in range(targets * part // parts, targets * (part + 1) // parts, group * 8):
            sums = tuple(jnp.zeros((8, width), jnp.float32) for _ in range(group * channels))
            sums = lax.fori_loop(
                0, sources, functools.partial(add_source, first=first), sums, unroll=4
            )
            for g in range(group):
                for c in range(channels):
                    start = (first + g * 8) * channels + c
                    res_ref[h, pl.ds(start, 8, stride=channels), :] = sums[g * channels + c]

    barrier = pltpu.get_barrier_semaphore()
    for k in range(1, boxes):
        pl.semaphore_signal(barrier, inc=1, device_id=(peer(k), z), device_id_type=MESH)

    @pl.when(z > 0)
    def _():
        pl.semaphore_signal(barrier, inc=1, device_id=(box, z - 1), device_id_type=MESH)

    @pl.when(z < n - 1)
    def _():
        pl.semaphore_signal(barrier, inc=1, device_id=(box, z + 1), device_id_type=MESH)

    ends = jnp.where(z > 0, 1, 0) + jnp.where(z < n - 1, 1, 0)
    lax.fori_loop(0, fine, turn_one, 0)
    lax.fori_loop(0, fine // 2, raise_pair, 0, unroll=2)
    low_ref[...] = jnp.zeros_like(low_ref)
    make_piece(band_at(0), 0)
    pl.semaphore_wait(barrier, boxes - 1 + ends)
    sum_send(0)
    make_piece(band_at(1), 0)
    sum_send(1)
    for i in range(2, n):
        make_piece(band_at(i), 0)

    shared = [0] * halves
    lowered = [0] * halves

    def share_to(h, last_step):
        while shared[h] <= min(last_step, n - 1):
            share_step(h, shared[h])
            shared[h] += 1

    def lower_to(h, last_step):
        while lowered[h] <= min(last_step, n - 1):
            lower_step(h, lowered[h])
            lowered[h] += 1

    for h in range(halves):
        tick = h * chunks
        for step in range(1, chunks + 1):
            if h == 0 and step < chunks:
                count_part(step - 1, chunks - 1)
                if step == 1:
                    for later in range(1, halves):
                        for i in range(n):
                            make_piece(band_at(i), later)
            if h == 0 and step == chunks:
                operator_half(h)
            if h and step == 1:
                apply_half(h - 1, 0, 2)
                apply_half(h - 1, 1, 2)
                back_start(h - 1)
            if h and step == 2:
                back_wait(h - 1)
                share_to(h - 1, 0)
                operator_half(h)
            sum_tick(tick + step)
        sum_finish(h)
        go_start(h)
        if h:
            share_to(h - 1, 1)
            lower_to(h - 1, 0)
        go_wait(h)
    last = halves - 1
    apply_half(last, 0, 2)
    apply_half(last, 1, 2)
    back_start(last)
    for h in range(last):
        share_to(h, 2)
        lower_to(h, 1)
    back_wait(last)
    share_to(last, 0)
    for h in range(last):
        share_to(h, n - 1)
        lower_to(h, 2)
    lower_to(last, 0)
    share_to(last, 1)
    for h in range(last):
        lower_to(h, n - 1)
    lower_to(last, 1)
    for step in range(2, n):
        share_to(last, step)
        lower_to(last, step)
    lax.fori_loop(0, fine, lower_last, 0, unroll=4)
    for h in range(halves):
        sum_drain(h)
        share_drain(h)
        for k in range(1, boxes):
            go_copy(h, k).wait_send()
            back_copy(h, k).wait_send()


def exchange(outgoing, slots, partner, kind, count, rows, n, boxes):
    fine, channels, fine_width = outgoing.shape
    parents = slots.shape[0] // 8
    targets = partner.shape[0]
    halves = TP // n // boxes
    block = parents * channels
    kinds = rows.shape[0]
    kind_blocks = -(-kinds // 128)
    shape = (n, boxes, halves, block, PP)
    vmem = pl.BlockSpec(memory_space=pltpu.VMEM)
    smem = pl.BlockSpec(memory_space=pltpu.SMEM)
    dma = pltpu.SemaphoreType.DMA
    consts = [jnp.asarray(t) for t in tables(channels, n, boxes, halves)]
    f32 = jnp.float32
    return pl.pallas_call(
        functools.partial(exchange_kernel, targets=targets, channels=channels),
        out_shape=jax.ShapeDtypeStruct(outgoing.shape, f32),
        in_specs=[vmem, smem] + [vmem] * 7 + [smem, vmem],
        out_specs=vmem,
        scratch_shapes=[
            pltpu.VMEM((fine, TP * channels, PP), f32),
            pltpu.VMEM((fine, 2, TP, PP), f32),
            pltpu.VMEM((fine, parents, PP), f32),
            pltpu.VMEM(shape, f32),
            pltpu.VMEM(shape, f32),
            pltpu.VMEM((2, boxes * channels, fine * PP), jnp.bfloat16),
            pltpu.VMEM((TF * channels, fine * PP), f32),
            pltpu.VMEM((kind_blocks, targets * targets, 128), f32),
            pltpu.VMEM((halves, targets * targets, 2 * PP), f32),
            pltpu.VMEM((halves, n, boxes, block, PP), f32),
            pltpu.VMEM((halves, n, boxes, block, PP), f32),
            pltpu.VMEM((halves, boxes, block, PP), f32),
            pltpu.VMEM((halves, boxes, block, PP), f32),
            pltpu.VMEM((halves, targets * channels, PP), f32),
        ]
        + [dma((halves, n))] * 4
        + [dma((halves, boxes))] * 4
        + [dma((halves, n))] * 4,
        compiler_params=pltpu.CompilerParams(
            vmem_limit_bytes=56 * 2**20, collective_id=0, has_side_effects=True
        ),
        name="exchange",
    )(
        outgoing, slots, *consts, jnp.asarray(np_phase()), partner, kind, count, rows
    )


def body(outgoing, fine_slot, translator, list_partner, list_kind, list_count):
    dir_count = lax.axis_size("dir")
    box_count = lax.axis_size("box")
    fine_here, channels, _ = outgoing.shape
    whole_rows = TP // dir_count % box_count == 0 and dir_count >= 4 and box_count % 2 == 0
    if not whole_rows or fine_here % 4 or channels % 8 or list_partner.shape[0] % 32:
        return general_body(
            outgoing, fine_slot, translator, list_partner, list_kind, list_count
        )
    box_index = lax.axis_index("box")
    kinds, _, dirs_here = translator.shape
    split_here = dirs_here // box_count
    rows = lax.dynamic_slice_in_dim(translator, box_index * split_here, split_here, 2)
    rows = rows.reshape(kinds, 2 * split_here)
    return exchange(
        outgoing, fine_slot, list_partner, list_kind, list_count, rows, dir_count, box_count
    )


def solution(mesh):
    placed = (P(("box", "dir"), None, None), P("box"), P(None, None, "dir"), P(), P(), P())
    return jax.shard_map(
        body, mesh=mesh, in_specs=placed, out_specs=P(("box", "dir"), None, None), check_vma=False
    )
```
